32 devices in a mesh: seq: 16 (over z, y, core), tensor: 2 (over x).
Axes of the slice: x: 2, y: 2, z: 4, core: 2. Of those that a mesh axis runs over, the one named last changes fastest.
Arguments:
- tokens: bfloat16 [16384, 1024], P('seq'), may hold values from -6 to 6
- scene_lengths: int32 [4], replicated, may hold values from 1 to 7168, as said below
- w_query: bfloat16 [1, 1024, 1024], P(None, 'seq', 'tensor'), may hold values from -0.1875 to 0.1875
- w_key: bfloat16 [1, 1024, 1024], P(None, 'seq', 'tensor'), may hold values from -0.1875 to 0.1875
- w_value: bfloat16 [1, 1024, 1024], P(None, 'seq', 'tensor'), may hold values from -0.1875 to 0.1875
- w_out: bfloat16 [1, 1024, 1024], P(None, 'tensor', 'seq'), may hold values from -0.75 to 0.75
- w_up: bfloat16 [1, 1024, 4096], P(None, 'seq', 'tensor'), may hold values from -0.1875 to 0.1875
- w_down: bfloat16 [1, 4096, 1024], P(None, 'tensor', 'seq'), may hold values from -0.09375 to 0.09375
- norm_gain: bfloat16 [1, 2, 1024], P(None, None, 'seq'), may hold values from 0.099609375 to 1.8984375
- norm_bias: bfloat16 [1, 2, 1024], P(None, None, 'seq'), may hold values from -1.5 to 1.5
- cotangent: bfloat16 [16384, 1024], P('seq'), may hold values from -6 to 6
Outputs:
- activations: bfloat16 [16384, 1024], P('seq')
- grad_tokens: float32 [16384, 1024], P('seq')
- grad_query: float32 [1, 1024, 1024], P(None, 'seq', 'tensor')
- grad_key: float32 [1, 1024, 1024], P(None, 'seq', 'tensor')
- grad_value: float32 [1, 1024, 1024], P(None, 'seq', 'tensor')
- grad_out: float32 [1, 1024, 1024], P(None, 'tensor', 'seq')
- grad_up: float32 [1, 1024, 4096], P(None, 'seq', 'tensor')
- grad_down: float32 [1, 4096, 1024], P(None, 'tensor', 'seq')
- grad_gain: float32 [1, 2, 1024], P(None, None, 'seq')
- grad_bias: float32 [1, 2, 1024], P(None, None, 'seq')
The draws below stay inside these ranges and needn't reach their ends.
Inputs may be any that keep to these rules, and one draw needn't show every extreme that they name: `scene_lengths`: the lengths sum to 16384. Exactly one scene, at a place drawn from the seed, has 7168 tokens; the others have fewer.
All inputs are finite; a program needn't handle non-finite values.
Results may differ from the reference program's by a relative error of at most 0.017.
Values may be sent and summed in bfloat16 or wider, within the bound.
A program may use at most 256 MiB of HBM per device.

```python
import math
import jax
import jax.numpy as jnp
from jax import lax

D = 1024
HEADS = 16
HEAD_DIM = 64
FF = 4096
LAYERS = 1
SCENE_MAX = 7168
TOKENS = 16384
SCENES = 4


def draw_scene_lengths(key, part):
    key = jax.random.fold_in(key, 7)
    first_key, second_key = jax.random.split(key)
    others_count = SCENES - 1
    remains = TOKENS - SCENE_MAX
    spare_tokens = min(remains - others_count, SCENE_MAX // 2 - SCENES)
    fixed_part = (remains - spare_tokens) // others_count
    spare_tokens = remains - fixed_part * others_count
    cut_points = jnp.sort(jax.random.permutation(first_key, spare_tokens - 1)[:others_count - 1] + 1).astype(jnp.int32)
    bounds_all = jnp.concatenate([jnp.zeros((1,), jnp.int32), cut_points, jnp.full((1,), spare_tokens, jnp.int32)])
    gap_sizes = bounds_all[1:] - bounds_all[:-1]
    shorter = (fixed_part + gap_sizes).astype(jnp.int32)
    long_place = jax.random.randint(second_key, (), 0, SCENES)
    places = jnp.arange(SCENES, dtype=jnp.int32)
    source_index = jnp.clip(jnp.where(places > long_place, places - 1, places), 0, others_count - 1)
    return jnp.where(places == long_place, SCENE_MAX, shorter[source_index]).astype(jnp.int32)


def level_of(own_key, shape, pieces, low, largest):
    level, own = 1.0, jax.random.fold_in(own_key, 6)
    for dim, parts in pieces:
        draws = jnp.exp(jax.random.uniform(jax.random.fold_in(own, dim), (parts,), jnp.float32, low / len(pieces), largest / len(pieces)))
        level = level * jnp.repeat(draws, shape[dim] // parts).reshape([-1 if axis == dim else 1 for axis in range(len(shape))])
    return level


def bell_draw(stream_key, shape, scale, limit, cuts=(), kind=jnp.bfloat16):
    values = jax.random.normal(stream_key, shape, jnp.float32) * scale
    if len(cuts) > 0:
        values = level_of(stream_key, shape, cuts, -0.22, 0.18) * values
    return jnp.clip(values, min=-limit, max=limit).astype(kind)


def setup_inputs(seed: int = 0) -> dict:
    keys = jax.random.split(jax.random.key(seed), 12)
    return {
        "tokens": bell_draw(keys[0], (TOKENS, D), 1.0, 6.0, ((0, 16),)),
        "scene_lengths": draw_scene_lengths(jax.random.fold_in(keys[11], 71), 0),
        "w_query": bell_draw(keys[2], (LAYERS, D, D), D ** -0.5, 0.1875, ((1, 16), (2, 2))),
        "w_key": bell_draw(keys[3], (LAYERS, D, D), D ** -0.5, 0.1875, ((1, 16), (2, 2))),
        "w_value": bell_draw(keys[4], (LAYERS, D, D), D ** -0.5, 0.1875, ((1, 16), (2, 2))),
        "w_out": bell_draw(keys[5], (LAYERS, D, D), (D // 16) ** -0.5, 0.75, ((1, 2), (2, 16))),
        "w_up": bell_draw(keys[6], (LAYERS, D, FF), D ** -0.5, 0.1875, ((1, 16), (2, 2))),
        "w_down": bell_draw(keys[7], (LAYERS, FF, D), FF ** -0.5, 0.09375, ((1, 2), (2, 16))),
        "norm_gain": jnp.clip(1.0 + 0.18 * jax.random.normal(keys[8], (LAYERS, 2, D), jnp.float32), 0.099609375, 1.8984375).astype(jnp.bfloat16),
        "norm_bias": bell_draw(keys[9], (LAYERS, 2, D), 0.3, 1.5, ((2, 16),)),
        "cotangent": bell_draw(keys[10], (TOKENS, D), 1.0, 6.0, ((0, 16),)),
    }


@jax.custom_vjp
def low(v):
    return lax.optimization_barrier(v.astype(jnp.bfloat16)).astype(jnp.float32)

@jax.custom_vjp
def low_back(v):
    return v

def low_keep(v):
    return (low(v), None)

def low_pass(kept, grad):
    return (grad,)

def back_keep(v):
    return (v, None)

def back_low(kept, grad):
    return (low(grad),)
low.defvjp(low_keep, low_pass)
low_back.defvjp(back_keep, back_low)
norm_eps = 1e-06
neg_large = -1e+30
highest = lax.Precision.HIGHEST

def layer_norm(stream, gain_row, bias_row):
    centred = stream - lax.optimization_barrier(jnp.mean(stream, axis=-1, keepdims=True))
    spread = lax.optimization_barrier(jnp.mean(centred * centred, axis=-1, keepdims=True))
    return centred * lax.rsqrt(spread + norm_eps) * gain_row + bias_row

def matmul(left, right):
    return jnp.dot(left, right, precision=highest)

def attention(query_heads, keys_heads, values_heads, segment):
    total_rows = query_heads.shape[0]
    blocksize = math.gcd(total_rows, 512)
    query_blocks = query_heads.reshape(total_rows // blocksize, blocksize, HEADS, HEAD_DIM)
    scene_blocks = segment.reshape(total_rows // blocksize, blocksize)
    score_scale = HEAD_DIM ** (-0.5)

    def one_block(pair):
        query_part, scene_part = pair
        scores = low_back(jnp.einsum('qhd,khd->hqk', query_part, keys_heads, precision=highest) * score_scale)
        allowed = (scene_part[:, None] == segment[None, :])[None]
        scores = jnp.where(allowed, scores, neg_large)
        running_top = lax.optimization_barrier(jnp.max(scores, axis=2, keepdims=True))
        weights_exp = jnp.exp(scores - running_top)
        probs = weights_exp / lax.optimization_barrier(jnp.sum(weights_exp, axis=2, keepdims=True))
        return jnp.einsum('hqk,khd->qhd', low(probs), values_heads, precision=highest)
    mixed = lax.map(jax.checkpoint(one_block), (query_blocks, scene_blocks))
    return mixed.reshape(total_rows, HEADS * HEAD_DIM)

def one_layer(stream, layer_weights, segment):
    query_w, key_w, value_w, out_w, up_w, down_w, gains, biases = layer_weights
    total_rows = stream.shape[0]
    normed_one = low(layer_norm(stream, gains[0], biases[0]))
    query_full = low_back(low(matmul(normed_one, query_w)))
    keys_full = low_back(low(matmul(normed_one, key_w)))
    values_full = low_back(low(matmul(normed_one, value_w)))
    mixed = attention(query_full.reshape(total_rows, HEADS, HEAD_DIM), keys_full.reshape(total_rows, HEADS, HEAD_DIM), values_full.reshape(total_rows, HEADS, HEAD_DIM), segment)
    mixed = low_back(low(mixed))
    stream_mid = stream + low_back(matmul(mixed, out_w))
    normed_two = low(layer_norm(stream_mid, gains[1], biases[1]))
    up_raw = low_back(matmul(normed_two, up_w))
    act_low = low(jax.nn.gelu(up_raw, approximate=True))
    return stream_mid + low_back(matmul(act_low, down_w))

def reference(tokens, scene_lengths, w_query, w_key, w_value, w_out, w_up, w_down, norm_gain, norm_bias, cotangent):
    scene_ends = jnp.cumsum(scene_lengths).astype(jnp.int32)
    positions = jnp.arange(tokens.shape[0], dtype=jnp.int32)
    counted = lax.optimization_barrier(jnp.sum((positions[:, None] >= scene_ends[None, :]).astype(jnp.int32), axis=1)).astype(jnp.int32)
    segment = jnp.where(positions >= scene_ends[-1], counted + positions, counted).astype(jnp.int32)
    params = (w_query.astype(jnp.float32), w_key.astype(jnp.float32), w_value.astype(jnp.float32), w_out.astype(jnp.float32), w_up.astype(jnp.float32), w_down.astype(jnp.float32), norm_gain.astype(jnp.float32), norm_bias.astype(jnp.float32))

    def forward(stream, weights_all):
        for layer_index in range(LAYERS):
            stream = one_layer(stream, tuple((entry[layer_index] for entry in weights_all)), segment)
        return stream
    stream_out, backward = jax.vjp(forward, tokens.astype(jnp.float32), params)
    grad_stream, grad_params = backward(cotangent.astype(jnp.float32))
    return (stream_out.astype(jnp.bfloat16), grad_stream, grad_params[0], grad_params[1], grad_params[2], grad_params[3], grad_params[4], grad_params[5], grad_params[6], grad_params[7])
```

```python
import functools

import jax
import jax.numpy as jnp
from jax import lax
from jax.experimental import pallas as pl
from jax.experimental.pallas import tpu as pltpu
from jax.sharding import PartitionSpec as P

HEAD_DIM = 64
BF = jnp.bfloat16
F32 = jnp.float32
norm_eps = 1e-06
neg_large = -1e30
log2_e = 1.4426950408889634
ln_2 = 0.6931471805599453
STAT_ROWS = 3
SAFE_BOUND = 60.0
VMEM_BYTES = 56 * 2**20


def dot(left, right, left_dim, right_dim):
    return lax.dot_general(
        left, right, (((left_dim,), (right_dim,)), ((), ())), preferred_element_type=F32
    )


def layer_norm(stream, gain_row, bias_row):
    centred = stream - jnp.mean(stream, axis=-1, keepdims=True)
    spread = jnp.mean(centred * centred, axis=-1, keepdims=True)
    return centred * lax.rsqrt(spread + norm_eps) * gain_row + bias_row


def gelu_tanh(value):
    return jax.nn.gelu(value, approximate=True)


def scene_span(ends_ref, scenes, first, last):
    low = jnp.int32(0)
    high = ends_ref[scenes - 1]
    for scene in range(scenes):
        low = jnp.where(first >= ends_ref[scene], ends_ref[scene], low)
    for scene in reversed(range(scenes)):
        high = jnp.where(last < ends_ref[scene], ends_ref[scene], high)
    return low, high


def scene_inside(ends_ref, scenes, row, position):
    start = jnp.zeros_like(row)
    end = jnp.zeros_like(row)
    before = jnp.int32(0)
    for scene in range(scenes):
        start = jnp.where(row == STAT_ROWS + scene, before, start)
        end = jnp.where(row == STAT_ROWS + scene, ends_ref[scene], end)
        before = ends_ref[scene]
    return (position >= start) & (position < end)


def key_extra(ends_ref, scenes, first, rows):
    row = lax.broadcasted_iota(jnp.int32, (64, rows), 0)
    position = first + lax.broadcasted_iota(jnp.int32, (64, rows), 1)
    inside = scene_inside(ends_ref, scenes, row, position)
    return jnp.where(row < STAT_ROWS, -1.0, jnp.where(inside, 1.0, 0.0)).astype(BF)


def query_extra(ends_ref, scenes, first, rows, stat):
    row = lax.broadcasted_iota(jnp.int32, (64, rows), 0)
    position = first + lax.broadcasted_iota(jnp.int32, (64, rows), 1)
    inside = scene_inside(ends_ref, scenes, row, position)
    is_scene = (row >= STAT_ROWS) & (row < STAT_ROWS + scenes)
    extra = jnp.where(is_scene & jnp.logical_not(inside), neg_large, 0.0)
    if stat is not None:
        extra = stat_rows(row, stat, extra)
    return extra.astype(BF)


def stat_rows(row, stat, extra):
    top = stat.astype(BF).astype(F32)
    middle = (stat - top).astype(BF).astype(F32)
    bottom = stat - top - middle
    extra = jnp.where(row == 0, top, extra)
    extra = jnp.where(row == 1, middle, extra)
    return jnp.where(row == 2, bottom, extra)


def walk_tiles(process, state, first, count, unit, sizes):
    at = first
    left = count
    for size in sizes:
        steps = left // size
        begin = at

        def step(index, carry, begin=begin, size=size):
            offset = pl.multiple_of((begin + index * size) * unit, unit)
            return process(offset, size * unit, carry)

        state = lax.fori_loop(0, steps, step, state)
        at = at + steps * size
        left = left - steps * size
    return state


def forward_kernel(
    ends_ref, me_ref, recv_ref, other_ref, out_ref, lse_ref, keys, values, key_top,
    *, scenes, group, total,
):
    block = pl.program_id(0)
    core = me_ref[0]
    sources = recv_ref.shape[0]
    rows = recv_ref.shape[2]

    @pl.when(block == 0)
    def _():
        values[64:80, :] = jnp.ones((16, total), BF)
        key_top[0] = 0.0
        for piece in range(group):
            place = core ^ piece

            def load(source, carry, piece=piece, place=place):
                first = pl.multiple_of((source * group + place) * rows, rows)
                if piece == 0:
                    key = recv_ref[source, 64:128, :]
                    value = recv_ref[source, 128:192, :]
                else:
                    key = other_ref[piece - 1, source, 0:64, :]
                    value = other_ref[piece - 1, source, 64:128, :]
                extra = key_extra(ends_ref, scenes, first, rows)
                keys[pl.ds(first, rows), :] = jnp.concatenate([key, extra], axis=0).T
                values[0:64, pl.ds(first, rows)] = value
                wide = key.astype(F32)
                key_top[0] = jnp.maximum(key_top[0], jnp.max(jnp.sum(wide * wide, axis=0)))
                return carry

            lax.fori_loop(0, sources, load, 0)

    first = (block * group + core) * rows
    low, high = scene_span(ends_ref, scenes, first, first + rows - 1)
    query = recv_ref[block, 0:64, :]
    wide = query.astype(F32)
    query_top = jnp.max(jnp.sum(wide * wide, axis=0))
    query = jnp.concatenate([query, query_extra(ends_ref, scenes, first, rows, None)], axis=0)
    unit = 256
    begin = low // unit
    count = (high + unit - 1) // unit - begin
    safe = query_top * key_top[0] <= SAFE_BOUND * SAFE_BOUND

    def scores_of(offset, size):
        return dot(keys[pl.ds(offset, size), :], query, 1, 0)

    def mix(offset, size, weights):
        return dot(values[:, pl.ds(offset, size)], weights.astype(BF), 1, 0)

    def write(total_mix, top):
        summed = total_mix[64:65, :]
        out_ref[0] = (total_mix[0:64, :] / summed).astype(BF)
        lse_ref[0] = top + jnp.log(summed) * log2_e

    @pl.when(safe)
    def _():
        def process(offset, size, carry):
            return carry + mix(offset, size, jnp.exp2(scores_of(offset, size)))

        write(
            walk_tiles(process, jnp.zeros((80, rows), F32), begin, count, unit, (8, 4, 2, 1)),
            0.0,
        )

    @pl.when(jnp.logical_not(safe))
    def _():
        def process(offset, size, carry):
            top, mixed = carry
            scores = scores_of(offset, size)
            new_top = jnp.maximum(top, jnp.max(scores, axis=0, keepdims=True))
            weights = jnp.exp2(scores - new_top)
            return new_top, mixed * jnp.exp2(top - new_top) + mix(offset, size, weights)

        start = (jnp.full((1, rows), neg_large, F32), jnp.zeros((80, rows), F32))
        top, mixed = walk_tiles(process, start, begin, count, unit, (1,))
        write(mixed, top)


def attention_forward(ends, me, recv, other, group):
    sources, _, rows = recv.shape
    total = sources * group * rows
    whole = pl.BlockSpec(memory_space=pltpu.VMEM)
    return pl.pallas_call(
        functools.partial(
            forward_kernel, scenes=ends.shape[0], group=group, total=total
        ),
        grid_spec=pltpu.PrefetchScalarGridSpec(
            num_scalar_prefetch=2,
            grid=(sources,),
            in_specs=[whole, whole],
            out_specs=[
                pl.BlockSpec((1, 64, rows), lambda b, *_: (b, 0, 0)),
                pl.BlockSpec((1, 1, rows), lambda b, *_: (b, 0, 0)),
            ],
            scratch_shapes=[
                pltpu.VMEM((total, 128), BF),
                pltpu.VMEM((80, total), BF),
                pltpu.SMEM((1,), F32),
            ],
        ),
        out_shape=[
            jax.ShapeDtypeStruct((sources, 64, rows), BF),
            jax.ShapeDtypeStruct((sources, 1, rows), F32),
        ],
        compiler_params=pltpu.CompilerParams(vmem_limit_bytes=VMEM_BYTES),
        cost_estimate=pl.CostEstimate(
            flops=60 * 10**9, bytes_accessed=8 * 10**6, transcendentals=45 * 10**6
        ),
        name="attention_forward",
    )(ends, me, recv, other)


def backward_kernel(
    ends_ref, me_ref, recv_ref, pieces_ref, dout_ref, out_ref, lse_ref,
    dquery_ref, dkeys_ref,
    queries, douts, queries_flat, douts_flat, dqueries,
    *, scenes, group,
):
    block = pl.program_id(0)
    core = me_ref[0]
    sources = recv_ref.shape[0]
    rows = recv_ref.shape[2]
    span = group * rows

    @pl.when(block == 0)
    def _():
        dqueries[...] = jnp.zeros_like(dqueries)

        def load(source, carry):
            first = source * span + core * rows
            at = pl.ds(pl.multiple_of(source * rows, rows), rows)
            query = recv_ref[source, 0:64, :]
            dout = dout_ref[source]
            delta = jnp.sum(
                dout.astype(F32) * out_ref[source].astype(F32), axis=0, keepdims=True
            )
            row = lax.broadcasted_iota(jnp.int32, (64, rows), 0)
            extra = query_extra(ends_ref, scenes, first, rows, lse_ref[source])
            queries[at, :] = jnp.concatenate([query, extra], axis=0).T
            extra = stat_rows(row, delta, jnp.zeros((64, rows), F32)).astype(BF)
            douts[at, :] = jnp.concatenate([dout, extra], axis=0).T
            queries_flat[:, at] = query
            douts_flat[:, at] = dout
            return carry

        lax.fori_loop(0, sources, load, 0)

    source = block // group
    place = block % group
    first = block * rows
    low, high = scene_span(ends_ref, scenes, first, first + rows - 1)
    extra = key_extra(ends_ref, scenes, first, rows)
    key = pieces_ref[0, 0, 0:64, :]
    key_wide = jnp.concatenate([key, extra], axis=0)
    value_wide = jnp.concatenate([pieces_ref[0, 0, 64:128, :], extra], axis=0)
    key_rows = key.T
    begin = (low - core * rows - rows + span) // span
    count = jnp.minimum((high - core * rows + span - 1) // span, sources) - begin

    def process(offset, size, carry):
        dkey, dvalue = carry
        at = pl.ds(offset, size)
        probs = jnp.exp2(dot(queries[at, :], key_wide, 1, 0))
        dprobs = dot(douts[at, :], value_wide, 1, 0)
        dscores = (probs * dprobs).astype(BF)
        dvalue = dvalue + dot(douts_flat[:, at], probs.astype(BF), 1, 0)
        dkey = dkey + dot(queries_flat[:, at], dscores, 1, 0)
        dqueries[at, :] += dot(dscores, key_rows, 1, 0)
        return dkey, dvalue

    zeros = jnp.zeros((64, rows), F32)
    dkey, dvalue = walk_tiles(process, (zeros, zeros), begin, count, rows, (4, 2, 1))
    dkeys_ref[0, 0, 0:64, :] = (dkey * ln_2).astype(BF)
    dkeys_ref[0, 0, 64:128, :] = dvalue.astype(BF)

    @pl.when(block == sources * group - 1)
    def _():
        def store(source, carry):
            at = pl.ds(pl.multiple_of(source * rows, rows), rows)
            dquery_ref[source] = (dqueries[at, :].T * HEAD_DIM**-0.5).astype(BF)
            return carry

        lax.fori_loop(0, sources, store, 0)


def attention_backward(ends, me, recv, pieces, dout, out, lse, group):
    sources, _, rows = recv.shape
    mine = sources * rows
    whole = pl.BlockSpec(memory_space=pltpu.VMEM)

    def piece_map(block, ends_ref, me_ref):
        return ((block % group) ^ me_ref[0], block // group, 0, 0)

    return pl.pallas_call(
        functools.partial(backward_kernel, scenes=ends.shape[0], group=group),
        grid_spec=pltpu.PrefetchScalarGridSpec(
            num_scalar_prefetch=2,
            grid=(sources * group,),
            in_specs=[whole, pl.BlockSpec((1, 1, 128, rows), piece_map), whole, whole, whole],
            out_specs=[whole, pl.BlockSpec((1, 1, 128, rows), piece_map)],
            scratch_shapes=[
                pltpu.VMEM((mine, 128), BF),
                pltpu.VMEM((mine, 128), BF),
                pltpu.VMEM((64, mine), BF),
                pltpu.VMEM((64, mine), BF),
                pltpu.VMEM((mine, 64), F32),
            ],
        ),
        out_shape=[
            jax.ShapeDtypeStruct((sources, 64, rows), BF),
            jax.ShapeDtypeStruct((group, sources, 128, rows), BF),
        ],
        compiler_params=pltpu.CompilerParams(vmem_limit_bytes=VMEM_BYTES),
        cost_estimate=pl.CostEstimate(
            flops=150 * 10**9, bytes_accessed=20 * 10**6, transcendentals=45 * 10**6
        ),
        name="attention_backward",
    )(ends, me, recv, pieces, dout, out, lse)


def swap_tensor(part):
    return lax.ppermute(part, "tensor", [(0, 1), (1, 0)])


def sum_tensor(part):
    low = part.astype(BF)
    return low.astype(F32) + swap_tensor(low).astype(F32)


def per_device(
    tokens, scene_lengths, w_query, w_key, w_value, w_out, w_up, w_down,
    norm_gain, norm_bias, cotangent,
):
    own_rows, width = tokens.shape
    devices = lax.axis_size("seq")
    heads = w_query.shape[2] // HEAD_DIM
    columns = heads * HEAD_DIM
    hidden = w_up.shape[2]
    group = devices // heads
    rows = own_rows // group
    me = lax.rem(lax.axis_index("seq"), group).astype(jnp.int32).reshape(1)
    half = lax.axis_index("tensor")
    ends = jnp.cumsum(scene_lengths).astype(jnp.int32)

    def to_owners(parts):
        return lax.all_to_all(parts, "seq", 0, 0, tiled=True)

    first_part = jnp.concatenate(
        [
            jnp.stack([w_query[0], w_key[0], w_value[0]], axis=1)
            .reshape(-1, 3, heads, HEAD_DIM)
            .transpose(0, 2, 1, 3)
            .reshape(-1, 3 * columns),
            norm_gain[0].T,
            norm_bias[0].T,
        ],
        axis=1,
    )
    first_all = lax.all_gather(first_part, "seq", axis=0, tiled=True)
    second_part = jnp.concatenate([w_out[0].T, w_up[0], w_down[0].T], axis=1)
    second_all = lax.all_gather(second_part, "seq", axis=0, tiled=True)
    w_heads = first_all[:, : 3 * columns]
    norms = first_all[:, 3 * columns :].astype(F32).T
    gains, biases = norms[0:2], norms[2:4]
    out_own = second_all[:, :columns]
    up_w = second_all[:, columns : columns + hidden]
    down_w = second_all[:, columns + hidden :]
    out_other = swap_tensor(out_own)

    stream = tokens.astype(F32)
    normed_one = layer_norm(stream, gains[0], biases[0]).astype(BF)
    projected = dot(w_heads, normed_one, 0, 1).reshape(heads, 3, HEAD_DIM, group, rows)
    factors = jnp.array([HEAD_DIM**-0.5 * log2_e, 1.0, 1.0], F32).reshape(1, 3, 1, 1, 1)
    projected = (projected * factors).astype(BF)
    projected = projected.transpose(0, 3, 1, 2, 4).reshape(devices, 3 * HEAD_DIM, rows)
    recv = to_owners(projected)
    own_piece = recv[:, HEAD_DIM:, :]

    def swap_core(part, by):
        return lax.ppermute(part, "seq", [(i, i ^ by) for i in range(devices)])

    others = jnp.stack([swap_core(own_piece, by) for by in range(1, group)])
    out_head, lse = attention_forward(ends, me, recv, others, group)

    mixed = to_owners(out_head).reshape(heads, group, HEAD_DIM, rows)
    mixed = mixed.transpose(1, 3, 0, 2).reshape(own_rows, columns)
    mixed_other = swap_tensor(mixed)

    def in_order(own, other):
        return jnp.where(
            half == 0,
            jnp.concatenate([own, other], axis=1),
            jnp.concatenate([other, own], axis=1),
        )

    mid = stream + dot(in_order(mixed, mixed_other), in_order(out_own, out_other), 1, 1)
    normed_raw, norm_two_back = jax.vjp(layer_norm, mid, gains[1], biases[1])
    normed_two = normed_raw.astype(BF)
    up_raw = dot(normed_two, up_w, 1, 0)
    act_raw, gelu_back = jax.vjp(gelu_tanh, up_raw)
    act = act_raw.astype(BF)
    dz = cotangent
    dup = gelu_back(dot(dz, down_w, 1, 0))[0].astype(BF)
    dnormed_two = sum_tensor(dot(dup, up_w, 1, 1))
    dmid_norm, dgain_two, dbias_two = norm_two_back(dnormed_two)
    dmid = dz.astype(F32) + dmid_norm
    dy = dmid.astype(BF)
    dout = dot(out_own, dy, 0, 1).astype(BF).reshape(heads, HEAD_DIM, group, rows)
    dout = to_owners(dout.transpose(0, 2, 1, 3).reshape(devices, HEAD_DIM, rows))

    last = mid + sum_tensor(dot(act, down_w, 1, 1))
    grads_second = jnp.concatenate(
        [dot(dy, mixed, 0, 0), dot(normed_two, dup, 0, 0), dot(dz, act, 0, 0)], axis=1
    ).astype(BF)
    grads_second = lax.psum_scatter(grads_second, "seq", scatter_dimension=0, tiled=True)

    pieces = jnp.concatenate([own_piece[None], others], axis=0)
    dquery, dpieces = attention_backward(ends, me, recv, pieces, dout, out_head, lse, group)
    dpiece = dpieces[0].astype(F32)
    for by in range(1, group):
        dpiece = dpiece + swap_core(dpieces[by], by).astype(F32)
    dheads = to_owners(jnp.concatenate([dquery, dpiece.astype(BF)], axis=1))
    dheads = dheads.reshape(heads, group, 3 * HEAD_DIM, rows)
    dheads = dheads.transpose(1, 3, 0, 2).reshape(own_rows, 3 * columns)

    dnormed_one = sum_tensor(dot(dheads, w_heads, 1, 1))
    norm_one_back = jax.vjp(layer_norm, stream, gains[0], biases[0])[1]
    dstream_norm, dgain_one, dbias_one = norm_one_back(dnormed_one)
    dstream = dmid + dstream_norm
    grads_first = dot(normed_one, dheads, 0, 0).astype(BF)
    grads_first = lax.psum_scatter(grads_first, "seq", scatter_dimension=0, tiled=True)
    norm_grads = jnp.stack([dgain_one, dgain_two, dbias_one, dbias_two])
    norm_grads = norm_grads.reshape(4, devices, -1).transpose(1, 0, 2)
    norm_grads = jnp.sum(to_owners(norm_grads), axis=0)

    grads_first = grads_first.astype(F32).reshape(-1, heads, 3, HEAD_DIM).transpose(2, 0, 1, 3)
    grads_first = grads_first.reshape(3, 1, -1, columns)
    grads_second = grads_second.astype(F32)
    return (
        last.astype(BF),
        dstream,
        grads_first[0],
        grads_first[1],
        grads_first[2],
        grads_second[:, :columns].T[None],
        grads_second[:, columns : columns + hidden][None],
        grads_second[:, columns + hidden :].T[None],
        norm_grads[None, 0:2],
        norm_grads[None, 2:4],
    )


def solution(mesh):
    placed = (
        P("seq", None),
        P(),
        P(None, "seq", "tensor"),
        P(None, "seq", "tensor"),
        P(None, "seq", "tensor"),
        P(None, "tensor", "seq"),
        P(None, "seq", "tensor"),
        P(None, "tensor", "seq"),
        P(None, None, "seq"),
        P(None, None, "seq"),
        P("seq", None),
    )
    return jax.shard_map(
        per_device,
        mesh=mesh,
        in_specs=placed,
        out_specs=(
            P("seq", None),
            P("seq", None),
            P(None, "seq", "tensor"),
            P(None, "seq", "tensor"),
            P(None, "seq", "tensor"),
            P(None, "tensor", "seq"),
            P(None, "seq", "tensor"),
            P(None, "tensor", "seq"),
            P(None, None, "seq"),
            P(None, None, "seq"),
        ),
        check_vma=False,
    )
```

```python
import functools

import jax
import jax.numpy as jnp
from jax import lax
from jax.experimental import pallas as pl
from jax.experimental.pallas import tpu as pltpu
from jax.sharding import PartitionSpec as P

HEAD_DIM = 64
BF = jnp.bfloat16
F32 = jnp.float32
norm_eps = 1e-06
neg_large = -1e30
log2_e = 1.4426950408889634
ln_2 = 0.6931471805599453
STAT_ROWS = 3
SAFE_BOUND = 60.0
PARTS = 2
VMEM_BYTES = 56 * 2**20


def dot(left, right, left_dim, right_dim):
    return lax.dot_general(
        left, right, (((left_dim,), (right_dim,)), ((), ())), preferred_element_type=F32
    )


def layer_norm(stream, gain_row, bias_row):
    centred = stream - jnp.mean(stream, axis=-1, keepdims=True)
    spread = jnp.mean(centred * centred, axis=-1, keepdims=True)
    return centred * lax.rsqrt(spread + norm_eps) * gain_row + bias_row


def gelu_tanh(value):
    return jax.nn.gelu(value, approximate=True)


def ring_of(devices):
    chips = devices // 2
    index = lax.axis_index("seq")
    core = lax.rem(index, 2)
    chip = index // 2
    if chips != 8:
        return chip, core, lambda place: 2 * place + core
    layer, column = chip // 2, lax.rem(chip, 2)
    place = layer + column * (7 - 2 * layer)

    def seq_index(place):
        side = place // 4
        depth = place + side * (7 - 2 * place)
        return depth * 4 + side * 2 + core

    return place, core, seq_index


def remote_copy(source, target, send_sem, recv_sem, seq):
    return pltpu.make_async_remote_copy(
        src_ref=source, dst_ref=target, send_sem=send_sem, recv_sem=recv_sem,
        device_id={"seq": seq}, device_id_type=pl.DeviceIdType.MESH,
    )


def meet(others):
    barrier = pltpu.get_barrier_semaphore()
    for other in others:
        pl.semaphore_signal(
            barrier, inc=1, device_id=other, device_id_type=pl.DeviceIdType.MESH
        )
    pl.semaphore_wait(barrier, len(others))


def project_kernel(
    tokens_ref, query_ref, key_ref, value_ref, gain_ref, bias_ref,
    sent_ref, normed_ref, weights_ref, norms_ref,
    gathered, scaled, send_right, recv_right, send_left, recv_left, send_peer, recv_peer,
    out_sem,
    *, devices, group, columns, width,
):
    chips = devices // 2
    depth = width // devices
    rows = tokens_ref.shape[0] // group
    place, core, seq_index = ring_of(devices)
    me = seq_index(place)
    right = seq_index(lax.rem(place + 1, chips))
    left = seq_index(lax.rem(place + chips - 1, chips))
    peer = me + 1 - 2 * core
    heads = columns // HEAD_DIM
    meet([{"seq": right}, {"seq": left}, {"seq": peer}])

    def slot(index):
        return gathered.at[pl.ds(pl.multiple_of(index * depth, depth), depth), :]

    mine = pl.ds(pl.multiple_of(me * depth, depth), depth)
    for which, ref in enumerate((query_ref, key_ref, value_ref)):
        gathered[mine, which * columns : (which + 1) * columns] = ref[0]
    norm_rows = jnp.concatenate(
        [gain_ref[0].astype(F32), bias_ref[0].astype(F32), jnp.zeros((124, depth), F32)], axis=0
    )
    gathered[mine, 3 * columns :] = norm_rows.T.astype(BF)

    to_right, to_left = chips // 2, chips - 1 - chips // 2

    def rightward(step):
        index = seq_index(lax.rem(place - step + chips, chips))
        return remote_copy(
            slot(index), slot(index), send_right.at[step], recv_right.at[step], right
        )

    def leftward(step):
        index = seq_index(lax.rem(place + step, chips))
        return remote_copy(slot(index), slot(index), send_left.at[step], recv_left.at[step], left)

    def across(distance):
        index = seq_index(lax.rem(place + distance + chips, chips))
        return remote_copy(
            slot(index), slot(index),
            send_peer.at[(distance + chips) % chips], recv_peer.at[(distance + chips) % chips], peer,
        )

    def arrive_right(step):
        index = seq_index(lax.rem(place - step - 1 + chips, chips))
        remote_copy(
            slot(index), slot(index), send_right.at[step], recv_right.at[step], right
        ).wait_recv()

    def arrive_left(step):
        index = seq_index(lax.rem(place + step + 1, chips))
        remote_copy(
            slot(index), slot(index), send_left.at[step], recv_left.at[step], left
        ).wait_recv()

    rightward(0).start()
    leftward(0).start()
    across(0).start()

    def normalize(index, carry):
        at = pl.ds(pl.multiple_of(index * 128, 128), 128)
        stream = tokens_ref[at, :].astype(F32)
        centred = stream - jnp.mean(stream, axis=-1, keepdims=True)
        spread = jnp.mean(centred * centred, axis=-1, keepdims=True)
        scaled[at, :] = centred * lax.rsqrt(spread + norm_eps)
        return carry

    lax.fori_loop(0, tokens_ref.shape[0] // 128, normalize, 0)

    for step in range(to_right):
        arrive_right(step)
        if step + 1 < to_right:
            rightward(step + 1).start()
        across(-step - 1).start()
        if step < to_left:
            arrive_left(step)
            if step + 1 < to_left:
                leftward(step + 1).start()
            across(step + 1).start()
    for distance in range(chips):
        index = seq_index(lax.rem(place + distance, chips)) + 1 - 2 * core
        remote_copy(
            slot(index), slot(index), send_peer.at[distance], recv_peer.at[distance], peer
        ).wait_recv()

    store = pltpu.make_async_copy(gathered.at[:, : 3 * columns], weights_ref, out_sem)
    store.start()
    norms = gathered[:, 3 * columns :].astype(F32).T
    norms_ref[...] = norms[0:8]

    def apply_norm(index, carry):
        at = pl.ds(pl.multiple_of(index * 128, 128), 128)
        normed_ref[at, :] = (scaled[at, :] * norms[0:1] + norms[2:3]).astype(BF)
        return carry

    lax.fori_loop(0, tokens_ref.shape[0] // 128, apply_norm, 0)
    for which in range(3):
        weights = gathered[:, which * columns : (which + 1) * columns].T
        factor = HEAD_DIM**-0.5 * log2_e if which == 0 else 1.0

        def project(core_index, carry, which=which, weights=weights, factor=factor):
            at = pl.ds(pl.multiple_of(core_index * rows, rows), rows)
            result = (dot(weights, normed_ref[at, :], 1, 1) * factor).astype(BF)
            for head in range(heads):
                sent_ref[head * group + core_index, which * HEAD_DIM : (which + 1) * HEAD_DIM, :] = (
                    result[head * HEAD_DIM : (head + 1) * HEAD_DIM, :]
                )
            return carry

        lax.fori_loop(0, group, project, 0)
    for step in range(to_right):
        rightward(step).wait_send()
    for step in range(to_left):
        leftward(step).wait_send()
    for distance in range(chips):
        across(distance).wait_send()
    store.wait()


def project(tokens, w_query, w_key, w_value, norm_gain, norm_bias, devices, group):
    own_rows, width = tokens.shape
    columns = w_query.shape[2]
    chips = devices // 2
    whole = pl.BlockSpec(memory_space=pltpu.VMEM)
    dma = pltpu.SemaphoreType.DMA
    return pl.pallas_call(
        functools.partial(
            project_kernel, devices=devices, group=group, columns=columns, width=width
        ),
        in_specs=[whole] * 6,
        out_specs=[whole, whole, pl.BlockSpec(memory_space=pl.ANY), whole],
        out_shape=[
            jax.ShapeDtypeStruct((devices, 3 * HEAD_DIM, own_rows // group), BF),
            jax.ShapeDtypeStruct((own_rows, width), BF),
            jax.ShapeDtypeStruct((width, 3 * columns), BF),
            jax.ShapeDtypeStruct((8, width), F32),
        ],
        scratch_shapes=[
            pltpu.VMEM((width, 3 * columns + 128), BF),
            pltpu.VMEM((own_rows, width), F32),
            dma((chips // 2,)), dma((chips // 2,)),
            dma((chips // 2,)), dma((chips // 2,)),
            dma((chips,)), dma((chips,)),
            dma,
        ],
        compiler_params=pltpu.CompilerParams(
            vmem_limit_bytes=VMEM_BYTES, collective_id=1, has_side_effects=True
        ),
        name="project",
    )(tokens, w_query, w_key, w_value, norm_gain, norm_bias)


def scene_span(ends_ref, scenes, first, last):
    low = jnp.int32(0)
    high = ends_ref[scenes - 1]
    for scene in range(scenes):
        low = jnp.where(first >= ends_ref[scene], ends_ref[scene], low)
    for scene in reversed(range(scenes)):
        high = jnp.where(last < ends_ref[scene], ends_ref[scene], high)
    return low, high


def scene_inside(ends_ref, scenes, row, position):
    start = jnp.zeros_like(row)
    end = jnp.zeros_like(row)
    before = jnp.int32(0)
    for scene in range(scenes):
        start = jnp.where(row == STAT_ROWS + scene, before, start)
        end = jnp.where(row == STAT_ROWS + scene, ends_ref[scene], end)
        before = ends_ref[scene]
    return (position >= start) & (position < end)


def key_extra(ends_ref, scenes, first, rows):
    row = lax.broadcasted_iota(jnp.int32, (64, rows), 0)
    position = first + lax.broadcasted_iota(jnp.int32, (64, rows), 1)
    inside = scene_inside(ends_ref, scenes, row, position)
    return jnp.where(row < STAT_ROWS, -1.0, jnp.where(inside, 1.0, 0.0)).astype(BF)


def query_extra(ends_ref, scenes, first, rows, stat):
    row = lax.broadcasted_iota(jnp.int32, (64, rows), 0)
    position = first + lax.broadcasted_iota(jnp.int32, (64, rows), 1)
    inside = scene_inside(ends_ref, scenes, row, position)
    is_scene = (row >= STAT_ROWS) & (row < STAT_ROWS + scenes)
    extra = jnp.where(is_scene & jnp.logical_not(inside), neg_large, 0.0)
    if stat is not None:
        extra = stat_rows(row, stat, extra)
    return extra.astype(BF)


def stat_rows(row, stat, extra):
    top = stat.astype(BF).astype(F32)
    middle = (stat - top).astype(BF).astype(F32)
    bottom = stat - top - middle
    extra = jnp.where(row == 0, top, extra)
    extra = jnp.where(row == 1, middle, extra)
    return jnp.where(row == 2, bottom, extra)


def walk_tiles(process, state, first, count, unit, sizes):
    at = first
    left = count
    for size in sizes:
        steps = left // size
        begin = at

        def step(index, carry, begin=begin, size=size):
            offset = pl.multiple_of((begin + index * size) * unit, unit)
            return process(offset, size * unit, carry)

        state = lax.fori_loop(0, steps, step, state)
        at = at + steps * size
        left = left - steps * size
    return state


def forward_kernel(
    ends_ref, me_ref, recv_ref, other_ref, out_ref, lse_ref, keys, values, key_top,
    *, scenes, group, total,
):
    block = pl.program_id(0)
    core = me_ref[0]
    sources = recv_ref.shape[0]
    rows = recv_ref.shape[2]

    @pl.when(block == 0)
    def _():
        values[64:80, :] = jnp.ones((16, total), BF)
        key_top[0] = 0.0
        for piece in range(group):
            place = core ^ piece

            def load(source, carry, piece=piece, place=place):
                first = pl.multiple_of((source * group + place) * rows, rows)
                if piece == 0:
                    key = recv_ref[source, 64:128, :]
                    value = recv_ref[source, 128:192, :]
                else:
                    key = other_ref[piece - 1, source, 0:64, :]
                    value = other_ref[piece - 1, source, 64:128, :]
                extra = key_extra(ends_ref, scenes, first, rows)
                keys[pl.ds(first, rows), :] = jnp.concatenate([key, extra], axis=0).T
                values[0:64, pl.ds(first, rows)] = value
                wide = key.astype(F32)
                key_top[0] = jnp.maximum(key_top[0], jnp.max(jnp.sum(wide * wide, axis=0)))
                return carry

            lax.fori_loop(0, sources, load, 0)

    first = (block * group + core) * rows
    low, high = scene_span(ends_ref, scenes, first, first + rows - 1)
    query = recv_ref[block, 0:64, :]
    wide = query.astype(F32)
    query_top = jnp.max(jnp.sum(wide * wide, axis=0))
    query = jnp.concatenate([query, query_extra(ends_ref, scenes, first, rows, None)], axis=0)
    unit = 256
    begin = low // unit
    count = (high + unit - 1) // unit - begin
    safe = query_top * key_top[0] <= SAFE_BOUND * SAFE_BOUND

    def scores_of(offset, size):
        return dot(keys[pl.ds(offset, size), :], query, 1, 0)

    def mix(offset, size, weights):
        return dot(values[:, pl.ds(offset, size)], weights.astype(BF), 1, 0)

    def write(total_mix, top):
        summed = total_mix[64:65, :]
        out_ref[0] = (total_mix[0:64, :] / summed).astype(BF)
        lse_ref[0] = top + jnp.log(summed) * log2_e

    @pl.when(safe)
    def _():
        def process(offset, size, carry):
            return carry + mix(offset, size, jnp.exp2(scores_of(offset, size)))

        write(
            walk_tiles(process, jnp.zeros((80, rows), F32), begin, count, unit, (8, 4, 2, 1)),
            0.0,
        )

    @pl.when(jnp.logical_not(safe))
    def _():
        def process(offset, size, carry):
            top, mixed = carry
            scores = scores_of(offset, size)
            new_top = jnp.maximum(top, jnp.max(scores, axis=0, keepdims=True))
            weights = jnp.exp2(scores - new_top)
            return new_top, mixed * jnp.exp2(top - new_top) + mix(offset, size, weights)

        start = (jnp.full((1, rows), neg_large, F32), jnp.zeros((80, rows), F32))
        top, mixed = walk_tiles(process, start, begin, count, unit, (1,))
        write(mixed, top)


def attention_forward(ends, me, recv, other, group):
    sources, _, rows = recv.shape
    total = sources * group * rows
    whole = pl.BlockSpec(memory_space=pltpu.VMEM)
    return pl.pallas_call(
        functools.partial(
            forward_kernel, scenes=ends.shape[0], group=group, total=total
        ),
        grid_spec=pltpu.PrefetchScalarGridSpec(
            num_scalar_prefetch=2,
            grid=(sources,),
            in_specs=[whole, whole],
            out_specs=[
                pl.BlockSpec((1, 64, rows), lambda b, *_: (b, 0, 0)),
                pl.BlockSpec((1, 1, rows), lambda b, *_: (b, 0, 0)),
            ],
            scratch_shapes=[
                pltpu.VMEM((total, 128), BF),
                pltpu.VMEM((80, total), BF),
                pltpu.SMEM((1,), F32),
            ],
        ),
        out_shape=[
            jax.ShapeDtypeStruct((sources, 64, rows), BF),
            jax.ShapeDtypeStruct((sources, 1, rows), F32),
        ],
        compiler_params=pltpu.CompilerParams(vmem_limit_bytes=VMEM_BYTES),
        cost_estimate=pl.CostEstimate(
            flops=60 * 10**9, bytes_accessed=8 * 10**6, transcendentals=45 * 10**6
        ),
        name="attention_forward",
    )(ends, me, recv, other)


def backward_kernel(ends_ref, me_ref, recv_ref, pieces_ref, *refs, scenes, group, parts):
    dout_refs = refs[:parts]
    out_ref, lse_ref, dquery_ref, dkeys_ref = refs[parts : parts + 4]
    queries, douts, queries_flat, douts_flat, dqueries = refs[parts + 4 :]
    block = pl.program_id(0)
    core = me_ref[0]
    sources = recv_ref.shape[0]
    rows = recv_ref.shape[2]
    span = group * rows

    @pl.when(block == 0)
    def _():
        dqueries[...] = jnp.zeros_like(dqueries)

        def load(source, carry):
            first = source * span + core * rows
            at = pl.ds(pl.multiple_of(source * rows, rows), rows)
            query = recv_ref[source, 0:64, :]
            dout = jnp.concatenate([ref[source] for ref in dout_refs], axis=1)
            delta = jnp.sum(
                dout.astype(F32) * out_ref[source].astype(F32), axis=0, keepdims=True
            )
            row = lax.broadcasted_iota(jnp.int32, (64, rows), 0)
            extra = query_extra(ends_ref, scenes, first, rows, lse_ref[source])
            queries[at, :] = jnp.concatenate([query, extra], axis=0).T
            extra = stat_rows(row, delta, jnp.zeros((64, rows), F32)).astype(BF)
            douts[at, :] = jnp.concatenate([dout, extra], axis=0).T
            queries_flat[:, at] = query
            douts_flat[:, at] = dout
            return carry

        lax.fori_loop(0, sources, load, 0)

    source = block // group
    place = block % group
    first = block * rows
    low, high = scene_span(ends_ref, scenes, first, first + rows - 1)
    extra = key_extra(ends_ref, scenes, first, rows)
    key = pieces_ref[0, 0, 0:64, :]
    key_wide = jnp.concatenate([key, extra], axis=0)
    value_wide = jnp.concatenate([pieces_ref[0, 0, 64:128, :], extra], axis=0)
    key_rows = key.T
    begin = (low - core * rows - rows + span) // span
    count = jnp.minimum((high - core * rows + span - 1) // span, sources) - begin

    def process(offset, size, carry):
        dkey, dvalue = carry
        at = pl.ds(offset, size)
        probs = jnp.exp2(dot(queries[at, :], key_wide, 1, 0))
        dprobs = dot(douts[at, :], value_wide, 1, 0)
        dscores = (probs * dprobs).astype(BF)
        dvalue = dvalue + dot(douts_flat[:, at], probs.astype(BF), 1, 0)
        dkey = dkey + dot(queries_flat[:, at], dscores, 1, 0)
        dqueries[at, :] += dot(dscores, key_rows, 1, 0)
        return dkey, dvalue

    zeros = jnp.zeros((64, rows), F32)
    dkey, dvalue = walk_tiles(process, (zeros, zeros), begin, count, rows, (4, 2, 1))
    dkeys_ref[0, 0, 0:64, :] = (dkey * ln_2).astype(BF)
    dkeys_ref[0, 0, 64:128, :] = dvalue.astype(BF)

    @pl.when(block == sources * group - 1)
    def _():
        def store(source, carry):
            at = pl.ds(pl.multiple_of(source * rows, rows), rows)
            dquery_ref[source] = (dqueries[at, :].T * HEAD_DIM**-0.5).astype(BF)
            return carry

        lax.fori_loop(0, sources, store, 0)


def attention_backward(ends, me, recv, pieces, dout, out, lse, group):
    sources, _, rows = recv.shape
    mine = sources * rows
    whole = pl.BlockSpec(memory_space=pltpu.VMEM)

    def piece_map(block, ends_ref, me_ref):
        return ((block % group) ^ me_ref[0], block // group, 0, 0)

    return pl.pallas_call(
        functools.partial(
            backward_kernel, scenes=ends.shape[0], group=group, parts=len(dout)
        ),
        grid_spec=pltpu.PrefetchScalarGridSpec(
            num_scalar_prefetch=2,
            grid=(sources * group,),
            in_specs=[whole, pl.BlockSpec((1, 1, 128, rows), piece_map)] + [whole] * (len(dout) + 2),
            out_specs=[whole, pl.BlockSpec((1, 1, 128, rows), piece_map)],
            scratch_shapes=[
                pltpu.VMEM((mine, 128), BF),
                pltpu.VMEM((mine, 128), BF),
                pltpu.VMEM((64, mine), BF),
                pltpu.VMEM((64, mine), BF),
                pltpu.VMEM((mine, 64), F32),
            ],
        ),
        out_shape=[
            jax.ShapeDtypeStruct((sources, 64, rows), BF),
            jax.ShapeDtypeStruct((group, sources, 128, rows), BF),
        ],
        compiler_params=pltpu.CompilerParams(vmem_limit_bytes=VMEM_BYTES),
        cost_estimate=pl.CostEstimate(
            flops=150 * 10**9, bytes_accessed=20 * 10**6, transcendentals=45 * 10**6
        ),
        name="attention_backward",
    )(ends, me, recv, pieces, *dout, out, lse)


def swap_tensor(part):
    return lax.ppermute(part, "tensor", [(0, 1), (1, 0)])


def sum_tensor(part):
    low = part.astype(BF)
    return low.astype(F32) + swap_tensor(low).astype(F32)


def per_device(
    tokens, scene_lengths, w_query, w_key, w_value, w_out, w_up, w_down,
    norm_gain, norm_bias, cotangent,
):
    own_rows, width = tokens.shape
    devices = lax.axis_size("seq")
    heads = w_query.shape[2] // HEAD_DIM
    columns = heads * HEAD_DIM
    hidden = w_up.shape[2]
    group = devices // heads
    rows = own_rows // group
    me = lax.rem(lax.axis_index("seq"), group).astype(jnp.int32).reshape(1)
    half = lax.axis_index("tensor")
    ends = jnp.cumsum(scene_lengths).astype(jnp.int32)

    def in_order(part):
        other = swap_tensor(part)
        return jnp.where(
            half == 0,
            jnp.concatenate([part, other], axis=-1),
            jnp.concatenate([other, part], axis=-1),
        )

    def to_owners(parts):
        return lax.all_to_all(parts, "seq", 0, 0, tiled=True)

    projected, normed_one, w_first, norms = project(
        tokens, w_query, w_key, w_value, norm_gain, norm_bias, devices, group
    )
    gains, biases = norms[0:2], norms[2:4]
    stream = tokens.astype(F32)
    out_part = in_order(w_out[0].T)
    second_part = jnp.concatenate([out_part, w_up[0], w_down[0].T], axis=1)
    recv = to_owners(projected)
    recv, second_part = lax.optimization_barrier((recv, second_part))
    second_all = lax.all_gather(second_part, "seq", axis=0, tiled=True)
    out_w = second_all[:, :width]
    out_own = lax.dynamic_slice_in_dim(out_w, half * columns, columns, 1)
    up_w = second_all[:, width : width + hidden]
    down_w = second_all[:, width + hidden :]
    own_piece = recv[:, HEAD_DIM:, :]

    def swap_core(part, by):
        return lax.ppermute(part, "seq", [(i, i ^ by) for i in range(devices)])

    others = jnp.stack([swap_core(own_piece, by) for by in range(1, group)])
    out_head, lse = attention_forward(ends, me, recv, others, group)

    part_rows = rows // PARTS

    def split(rows_all):
        cut = rows_all.reshape(group, PARTS, part_rows, rows_all.shape[1])
        return [cut[:, part].reshape(group * part_rows, -1) for part in range(PARTS)]

    def join(pieces_all):
        cut = [piece.reshape(group, part_rows, -1) for piece in pieces_all]
        return jnp.stack(cut, axis=1).reshape(own_rows, -1)

    mixed_parts, up_parts, mids, normed_parts, acts, dups, dys, dmids, douts = ([] for _ in range(9))
    dgain_two = dbias_two = 0.0
    dz_parts = split(cotangent)
    stream_parts = split(stream)
    for part in range(PARTS):
        piece = to_owners(out_head[:, :, part * part_rows : (part + 1) * part_rows])
        piece = piece.reshape(heads, group, HEAD_DIM, part_rows)
        mixed = piece.transpose(1, 3, 0, 2).reshape(group * part_rows, columns)
        mid = stream_parts[part] + dot(in_order(mixed), out_w, 1, 1)
        normed_raw, norm_two_back = jax.vjp(layer_norm, mid, gains[1], biases[1])
        normed_two = normed_raw.astype(BF)
        up_raw = dot(normed_two, up_w, 1, 0)
        act_raw, gelu_back = jax.vjp(gelu_tanh, up_raw)
        dz = dz_parts[part]
        dup = gelu_back(dot(dz, down_w, 1, 0))[0].astype(BF)
        dnormed_two = sum_tensor(dot(dup, up_w, 1, 1))
        dmid_norm, dgain, dbias = norm_two_back(dnormed_two)
        dgain_two, dbias_two = dgain_two + dgain, dbias_two + dbias
        dmid = dz.astype(F32) + dmid_norm
        dy = dmid.astype(BF)
        dout = dot(out_own, dy, 0, 1).astype(BF).reshape(heads, HEAD_DIM, group, part_rows)
        dout = dout.transpose(0, 2, 1, 3).reshape(devices, HEAD_DIM, part_rows)
        douts.append(to_owners(dout))
        mixed_parts.append(mixed)
        mids.append(mid)
        normed_parts.append(normed_two)
        acts.append(act_raw.astype(BF))
        dups.append(dup)
        dys.append(dy)
        dmids.append(dmid)
    dmid = join(dmids)
    act, dup_all, _ = lax.optimization_barrier((join(acts), join(dups), dout))
    last = join(mids) + sum_tensor(dot(act, down_w, 1, 1))
    grads_second = [
        dot(join(dys), join(mixed_parts), 0, 0),
        dot(join(normed_parts), dup_all, 0, 0),
        dot(cotangent, act, 0, 0),
    ]
    grads_second = [
        lax.psum_scatter(grad.astype(BF), "seq", scatter_dimension=0, tiled=True).astype(F32)
        for grad in grads_second
    ]

    pieces = jnp.concatenate([own_piece[None], others], axis=0)
    dquery, dpieces = attention_backward(ends, me, recv, pieces, douts, out_head, lse, group)
    dpiece = dpieces[0].astype(F32)
    for by in range(1, group):
        dpiece = dpiece + swap_core(dpieces[by], by).astype(F32)
    dheads = to_owners(jnp.concatenate([dquery, dpiece.astype(BF)], axis=1))
    dheads = dheads.reshape(heads, group, 3, HEAD_DIM, rows)
    dheads = dheads.transpose(1, 4, 2, 0, 3).reshape(own_rows, 3 * columns)

    dnormed_one = sum_tensor(dot(dheads, w_first, 1, 1))
    norm_one_back = jax.vjp(layer_norm, stream, gains[0], biases[0])[1]
    dstream_norm, dgain_one, dbias_one = norm_one_back(dnormed_one)
    dstream = dmid + dstream_norm
    grads_first = dot(normed_one, dheads, 0, 0).astype(BF)
    grads_first = lax.psum_scatter(grads_first, "seq", scatter_dimension=0, tiled=True)
    norm_grads = jnp.stack([dgain_one, dgain_two, dbias_one, dbias_two])
    norm_grads = norm_grads.reshape(4, devices, -1).transpose(1, 0, 2)
    norm_grads = jnp.sum(to_owners(norm_grads), axis=0)

    grads_first = grads_first.astype(F32).reshape(1, -1, 3, columns)
    return (
        last.astype(BF),
        dstream,
        grads_first[:, :, 0],
        grads_first[:, :, 1],
        grads_first[:, :, 2],
        grads_second[0].T[None],
        grads_second[1][None],
        grads_second[2].T[None],
        norm_grads[None, 0:2],
        norm_grads[None, 2:4],
    )


def solution(mesh):
    placed = (
        P("seq", None),
        P(),
        P(None, "seq", "tensor"),
        P(None, "seq", "tensor"),
        P(None, "seq", "tensor"),
        P(None, "tensor", "seq"),
        P(None, "seq", "tensor"),
        P(None, "tensor", "seq"),
        P(None, None, "seq"),
        P(None, None, "seq"),
        P("seq", None),
    )
    return jax.shard_map(
        per_device,
        mesh=mesh,
        in_specs=placed,
        out_specs=(
            P("seq", None),
            P("seq", None),
            P(None, "seq", "tensor"),
            P(None, "seq", "tensor"),
            P(None, "seq", "tensor"),
            P(None, "tensor", "seq"),
            P(None, "seq", "tensor"),
            P(None, "tensor", "seq"),
            P(None, None, "seq"),
            P(None, None, "seq"),
        ),
        check_vma=False,
    )
```

```python
import functools

import jax
import jax.numpy as jnp
from jax import lax
from jax.experimental import pallas as pl
from jax.experimental.pallas import tpu as pltpu
from jax.sharding import PartitionSpec as P

HEAD_DIM = 64
BF = jnp.bfloat16
F32 = jnp.float32
norm_eps = 1e-06
neg_large = -1e30
log2_e = 1.4426950408889634
ln_2 = 0.6931471805599453
STAT_ROWS = 3
SAFE_BOUND = 60.0
VMEM_BYTES = 56 * 2**20


def dot(left, right, left_dim, right_dim):
    return lax.dot_general(
        left, right, (((left_dim,), (right_dim,)), ((), ())), preferred_element_type=F32
    )


def ring_of(devices):
    chips = devices // 2
    index = lax.axis_index("seq")
    core = lax.rem(index, 2)
    chip = index // 2
    if chips != 8:
        return chip, core, lambda place: 2 * place + core
    layer, column = chip // 2, lax.rem(chip, 2)
    place = layer + column * (7 - 2 * layer)

    def seq_index(place):
        side = place // 4
        depth = place + side * (7 - 2 * place)
        return depth * 4 + side * 2 + core

    return place, core, seq_index


def remote_copy(source, target, send_sem, recv_sem, seq):
    return pltpu.make_async_remote_copy(
        src_ref=source, dst_ref=target, send_sem=send_sem, recv_sem=recv_sem,
        device_id={"seq": seq}, device_id_type=pl.DeviceIdType.MESH,
    )


def meet(others):
    barrier = pltpu.get_barrier_semaphore()
    for other in others:
        pl.semaphore_signal(
            barrier, inc=1, device_id=other, device_id_type=pl.DeviceIdType.MESH
        )
    pl.semaphore_wait(barrier, len(others))


def project_kernel(
    tokens_ref, query_ref, key_ref, value_ref, gain_ref, bias_ref,
    sent_ref, normed_ref, weights_ref, norms_ref,
    gathered, scaled, send_right, recv_right, send_left, recv_left, send_peer, recv_peer,
    out_sem,
    *, devices, group, columns, width,
):
    chips = devices // 2
    depth = width // devices
    rows = tokens_ref.shape[0] // group
    place, core, seq_index = ring_of(devices)
    me = seq_index(place)
    right = seq_index(lax.rem(place + 1, chips))
    left = seq_index(lax.rem(place + chips - 1, chips))
    peer = me + 1 - 2 * core
    heads = columns // HEAD_DIM
    meet([{"seq": right}, {"seq": left}, {"seq": peer}])

    def slot(index):
        return gathered.at[pl.ds(pl.multiple_of(index * depth, depth), depth), :]

    mine = pl.ds(pl.multiple_of(me * depth, depth), depth)
    for which, ref in enumerate((query_ref, key_ref, value_ref)):
        gathered[mine, which * columns : (which + 1) * columns] = ref[0]
    norm_rows = jnp.concatenate(
        [gain_ref[0].astype(F32), bias_ref[0].astype(F32), jnp.zeros((124, depth), F32)], axis=0
    )
    gathered[mine, 3 * columns :] = norm_rows.T.astype(BF)

    to_right, to_left = chips // 2, chips - 1 - chips // 2

    def rightward(step):
        index = seq_index(lax.rem(place - step + chips, chips))
        return remote_copy(
            slot(index), slot(index), send_right.at[step], recv_right.at[step], right
        )

    def leftward(step):
        index = seq_index(lax.rem(place + step, chips))
        return remote_copy(slot(index), slot(index), send_left.at[step], recv_left.at[step], left)

    def across(distance):
        index = seq_index(lax.rem(place + distance + chips, chips))
        return remote_copy(
            slot(index), slot(index),
            send_peer.at[(distance + chips) % chips], recv_peer.at[(distance + chips) % chips], peer,
        )

    def arrive_right(step):
        index = seq_index(lax.rem(place - step - 1 + chips, chips))
        remote_copy(
            slot(index), slot(index), send_right.at[step], recv_right.at[step], right
        ).wait_recv()

    def arrive_left(step):
        index = seq_index(lax.rem(place + step + 1, chips))
        remote_copy(
            slot(index), slot(index), send_left.at[step], recv_left.at[step], left
        ).wait_recv()

    rightward(0).start()
    leftward(0).start()
    across(0).start()

    def normalize(index, carry):
        at = pl.ds(pl.multiple_of(index * 128, 128), 128)
        stream = tokens_ref[at, :].astype(F32)
        centred = stream - jnp.mean(stream, axis=-1, keepdims=True)
        spread = jnp.mean(centred * centred, axis=-1, keepdims=True)
        scaled[at, :] = centred * lax.rsqrt(spread + norm_eps)
        return carry

    lax.fori_loop(0, tokens_ref.shape[0] // 128, normalize, 0)

    for step in range(to_right):
        arrive_right(step)
        if step + 1 < to_right:
            rightward(step + 1).start()
        across(-step - 1).start()
        if step < to_left:
            arrive_left(step)
            if step + 1 < to_left:
                leftward(step + 1).start()
            across(step + 1).start()
    for distance in range(chips):
        index = seq_index(lax.rem(place + distance, chips)) + 1 - 2 * core
        remote_copy(
            slot(index), slot(index), send_peer.at[distance], recv_peer.at[distance], peer
        ).wait_recv()

    store = pltpu.make_async_copy(gathered.at[:, : 3 * columns], weights_ref, out_sem)
    store.start()
    norms = gathered[:, 3 * columns :].astype(F32).T
    norms_ref[...] = norms[0:8]

    def apply_norm(index, carry):
        at = pl.ds(pl.multiple_of(index * 128, 128), 128)
        normed_ref[at, :] = (scaled[at, :] * norms[0:1] + norms[2:3]).astype(BF)
        return carry

    lax.fori_loop(0, tokens_ref.shape[0] // 128, apply_norm, 0)
    for which in range(3):
        weights = gathered[:, which * columns : (which + 1) * columns].T
        factor = HEAD_DIM**-0.5 * log2_e if which == 0 else 1.0

        def project(core_index, carry, which=which, weights=weights, factor=factor):
            at = pl.ds(pl.multiple_of(core_index * rows, rows), rows)
            result = (dot(weights, normed_ref[at, :], 1, 1) * factor).astype(BF)
            for head in range(heads):
                sent_ref[head * group + core_index, which * HEAD_DIM : (which + 1) * HEAD_DIM, :] = (
                    result[head * HEAD_DIM : (head + 1) * HEAD_DIM, :]
                )
            return carry

        lax.fori_loop(0, group, project, 0)
    for step in range(to_right):
        rightward(step).wait_send()
    for step in range(to_left):
        leftward(step).wait_send()
    for distance in range(chips):
        across(distance).wait_send()
    store.wait()


def project(tokens, w_query, w_key, w_value, norm_gain, norm_bias, devices, group):
    own_rows, width = tokens.shape
    columns = w_query.shape[2]
    chips = devices // 2
    whole = pl.BlockSpec(memory_space=pltpu.VMEM)
    dma = pltpu.SemaphoreType.DMA
    return pl.pallas_call(
        functools.partial(
            project_kernel, devices=devices, group=group, columns=columns, width=width
        ),
        in_specs=[whole] * 6,
        out_specs=[whole, whole, pl.BlockSpec(memory_space=pl.ANY), whole],
        out_shape=[
            jax.ShapeDtypeStruct((devices, 3 * HEAD_DIM, own_rows // group), BF),
            jax.ShapeDtypeStruct((own_rows, width), BF),
            jax.ShapeDtypeStruct((width, 3 * columns), BF),
            jax.ShapeDtypeStruct((8, width), F32),
        ],
        scratch_shapes=[
            pltpu.VMEM((width, 3 * columns + 128), BF),
            pltpu.VMEM((own_rows, width), F32),
            dma((chips // 2,)), dma((chips // 2,)),
            dma((chips // 2,)), dma((chips // 2,)),
            dma((chips,)), dma((chips,)),
            dma,
        ],
        compiler_params=pltpu.CompilerParams(
            vmem_limit_bytes=VMEM_BYTES, collective_id=1, has_side_effects=True
        ),
        name="project",
    )(tokens, w_query, w_key, w_value, norm_gain, norm_bias)


def finish_kernel(
    dheads_ref, normed_ref, weights_ref, tokens_ref, dmid_ref, norms_ref, second_ref,
    dstream_ref, dquery_ref, dkey_ref, dvalue_ref, dgain_ref, dbias_ref,
    flat, partial_sent, partial_got, partial, from_peer, first_right, first_left,
    ring_right, ring_left, total, few_sent, few_got,
    x_send, x_recv, peer_send, peer_recv, right_send, right_recv, left_send, left_recv,
    few_send, few_recv,
    *, devices, group, columns, width,
):
    chips = devices // 2
    depth = width // devices
    own_rows = tokens_ref.shape[0]
    rows = own_rows // group
    heads = columns // HEAD_DIM
    wide = 3 * columns + 128
    cut = first_right.shape[1]
    place, core, seq_index = ring_of(devices)
    me = seq_index(place)
    right = {"seq": seq_index(lax.rem(place + 1, chips))}
    left = {"seq": seq_index(lax.rem(place + chips - 1, chips))}
    peer = {"seq": me + 1 - 2 * core}
    across = {"tensor": 1 - lax.axis_index("tensor")}
    meet([right, left, peer, across])

    def copy_to(source, target, send_sem, recv_sem, where):
        return pltpu.make_async_remote_copy(
            src_ref=source, dst_ref=target, send_sem=send_sem, recv_sem=recv_sem,
            device_id=where, device_id_type=pl.DeviceIdType.MESH,
        )

    def flatten(index, carry):
        head = index // group
        part = lax.rem(index, group)
        at = pl.ds(pl.multiple_of(part * rows, rows), rows)
        for which in range(3):
            to = pl.ds(
                pl.multiple_of(which * columns + head * HEAD_DIM, HEAD_DIM), HEAD_DIM
            )
            flat[to, at] = dheads_ref[index, which * HEAD_DIM : (which + 1) * HEAD_DIM, :]
        return carry

    lax.fori_loop(0, devices, flatten, 0)

    parts = 4
    part_rows = own_rows // parts

    def x_copy(part):
        at = pl.ds(part * part_rows, part_rows)
        return copy_to(
            partial_sent.at[at, :], partial_got.at[at, :], x_send.at[part], x_recv.at[part], across
        )

    def unit_rows(at):
        stream = tokens_ref[at, :].astype(F32)
        centred = stream - jnp.mean(stream, axis=-1, keepdims=True)
        spread = jnp.mean(centred * centred, axis=-1, keepdims=True)
        inverse = lax.rsqrt(spread + norm_eps)
        return centred * inverse, inverse

    gain_sum = jnp.zeros((1, width), F32)
    bias_sum = jnp.zeros((1, width), F32)
    for part in range(parts):
        at = pl.ds(part * part_rows, part_rows)
        result = dot(flat[:, at].T, weights_ref[...], 1, 1)
        partial_sent[at, :] = result.astype(BF)
        x_copy(part).start()
        unit, _ = unit_rows(at)
        gain_sum = gain_sum + jnp.sum(result * unit, axis=0, keepdims=True)
        bias_sum = bias_sum + jnp.sum(result, axis=0, keepdims=True)

    lines = 256
    for line in range(width // lines):
        at = slice(line * lines, (line + 1) * lines)
        partial[at, 0 : 3 * columns] = dot(normed_ref[:, at].T, flat[...], 1, 1).astype(BF)
    norm_rows = jnp.concatenate(
        [
            gain_sum, second_ref[0:1, :] * 0.5, bias_sum, second_ref[1:2, :] * 0.5,
            jnp.zeros((124, width), F32),
        ],
        axis=0,
    )
    partial[:, 3 * columns :] = norm_rows.T.astype(BF)

    order = []
    for step in range(chips // 2):
        for offset in (-step - 1, step + 1):
            if offset % chips not in order:
                order.append(offset % chips)
    order.append(0)

    def peer_copy(number):
        where = lax.rem(place + order[number], chips)
        theirs = seq_index(where) + 1 - 2 * core
        return copy_to(
            partial.at[pl.ds(pl.multiple_of(theirs * depth, depth), depth), :],
            from_peer.at[pl.ds(pl.multiple_of(where * depth, depth), depth), :],
            peer_send.at[number], peer_recv.at[number], peer,
        )

    for number in range(chips):
        peer_copy(number).start()

    waited = []

    def chip_block(offset, low, high):
        number = order.index(offset % chips)
        if number not in waited:
            peer_copy(number).wait_recv()
            waited.append(number)
        where = lax.rem(place + offset % chips, chips)
        own = pl.ds(pl.multiple_of(seq_index(where) * depth, depth), depth)
        got = pl.ds(pl.multiple_of(where * depth, depth), depth)
        return partial[own, low:high].astype(F32) + from_peer[got, low:high].astype(F32)

    def finish_norm(part):
        x_copy(part).wait_recv()

        def piece(index, carry):
            at = pl.ds(pl.multiple_of(part * part_rows + index * 128, 128), 128)
            dnormed = partial_sent[at, :].astype(F32) + partial_got[at, :].astype(F32)
            unit, inverse = unit_rows(at)
            dunit = dnormed * norms_ref[0:1, :]
            mean = jnp.mean(dunit, axis=-1, keepdims=True)
            along = jnp.mean(dunit * unit, axis=-1, keepdims=True)
            dstream_ref[at, :] = dmid_ref[at, :] + (dunit - mean - unit * along) * inverse
            return carry

        lax.fori_loop(0, part_rows // 128, piece, 0)

    steps = chips - 1

    def ring_copy(step, toward_right):
        if toward_right:
            source = first_right if step == 0 else ring_right.at[step - 1]
            return copy_to(
                source, ring_right.at[step], right_send.at[step], right_recv.at[step], right
            )
        source = first_left if step == 0 else ring_left.at[step - 1]
        return copy_to(source, ring_left.at[step], left_send.at[step], left_recv.at[step], left)

    first_right[...] = chip_block(-1, 0, cut).astype(BF)
    ring_copy(0, True).start()
    first_left[...] = chip_block(1, cut, wide).astype(BF)
    ring_copy(0, False).start()
    for step in range(steps):
        if step in (0, steps // 2, steps - 1):
            finish_norm((0, steps // 2, steps - 1).index(step))
        for toward_right, ring, low, high in (
            (True, ring_right, 0, cut), (False, ring_left, cut, wide),
        ):
            ring_copy(step, toward_right).wait_recv()
            offset = -step - 2 if toward_right else step + 2
            summed = ring[step].astype(F32) + chip_block(offset, low, high)
            if step + 1 < steps:
                ring[step] = summed.astype(BF)
                ring_copy(step + 1, toward_right).start()
            else:
                total[:, low:high] = summed
    few_sent[...] = total[:, 3 * columns :]
    few = copy_to(few_sent, few_got, few_send, few_recv, across)
    few.start()
    dquery_ref[0] = total[:, 0:columns]
    dkey_ref[0] = total[:, columns : 2 * columns]
    dvalue_ref[0] = total[:, 2 * columns : 3 * columns]
    finish_norm(3)
    few.wait()
    norm_rows = (few_sent[...] + few_got[...]).T
    dgain_ref[0] = norm_rows[0:2, :]
    dbias_ref[0] = norm_rows[2:4, :]
    for part in range(parts):
        x_copy(part).wait_send()
    for number in range(chips):
        peer_copy(number).wait_send()
    for step in range(steps):
        ring_copy(step, True).wait_send()
        ring_copy(step, False).wait_send()


def finish(dheads, normed, weights, tokens, dmid, norms, second, devices, group):
    own_rows, width = tokens.shape
    columns = weights.shape[1] // 3
    chips = devices // 2
    depth = width // devices
    wide = 3 * columns + 128
    cut = (wide // 128 + 1) // 2 * 128
    steps = chips - 1
    whole = pl.BlockSpec(memory_space=pltpu.VMEM)
    dma = pltpu.SemaphoreType.DMA
    return pl.pallas_call(
        functools.partial(
            finish_kernel, devices=devices, group=group, columns=columns, width=width
        ),
        in_specs=[whole] * 7,
        out_specs=[whole] * 6,
        out_shape=[jax.ShapeDtypeStruct((own_rows, width), F32)]
        + [jax.ShapeDtypeStruct((1, depth, columns), F32)] * 3
        + [jax.ShapeDtypeStruct((1, 2, depth), F32)] * 2,
        scratch_shapes=[
            pltpu.VMEM((3 * columns, own_rows), BF),
            pltpu.VMEM((own_rows, width), BF),
            pltpu.VMEM((own_rows, width), BF),
            pltpu.VMEM((width, wide), BF),
            pltpu.VMEM((chips * depth, wide), BF),
            pltpu.VMEM((depth, cut), BF),
            pltpu.VMEM((depth, wide - cut), BF),
            pltpu.VMEM((steps, depth, cut), BF),
            pltpu.VMEM((steps, depth, wide - cut), BF),
            pltpu.VMEM((depth, wide), F32),
            pltpu.VMEM((depth, 128), F32),
            pltpu.VMEM((depth, 128), F32),
            dma((4,)), dma((4,)),
            dma((chips,)), dma((chips,)),
            dma((steps,)), dma((steps,)),
            dma((steps,)), dma((steps,)),
            dma, dma,
        ],
        compiler_params=pltpu.CompilerParams(
            vmem_limit_bytes=VMEM_BYTES, collective_id=2, has_side_effects=True
        ),
        name="finish",
    )(dheads, normed, weights, tokens, dmid, norms, second)


def middle_kernel(
    mixed_ref, tokens_ref, dz_ref, second_ref, norms_ref,
    dout_ref, dmid_ref, mid_ref, z_ref, grads_ref, norm_grads_ref,
    weights, tokens, dz, flat, flat_other, normed, act, dup, mid, dmid, dsent, dgot, dy, z,
    out_t, dout, stage,
    load_sem, flat_send, flat_recv, x_send, x_recv, head_send, head_recv, store_sem, stage_sem,
    *, devices, group, columns, hidden,
):
    own_rows, width = tokens.shape
    rows = own_rows // group
    heads = columns // HEAD_DIM
    parts = x_send.shape[0]
    part_rows = own_rows // parts
    block = 512
    me = lax.axis_index("seq").astype(jnp.int32)
    core = lax.rem(me, group)
    half = lax.axis_index("tensor").astype(jnp.int32)
    across = {"tensor": 1 - half}

    loads = [
        pltpu.make_async_copy(second_ref.at[:, 0:width], weights.at[:, 0:width], load_sem.at[0]),
        pltpu.make_async_copy(tokens_ref, tokens, load_sem.at[1]),
        pltpu.make_async_copy(second_ref.at[:, width:], weights.at[:, width:], load_sem.at[2]),
        pltpu.make_async_copy(dz_ref, dz, load_sem.at[3]),
    ]
    for load in loads:
        load.start()

    barrier = pltpu.get_barrier_semaphore()
    for other in range(devices):
        @pl.when(me != other)
        def _(other=other):
            pl.semaphore_signal(
                barrier, inc=1, device_id={"seq": other}, device_id_type=pl.DeviceIdType.MESH
            )

    pl.semaphore_signal(
        barrier, inc=1, device_id=across, device_id_type=pl.DeviceIdType.MESH
    )
    pl.semaphore_wait(barrier, devices)

    def copy_to(source, target, send_sem, recv_sem, where):
        return pltpu.make_async_remote_copy(
            src_ref=source, dst_ref=target, send_sem=send_sem, recv_sem=recv_sem,
            device_id=where, device_id_type=pl.DeviceIdType.MESH,
        )

    def rows_of(part):
        return pl.ds(pl.multiple_of(part * part_rows, part_rows), part_rows)

    def flatten(index, carry):
        head = index // group
        at = pl.ds(pl.multiple_of(lax.rem(index, group) * rows, rows), rows)
        flat[pl.ds(pl.multiple_of(head * HEAD_DIM, HEAD_DIM), HEAD_DIM), at] = mixed_ref[index]
        return carry

    lax.fori_loop(0, devices, flatten, 0)

    def flat_copy(part):
        at = rows_of(part)
        return copy_to(
            flat.at[:, at], flat_other.at[:, at], flat_send.at[part], flat_recv.at[part], across
        )

    def x_copy(part):
        at = rows_of(part)
        return copy_to(dsent.at[at, :], dgot.at[at, :], x_send.at[part], x_recv.at[part], across)

    for part in range(parts):
        flat_copy(part).start()
    loads[0].wait()
    out_t[...] = weights[:, pl.ds(pl.multiple_of(half * columns, columns), columns)].T
    for load in loads[1:]:
        load.wait()
    first_half = half == 0

    def unit_rows(at):
        stream = mid[at, :]
        centred = stream - jnp.mean(stream, axis=-1, keepdims=True)
        spread = jnp.mean(centred * centred, axis=-1, keepdims=True)
        inverse = lax.rsqrt(spread + norm_eps)
        return centred * inverse, inverse

    def store_mid(part):
        at = rows_of(part)
        return pltpu.make_async_copy(mid.at[at, :], mid_ref.at[at, :], store_sem.at[0, part])

    def forward(part, carry):
        at = rows_of(part)
        flat_copy(part).wait_recv()
        own, other = flat[:, at], flat_other[:, at]
        low = jnp.where(first_half, own, other).T
        high = jnp.where(first_half, other, own).T
        projected = dot(low, weights[:, 0:columns], 1, 1) + dot(
            high, weights[:, columns:width], 1, 1
        )
        mid[at, :] = tokens[at, :].astype(F32) + projected
        store_mid(part).start()
        unit, _ = unit_rows(at)
        normed[at, :] = (unit * norms_ref[1:2, :] + norms_ref[3:4, :]).astype(BF)

        def hidden_block(index, total):
            cut = pl.ds(pl.multiple_of(index * block, block), block)
            up_cut = pl.ds(pl.multiple_of(width + index * block, block), block)
            down_cut = pl.ds(pl.multiple_of(width + hidden + index * block, block), block)
            up_w = weights[:, up_cut]
            up = dot(normed[at, :], up_w, 1, 0)
            dact = dot(dz[at, :], weights[:, down_cut], 1, 0)
            square = up * up
            bend = jnp.tanh(0.7978845608028654 * up * (1.0 + 0.044715 * square))
            grow = 0.5 + 0.5 * bend
            slope = grow + 0.5 * up * (1.0 - bend * bend) * (
                0.7978845608028654 + 0.10703222440890037 * square
            )
            act[at, cut] = (up * grow).astype(BF)
            dup_block = (dact * slope).astype(BF)
            dup[at, cut] = dup_block
            return total + dot(dup_block, up_w, 1, 1)

        total = lax.fori_loop(
            0, hidden // block, hidden_block, jnp.zeros((part_rows, width), F32)
        )
        dsent[at, :] = total.astype(BF)
        x_copy(part).start()
        return carry

    lax.fori_loop(0, parts, forward, 0)

    piece_rows = min(part_rows, rows)
    pieces = rows // piece_rows

    def head_copies(piece, head):
        start = piece * piece_rows
        owner = head * group + start // rows
        slot = lax.rem(piece, pieces)
        source = dout.at[
            pl.ds(pl.multiple_of(head * HEAD_DIM, HEAD_DIM), HEAD_DIM),
            pl.ds(pl.multiple_of(start, piece_rows), piece_rows),
        ]
        target = dout_ref.at[me, :, pl.ds(pl.multiple_of(slot * piece_rows, piece_rows), piece_rows)]
        away = copy_to(
            source, target, head_send.at[head, piece], head_recv.at[me, slot], {"seq": owner}
        )
        home = pltpu.make_async_copy(source, target, head_send.at[head, piece])
        return away, home, owner == me

    def send_heads(part):
        def send(index, carry):
            piece = part * (part_rows // piece_rows) + index // heads
            away, home, is_home = head_copies(piece, lax.rem(index, heads))

            @pl.when(is_home)
            def _():
                home.start()

            @pl.when(jnp.logical_not(is_home))
            def _():
                away.start()

            return carry

        lax.fori_loop(0, heads * (part_rows // piece_rows), send, 0)

    def store_dmid(part):
        at = rows_of(part)
        return pltpu.make_async_copy(dmid.at[at, :], dmid_ref.at[at, :], store_sem.at[1, part])

    def backward(part, sums):
        gain_sum, bias_sum = sums
        at = rows_of(part)
        x_copy(part).wait_recv()
        dnormed = dsent[at, :].astype(F32) + dgot[at, :].astype(F32)
        unit, inverse = unit_rows(at)
        dunit = dnormed * norms_ref[1:2, :]
        mean = jnp.mean(dunit, axis=-1, keepdims=True)
        along = jnp.mean(dunit * unit, axis=-1, keepdims=True)
        result = dz[at, :].astype(F32) + (dunit - mean - unit * along) * inverse
        dmid[at, :] = result
        store_dmid(part).start()
        low = result.astype(BF)
        dy[at, :] = low
        dout[:, at] = dot(out_t[...], low, 1, 1).astype(BF)
        send_heads(part)
        gain_sum = gain_sum + jnp.sum(dnormed * unit, axis=0, keepdims=True)
        bias_sum = bias_sum + jnp.sum(dnormed, axis=0, keepdims=True)
        return gain_sum, bias_sum

    def last_product(part, carry):
        at = rows_of(part)
        z[at, :] = dot(act[at, :], weights[:, width + hidden :], 1, 1).astype(BF)
        return carry

    lax.fori_loop(0, parts, last_product, 0)
    store_z = pltpu.make_async_copy(z, z_ref, load_sem.at[0])
    store_z.start()

    def grads_into(left_t, right_ref, first_column):
        blocks = right_ref.shape[1] // block

        def store(index, slot):
            cut = pl.ds(pl.multiple_of(first_column + index * block, block), block)
            return pltpu.make_async_copy(stage.at[slot], grads_ref.at[:, cut], stage_sem.at[slot])

        def one(index, carry):
            slot = lax.rem(index, 2)

            @pl.when(index >= 2)
            def _():
                store(index - 2, slot).wait()

            cut = pl.ds(pl.multiple_of(index * block, block), block)
            stage[slot] = dot(left_t, right_ref[:, cut], 1, 0).astype(BF)
            store(index, slot).start()
            return carry

        lax.fori_loop(0, blocks, one, 0)
        for index in range(blocks - 2, blocks):
            store(index, index % 2).wait()

    sums = (jnp.zeros((1, width), F32), jnp.zeros((1, width), F32))
    sums = backward(0, sums)
    grads_into(normed[...].T, dup, columns)
    sums = backward(1, sums)
    grads_into(dz[...].T, act, columns + hidden)
    for part in range(2, parts):
        sums = backward(part, sums)
    stage[0] = dot(dy[...].T, flat[...], 1, 1).astype(BF)
    store_out = pltpu.make_async_copy(stage.at[0], grads_ref.at[:, 0:columns], stage_sem.at[0])
    store_out.start()
    norm_grads_ref[...] = jnp.concatenate([*sums, jnp.zeros((6, width), F32)], axis=0)

    def wait_sent(index, carry):
        away, home, is_home = head_copies(index // heads, lax.rem(index, heads))

        @pl.when(is_home)
        def _():
            home.wait()

        @pl.when(jnp.logical_not(is_home))
        def _():
            away.wait_send()

        return carry

    lax.fori_loop(0, heads * (own_rows // piece_rows), wait_sent, 0)

    def wait_heads(index, carry):
        source = index // pieces
        slot = lax.rem(index, pieces)
        cut = pl.ds(pl.multiple_of(slot * piece_rows, piece_rows), piece_rows)

        @pl.when(source != me)
        def _():
            copy_to(
                dout.at[0:HEAD_DIM, 0:piece_rows], dout_ref.at[source, :, cut],
                head_send.at[0, 0], head_recv.at[source, slot], {"seq": source},
            ).wait_recv()

        return carry

    lax.fori_loop(0, devices * pieces, wait_heads, 0)
    for part in range(parts):
        flat_copy(part).wait_send()
        x_copy(part).wait_send()
        store_mid(part).wait()
        store_dmid(part).wait()
    store_z.wait()
    store_out.wait()


def middle(mixed, tokens, dz, second, norms, devices, group, columns):
    own_rows, width = tokens.shape
    rows = own_rows // group
    hidden = (second.shape[1] - width) // 2
    parts = 4
    piece_rows = min(own_rows // parts, rows)
    whole = pl.BlockSpec(memory_space=pltpu.VMEM)
    far = pl.BlockSpec(memory_space=pl.ANY)
    dma = pltpu.SemaphoreType.DMA
    vmem = pltpu.VMEM
    return pl.pallas_call(
        functools.partial(
            middle_kernel, devices=devices, group=group, columns=columns, hidden=hidden
        ),
        in_specs=[whole, far, far, far, whole],
        out_specs=[far] * 5 + [whole],
        out_shape=[
            jax.ShapeDtypeStruct((devices, HEAD_DIM, rows), BF),
            jax.ShapeDtypeStruct((own_rows, width), F32),
            jax.ShapeDtypeStruct((own_rows, width), F32),
            jax.ShapeDtypeStruct((own_rows, width), BF),
            jax.ShapeDtypeStruct((width, columns + 2 * hidden), BF),
            jax.ShapeDtypeStruct((8, width), F32),
        ],
        scratch_shapes=[
            vmem((width, width + 2 * hidden), BF),
            vmem((own_rows, width), BF), vmem((own_rows, width), BF),
            vmem((columns, own_rows), BF), vmem((columns, own_rows), BF),
            vmem((own_rows, width), BF),
            vmem((own_rows, hidden), BF), vmem((own_rows, hidden), BF),
            vmem((own_rows, width), F32), vmem((own_rows, width), F32),
            vmem((own_rows, width), BF), vmem((own_rows, width), BF),
            vmem((own_rows, width), BF), vmem((own_rows, width), BF),
            vmem((columns, width), BF), vmem((columns, own_rows), BF),
            vmem((2, width, 512), BF),
            dma((4,)), dma((parts,)), dma((parts,)), dma((parts,)), dma((parts,)),
            dma((columns // HEAD_DIM, own_rows // piece_rows)),
            dma((devices, rows // piece_rows)),
            dma((2, parts)), dma((2,)),
        ],
        compiler_params=pltpu.CompilerParams(
            vmem_limit_bytes=60 * 2**20, collective_id=3, has_side_effects=True
        ),
        name="middle",
    )(mixed, tokens, dz, second, norms)


def scene_span(ends_ref, scenes, first, last):
    low = jnp.int32(0)
    high = ends_ref[scenes - 1]
    for scene in range(scenes):
        low = jnp.where(first >= ends_ref[scene], ends_ref[scene], low)
    for scene in reversed(range(scenes)):
        high = jnp.where(last < ends_ref[scene], ends_ref[scene], high)
    return low, high


def scene_inside(ends_ref, scenes, row, position):
    start = jnp.zeros_like(row)
    end = jnp.zeros_like(row)
    before = jnp.int32(0)
    for scene in range(scenes):
        start = jnp.where(row == STAT_ROWS + scene, before, start)
        end = jnp.where(row == STAT_ROWS + scene, ends_ref[scene], end)
        before = ends_ref[scene]
    return (position >= start) & (position < end)


def key_extra(ends_ref, scenes, first, rows):
    row = lax.broadcasted_iota(jnp.int32, (64, rows), 0)
    position = first + lax.broadcasted_iota(jnp.int32, (64, rows), 1)
    inside = scene_inside(ends_ref, scenes, row, position)
    return jnp.where(row < STAT_ROWS, -1.0, jnp.where(inside, 1.0, 0.0)).astype(BF)


def query_extra(ends_ref, scenes, first, rows, stat):
    row = lax.broadcasted_iota(jnp.int32, (64, rows), 0)
    position = first + lax.broadcasted_iota(jnp.int32, (64, rows), 1)
    inside = scene_inside(ends_ref, scenes, row, position)
    is_scene = (row >= STAT_ROWS) & (row < STAT_ROWS + scenes)
    extra = jnp.where(is_scene & jnp.logical_not(inside), neg_large, 0.0)
    if stat is not None:
        extra = stat_rows(row, stat, extra)
    return extra.astype(BF)


def stat_rows(row, stat, extra):
    top = stat.astype(BF).astype(F32)
    middle = (stat - top).astype(BF).astype(F32)
    bottom = stat - top - middle
    extra = jnp.where(row == 0, top, extra)
    extra = jnp.where(row == 1, middle, extra)
    return jnp.where(row == 2, bottom, extra)


def walk_tiles(process, state, first, count, unit, sizes):
    at = first
    left = count
    for size in sizes:
        steps = left // size
        begin = at

        def step(index, carry, begin=begin, size=size):
            offset = pl.multiple_of((begin + index * size) * unit, unit)
            return process(offset, size * unit, carry)

        state = lax.fori_loop(0, steps, step, state)
        at = at + steps * size
        left = left - steps * size
    return state


def forward_kernel(
    ends_ref, me_ref, recv_ref, other_ref, out_ref, lse_ref, keys, values, key_top,
    *, scenes, group, total,
):
    block = pl.program_id(0)
    core = me_ref[0]
    sources = recv_ref.shape[0]
    rows = recv_ref.shape[2]

    @pl.when(block == 0)
    def _():
        values[64:80, :] = jnp.ones((16, total), BF)
        key_top[0] = 0.0
        for piece in range(group):
            place = core ^ piece

            def load(source, carry, piece=piece, place=place):
                first = pl.multiple_of((source * group + place) * rows, rows)
                if piece == 0:
                    key = recv_ref[source, 64:128, :]
                    value = recv_ref[source, 128:192, :]
                else:
                    key = other_ref[piece - 1, source, 0:64, :]
                    value = other_ref[piece - 1, source, 64:128, :]
                extra = key_extra(ends_ref, scenes, first, rows)
                keys[pl.ds(first, rows), :] = jnp.concatenate([key, extra], axis=0).T
                values[0:64, pl.ds(first, rows)] = value
                wide = key.astype(F32)
                key_top[0] = jnp.maximum(key_top[0], jnp.max(jnp.sum(wide * wide, axis=0)))
                return carry

            lax.fori_loop(0, sources, load, 0)

    first = (block * group + core) * rows
    low, high = scene_span(ends_ref, scenes, first, first + rows - 1)
    query = recv_ref[block, 0:64, :]
    wide = query.astype(F32)
    query_top = jnp.max(jnp.sum(wide * wide, axis=0))
    query = jnp.concatenate([query, query_extra(ends_ref, scenes, first, rows, None)], axis=0)
    unit = 256
    begin = low // unit
    count = (high + unit - 1) // unit - begin
    safe = query_top * key_top[0] <= SAFE_BOUND * SAFE_BOUND

    def scores_of(offset, size):
        return dot(keys[pl.ds(offset, size), :], query, 1, 0)

    def mix(offset, size, weights):
        return dot(values[:, pl.ds(offset, size)], weights.astype(BF), 1, 0)

    def write(total_mix, top):
        summed = total_mix[64:65, :]
        out_ref[0] = (total_mix[0:64, :] / summed).astype(BF)
        lse_ref[0] = top + jnp.log(summed) * log2_e

    @pl.when(safe)
    def _():
        def process(offset, size, carry):
            return carry + mix(offset, size, jnp.exp2(scores_of(offset, size)))

        write(
            walk_tiles(process, jnp.zeros((80, rows), F32), begin, count, unit, (8, 4, 2, 1)),
            0.0,
        )

    @pl.when(jnp.logical_not(safe))
    def _():
        def process(offset, size, carry):
            top, mixed = carry
            scores = scores_of(offset, size)
            new_top = jnp.maximum(top, jnp.max(scores, axis=0, keepdims=True))
            weights = jnp.exp2(scores - new_top)
            return new_top, mixed * jnp.exp2(top - new_top) + mix(offset, size, weights)

        start = (jnp.full((1, rows), neg_large, F32), jnp.zeros((80, rows), F32))
        top, mixed = walk_tiles(process, start, begin, count, unit, (1,))
        write(mixed, top)


def attention_forward(ends, me, recv, other, group):
    sources, _, rows = recv.shape
    total = sources * group * rows
    whole = pl.BlockSpec(memory_space=pltpu.VMEM)
    return pl.pallas_call(
        functools.partial(
            forward_kernel, scenes=ends.shape[0], group=group, total=total
        ),
        grid_spec=pltpu.PrefetchScalarGridSpec(
            num_scalar_prefetch=2,
            grid=(sources,),
            in_specs=[whole, whole],
            out_specs=[
                pl.BlockSpec((1, 64, rows), lambda b, *_: (b, 0, 0)),
                pl.BlockSpec((1, 1, rows), lambda b, *_: (b, 0, 0)),
            ],
            scratch_shapes=[
                pltpu.VMEM((total, 128), BF),
                pltpu.VMEM((80, total), BF),
                pltpu.SMEM((1,), F32),
            ],
        ),
        out_shape=[
            jax.ShapeDtypeStruct((sources, 64, rows), BF),
            jax.ShapeDtypeStruct((sources, 1, rows), F32),
        ],
        compiler_params=pltpu.CompilerParams(vmem_limit_bytes=VMEM_BYTES),
        cost_estimate=pl.CostEstimate(
            flops=60 * 10**9, bytes_accessed=8 * 10**6, transcendentals=45 * 10**6
        ),
        name="attention_forward",
    )(ends, me, recv, other)


def backward_kernel(ends_ref, me_ref, recv_ref, pieces_ref, *refs, scenes, group, parts):
    dout_refs = refs[:parts]
    out_ref, lse_ref, dquery_ref, dkeys_ref = refs[parts : parts + 4]
    queries, douts, queries_flat, douts_flat, dqueries = refs[parts + 4 :]
    block = pl.program_id(0)
    core = me_ref[0]
    sources = recv_ref.shape[0]
    rows = recv_ref.shape[2]
    span = group * rows

    @pl.when(block == 0)
    def _():
        dqueries[...] = jnp.zeros_like(dqueries)

        def load(source, carry):
            first = source * span + core * rows
            at = pl.ds(pl.multiple_of(source * rows, rows), rows)
            query = recv_ref[source, 0:64, :]
            dout = jnp.concatenate([ref[source] for ref in dout_refs], axis=1)
            delta = jnp.sum(
                dout.astype(F32) * out_ref[source].astype(F32), axis=0, keepdims=True
            )
            row = lax.broadcasted_iota(jnp.int32, (64, rows), 0)
            extra = query_extra(ends_ref, scenes, first, rows, lse_ref[source])
            queries[at, :] = jnp.concatenate([query, extra], axis=0).T
            extra = stat_rows(row, delta, jnp.zeros((64, rows), F32)).astype(BF)
            douts[at, :] = jnp.concatenate([dout, extra], axis=0).T
            queries_flat[:, at] = query
            douts_flat[:, at] = dout
            return carry

        lax.fori_loop(0, sources, load, 0)

    source = block // group
    place = block % group
    first = block * rows
    low, high = scene_span(ends_ref, scenes, first, first + rows - 1)
    extra = key_extra(ends_ref, scenes, first, rows)
    key = pieces_ref[0, 0, 0:64, :]
    key_wide = jnp.concatenate([key, extra], axis=0)
    value_wide = jnp.concatenate([pieces_ref[0, 0, 64:128, :], extra], axis=0)
    key_rows = key.T
    begin = (low - core * rows - rows + span) // span
    count = jnp.minimum((high - core * rows + span - 1) // span, sources) - begin

    def process(offset, size, carry):
        dkey, dvalue = carry
        at = pl.ds(offset, size)
        probs = jnp.exp2(dot(queries[at, :], key_wide, 1, 0))
        dprobs = dot(douts[at, :], value_wide, 1, 0)
        dscores = (probs * dprobs).astype(BF)
        dvalue = dvalue + dot(douts_flat[:, at], probs.astype(BF), 1, 0)
        dkey = dkey + dot(queries_flat[:, at], dscores, 1, 0)
        dqueries[at, :] += dot(dscores, key_rows, 1, 0)
        return dkey, dvalue

    zeros = jnp.zeros((64, rows), F32)
    dkey, dvalue = walk_tiles(process, (zeros, zeros), begin, count, rows, (4, 2, 1))
    dkeys_ref[0, 0, 0:64, :] = (dkey * ln_2).astype(BF)
    dkeys_ref[0, 0, 64:128, :] = dvalue.astype(BF)

    @pl.when(block == sources * group - 1)
    def _():
        def store(source, carry):
            at = pl.ds(pl.multiple_of(source * rows, rows), rows)
            dquery_ref[source] = (dqueries[at, :].T * HEAD_DIM**-0.5).astype(BF)
            return carry

        lax.fori_loop(0, sources, store, 0)


def attention_backward(ends, me, recv, pieces, dout, out, lse, group):
    sources, _, rows = recv.shape
    mine = sources * rows
    whole = pl.BlockSpec(memory_space=pltpu.VMEM)

    def piece_map(block, ends_ref, me_ref):
        return ((block % group) ^ me_ref[0], block // group, 0, 0)

    return pl.pallas_call(
        functools.partial(
            backward_kernel, scenes=ends.shape[0], group=group, parts=len(dout)
        ),
        grid_spec=pltpu.PrefetchScalarGridSpec(
            num_scalar_prefetch=2,
            grid=(sources * group,),
            in_specs=[whole, pl.BlockSpec((1, 1, 128, rows), piece_map)] + [whole] * (len(dout) + 2),
            out_specs=[whole, pl.BlockSpec((1, 1, 128, rows), piece_map)],
            scratch_shapes=[
                pltpu.VMEM((mine, 128), BF),
                pltpu.VMEM((mine, 128), BF),
                pltpu.VMEM((64, mine), BF),
                pltpu.VMEM((64, mine), BF),
                pltpu.VMEM((mine, 64), F32),
            ],
        ),
        out_shape=[
            jax.ShapeDtypeStruct((sources, 64, rows), BF),
            jax.ShapeDtypeStruct((group, sources, 128, rows), BF),
        ],
        compiler_params=pltpu.CompilerParams(vmem_limit_bytes=VMEM_BYTES),
        cost_estimate=pl.CostEstimate(
            flops=150 * 10**9, bytes_accessed=20 * 10**6, transcendentals=45 * 10**6
        ),
        name="attention_backward",
    )(ends, me, recv, pieces, *dout, out, lse)


def swap_tensor(part):
    return lax.ppermute(part, "tensor", [(0, 1), (1, 0)])


def per_device(
    tokens, scene_lengths, w_query, w_key, w_value, w_out, w_up, w_down,
    norm_gain, norm_bias, cotangent,
):
    own_rows, width = tokens.shape
    devices = lax.axis_size("seq")
    heads = w_query.shape[2] // HEAD_DIM
    columns = heads * HEAD_DIM
    hidden = w_up.shape[2]
    group = devices // heads
    rows = own_rows // group
    me = lax.rem(lax.axis_index("seq"), group).astype(jnp.int32).reshape(1)
    half = lax.axis_index("tensor")
    ends = jnp.cumsum(scene_lengths).astype(jnp.int32)

    def in_order(part):
        other = swap_tensor(part)
        return jnp.where(
            half == 0,
            jnp.concatenate([part, other], axis=-1),
            jnp.concatenate([other, part], axis=-1),
        )

    def to_owners(parts):
        return lax.all_to_all(parts, "seq", 0, 0, tiled=True)

    projected, normed_one, w_first, norms = project(
        tokens, w_query, w_key, w_value, norm_gain, norm_bias, devices, group
    )
    out_part = in_order(w_out[0].T)
    second_part = jnp.concatenate([out_part, w_up[0], w_down[0].T], axis=1)
    recv = to_owners(projected)
    recv, second_part = lax.optimization_barrier((recv, second_part))
    second_all = lax.all_gather(second_part, "seq", axis=0, tiled=True)
    own_piece = recv[:, HEAD_DIM:, :]

    def swap_core(part, by):
        return lax.ppermute(part, "seq", [(i, i ^ by) for i in range(devices)])

    others = jnp.stack([swap_core(own_piece, by) for by in range(1, group)])
    out_head, lse = attention_forward(ends, me, recv, others, group)

    dout, dmid, mid, z, grads_second, second_norms = middle(
        to_owners(out_head), tokens, cotangent, second_all, norms, devices, group, columns
    )
    grads_second = lax.psum_scatter(grads_second, "seq", scatter_dimension=0, tiled=True)
    grads_second = grads_second.astype(F32)

    pieces = jnp.concatenate([own_piece[None], others], axis=0)
    dquery, dpieces = attention_backward(ends, me, recv, pieces, [dout], out_head, lse, group)
    dpiece = dpieces[0].astype(F32)
    for by in range(1, group):
        dpiece = dpiece + swap_core(dpieces[by], by).astype(F32)
    dsent = jnp.concatenate([dquery, dpiece.astype(BF)], axis=1)
    z, dsent = lax.optimization_barrier((z, dsent))
    dheads = to_owners(dsent)
    last = mid + (z.astype(F32) + swap_tensor(z).astype(F32))
    dstream, dquery_w, dkey_w, dvalue_w, dgain, dbias = finish(
        dheads, normed_one, w_first, tokens, dmid, norms, second_norms, devices, group
    )
    return (
        last.astype(BF),
        dstream,
        dquery_w,
        dkey_w,
        dvalue_w,
        grads_second[:, :columns].T[None],
        grads_second[:, columns : columns + hidden][None],
        grads_second[:, columns + hidden :].T[None],
        dgain,
        dbias,
    )


def solution(mesh):
    placed = (
        P("seq", None),
        P(),
        P(None, "seq", "tensor"),
        P(None, "seq", "tensor"),
        P(None, "seq", "tensor"),
        P(None, "tensor", "seq"),
        P(None, "seq", "tensor"),
        P(None, "tensor", "seq"),
        P(None, None, "seq"),
        P(None, None, "seq"),
        P("seq", None),
    )
    return jax.shard_map(
        per_device,
        mesh=mesh,
        in_specs=placed,
        out_specs=(
            P("seq", None),
            P("seq", None),
            P(None, "seq", "tensor"),
            P(None, "seq", "tensor"),
            P(None, "seq", "tensor"),
            P(None, "tensor", "seq"),
            P(None, "seq", "tensor"),
            P(None, "tensor", "seq"),
            P(None, None, "seq"),
            P(None, None, "seq"),
        ),
        check_vma=False,
    )
```

```python
import functools

import jax
import jax.numpy as jnp
from jax import lax
from jax.experimental import pallas as pl
from jax.experimental.pallas import tpu as pltpu
from jax.sharding import PartitionSpec as P

HEAD_DIM = 64
BF = jnp.bfloat16
F32 = jnp.float32
norm_eps = 1e-06
neg_large = -1e30
log2_e = 1.4426950408889634
ln_2 = 0.6931471805599453
STAT_ROWS = 3
SAFE_BOUND = 60.0
VMEM_BYTES = 56 * 2**20


def dot(left, right, left_dim, right_dim):
    return lax.dot_general(
        left, right, (((left_dim,), (right_dim,)), ((), ())), preferred_element_type=F32
    )


def ring_of(devices):
    chips = devices // 2
    index = lax.axis_index("seq")
    core = lax.rem(index, 2)
    chip = index // 2
    if chips != 8:
        return chip, core, lambda place: 2 * place + core
    layer, column = chip // 2, lax.rem(chip, 2)
    place = layer + column * (7 - 2 * layer)

    def seq_index(place):
        side = place // 4
        depth = place + side * (7 - 2 * place)
        return depth * 4 + side * 2 + core

    return place, core, seq_index


def remote_copy(source, target, send_sem, recv_sem, seq):
    return pltpu.make_async_remote_copy(
        src_ref=source, dst_ref=target, send_sem=send_sem, recv_sem=recv_sem,
        device_id={"seq": seq}, device_id_type=pl.DeviceIdType.MESH,
    )


def meet(others):
    barrier = pltpu.get_barrier_semaphore()
    for other in others:
        pl.semaphore_signal(
            barrier, inc=1, device_id=other, device_id_type=pl.DeviceIdType.MESH
        )
    pl.semaphore_wait(barrier, len(others))


def project_kernel(
    tokens_ref, query_ref, key_ref, value_ref, gain_ref, bias_ref,
    recv_ref, others_ref, normed_ref, weights_ref, norms_ref,
    gathered, scaled, sent, send_right, recv_right, send_left, recv_left, send_peer, recv_peer,
    head_send, head_recv, home_sem, core_send, core_recv, out_sem,
    *, devices, group, columns, width,
):
    chips = devices // 2
    depth = width // devices
    rows = tokens_ref.shape[0] // group
    place, core, seq_index = ring_of(devices)
    me = seq_index(place)
    right = seq_index(lax.rem(place + 1, chips))
    left = seq_index(lax.rem(place + chips - 1, chips))
    peer = me + 1 - 2 * core
    heads = columns // HEAD_DIM
    meet([{"seq": lax.rem(me + step, devices)} for step in range(1, devices)])

    def slot(index):
        return gathered.at[pl.ds(pl.multiple_of(index * depth, depth), depth), :]

    mine = pl.ds(pl.multiple_of(me * depth, depth), depth)
    for which, ref in enumerate((query_ref, key_ref, value_ref)):
        gathered[mine, which * columns : (which + 1) * columns] = ref[0]
    norm_rows = jnp.concatenate(
        [gain_ref[0].astype(F32), bias_ref[0].astype(F32), jnp.zeros((124, depth), F32)], axis=0
    )
    gathered[mine, 3 * columns :] = norm_rows.T.astype(BF)

    to_right, to_left = chips // 2, chips - 1 - chips // 2

    def rightward(step):
        index = seq_index(lax.rem(place - step + chips, chips))
        return remote_copy(
            slot(index), slot(index), send_right.at[step], recv_right.at[step], right
        )

    def leftward(step):
        index = seq_index(lax.rem(place + step, chips))
        return remote_copy(slot(index), slot(index), send_left.at[step], recv_left.at[step], left)

    def across(distance):
        index = seq_index(lax.rem(place + distance + chips, chips))
        return remote_copy(
            slot(index), slot(index),
            send_peer.at[(distance + chips) % chips], recv_peer.at[(distance + chips) % chips], peer,
        )

    def arrive_right(step):
        index = seq_index(lax.rem(place - step - 1 + chips, chips))
        remote_copy(
            slot(index), slot(index), send_right.at[step], recv_right.at[step], right
        ).wait_recv()

    def arrive_left(step):
        index = seq_index(lax.rem(place + step + 1, chips))
        remote_copy(
            slot(index), slot(index), send_left.at[step], recv_left.at[step], left
        ).wait_recv()

    rightward(0).start()
    leftward(0).start()
    across(0).start()

    def normalize(index, carry):
        at = pl.ds(pl.multiple_of(index * 128, 128), 128)
        stream = tokens_ref[at, :].astype(F32)
        centred = stream - jnp.mean(stream, axis=-1, keepdims=True)
        spread = jnp.mean(centred * centred, axis=-1, keepdims=True)
        scaled[at, :] = centred * lax.rsqrt(spread + norm_eps)
        return carry

    lax.fori_loop(0, tokens_ref.shape[0] // 128, normalize, 0)

    for step in range(to_right):
        arrive_right(step)
        if step + 1 < to_right:
            rightward(step + 1).start()
        across(-step - 1).start()
        if step < to_left:
            arrive_left(step)
            if step + 1 < to_left:
                leftward(step + 1).start()
            across(step + 1).start()
    for distance in range(chips):
        index = seq_index(lax.rem(place + distance, chips)) + 1 - 2 * core
        remote_copy(
            slot(index), slot(index), send_peer.at[distance], recv_peer.at[distance], peer
        ).wait_recv()

    store = pltpu.make_async_copy(gathered.at[:, : 3 * columns], weights_ref, out_sem)
    store.start()
    norms = gathered[:, 3 * columns :].astype(F32).T
    norms_ref[...] = norms[0:8]

    def apply_norm(index, carry):
        at = pl.ds(pl.multiple_of(index * 128, 128), 128)
        normed_ref[at, :] = (scaled[at, :] * norms[0:1] + norms[2:3]).astype(BF)
        return carry

    lax.fori_loop(0, tokens_ref.shape[0] // 128, apply_norm, 0)

    def head_copy(step, which):
        where = lax.rem(me + step, devices)
        at = slice(which * HEAD_DIM, (which + 1) * HEAD_DIM)
        return remote_copy(
            sent.at[where, at, :], recv_ref.at[me, at, :], head_send.at[step, which],
            head_recv.at[me, which], where,
        )

    def core_copy(source_ref, source):
        return remote_copy(
            source_ref.at[source, HEAD_DIM:, :], others_ref.at[0, source], core_send.at[source],
            core_recv.at[source], peer,
        )

    home = pltpu.make_async_copy(sent.at[me], recv_ref.at[me], home_sem)
    for which in (1, 2, 0):
        weights = gathered[:, which * columns : (which + 1) * columns].T
        factor = HEAD_DIM**-0.5 * log2_e if which == 0 else 1.0

        def project(core_index, carry, which=which, weights=weights, factor=factor):
            at = pl.ds(pl.multiple_of(core_index * rows, rows), rows)
            result = (dot(weights, normed_ref[at, :], 1, 1) * factor).astype(BF)
            for head in range(heads):
                sent[head * group + core_index, which * HEAD_DIM : (which + 1) * HEAD_DIM, :] = (
                    result[head * HEAD_DIM : (head + 1) * HEAD_DIM, :]
                )
            return carry

        lax.fori_loop(0, group, project, 0)

        def send(step, carry, which=which):
            head_copy(step, which).start()
            return carry

        lax.fori_loop(1, devices, send, 0)
        if which == 2 and group == 2:
            core_copy(sent, me).start()
    home.start()

    def wait_head(step, carry, which):
        source = lax.rem(me - step + devices, devices)
        at = slice(which * HEAD_DIM, (which + 1) * HEAD_DIM)
        remote_copy(
            sent.at[source, at, :], recv_ref.at[source, at, :], head_send.at[0, which],
            head_recv.at[source, which], source,
        ).wait_recv()
        return carry

    def forward(step, carry):
        wait_head(step, carry, 1)
        wait_head(step, carry, 2)
        if group == 2:
            core_copy(recv_ref, lax.rem(me - step + devices, devices)).start()
        return carry

    lax.fori_loop(1, devices, forward, 0)
    lax.fori_loop(1, devices, functools.partial(wait_head, which=0), 0)
    home.wait()

    def finish_core(source, carry):
        core_copy(recv_ref, source).wait()
        return carry

    if group == 2:
        lax.fori_loop(0, devices, finish_core, 0)

    def wait_sent(step, carry):
        for which in range(3):
            head_copy(step, which).wait_send()
        return carry

    lax.fori_loop(1, devices, wait_sent, 0)
    for step in range(to_right):
        rightward(step).wait_send()
    for step in range(to_left):
        leftward(step).wait_send()
    for distance in range(chips):
        across(distance).wait_send()
    store.wait()


def project(tokens, w_query, w_key, w_value, norm_gain, norm_bias, devices, group):
    own_rows, width = tokens.shape
    columns = w_query.shape[2]
    chips = devices // 2
    rows = own_rows // group
    whole = pl.BlockSpec(memory_space=pltpu.VMEM)
    far = pl.BlockSpec(memory_space=pl.ANY)
    dma = pltpu.SemaphoreType.DMA
    return pl.pallas_call(
        functools.partial(
            project_kernel, devices=devices, group=group, columns=columns, width=width
        ),
        in_specs=[whole] * 6,
        out_specs=[far, far, whole, far, whole],
        out_shape=[
            jax.ShapeDtypeStruct((devices, 3 * HEAD_DIM, rows), BF),
            jax.ShapeDtypeStruct((1, devices, 2 * HEAD_DIM, rows), BF),
            jax.ShapeDtypeStruct((own_rows, width), BF),
            jax.ShapeDtypeStruct((width, 3 * columns), BF),
            jax.ShapeDtypeStruct((8, width), F32),
        ],
        scratch_shapes=[
            pltpu.VMEM((width, 3 * columns + 128), BF),
            pltpu.VMEM((own_rows, width), F32),
            pltpu.VMEM((devices, 3 * HEAD_DIM, rows), BF),
            dma((chips // 2,)), dma((chips // 2,)),
            dma((chips // 2,)), dma((chips // 2,)),
            dma((chips,)), dma((chips,)),
            dma((devices, 3)), dma((devices, 3)), dma,
            dma((devices,)), dma((devices,)),
            dma,
        ],
        compiler_params=pltpu.CompilerParams(
            vmem_limit_bytes=VMEM_BYTES, collective_id=1, has_side_effects=True
        ),
        name="project",
    )(tokens, w_query, w_key, w_value, norm_gain, norm_bias)


def finish_kernel(
    dquery_ref, dpieces_far, normed_far, weights_far, tokens_far, dmid_far, mid_far, z_far,
    z_other_far, norms_ref, second_ref,
    dstream_far, last_far, dquery_w_ref, dkey_w_ref, dvalue_w_ref, dgain_ref, dbias_ref,
    normed, weights, tokens, dmid, mid, z, z_other, own_piece,
    core_got, sent, got, flat, partial_sent, partial_got, summed_grads, partial, from_peer,
    first_right, first_left, ring_right, ring_left, total, few_sent, few_got,
    load_sem, store_sem, core_send, core_recv, head_send, head_recv, x_send, x_recv,
    peer_send, peer_recv, right_send, right_recv, left_send, left_recv, few_send, few_recv,
    *, devices, group, cores, columns, width,
):
    chips = devices // 2
    depth = width // devices
    own_rows = tokens.shape[0]
    rows = own_rows // group
    heads = columns // HEAD_DIM
    wide = 3 * columns + 128
    cut = first_right.shape[1]
    lanes = 128
    chunks = rows // lanes
    place, core, seq_index = ring_of(devices)
    me = seq_index(place)
    right = {"seq": seq_index(lax.rem(place + 1, chips))}
    left = {"seq": seq_index(lax.rem(place + chips - 1, chips))}
    peer = {"seq": me + 1 - 2 * core}
    across = {"tensor": 1 - lax.axis_index("tensor")}
    group_place = lax.rem(me, group)

    loads = {}
    for number, (name, far, near) in enumerate((
        ("piece", dpieces_far.at[0], own_piece), ("tokens", tokens_far, tokens), ("weights", weights_far, weights),
        ("normed", normed_far, normed), ("z", z_far, z), ("z_other", z_other_far, z_other),
        ("mid", mid_far, mid), ("dmid", dmid_far, dmid),
    )):
        loads[name] = pltpu.make_async_copy(far, near, load_sem.at[number])
        loads[name].start()

    barrier = pltpu.get_barrier_semaphore()
    for step in range(1, devices):
        pl.semaphore_signal(
            barrier, inc=1, device_id={"seq": lax.rem(me + step, devices)},
            device_id_type=pl.DeviceIdType.MESH,
        )
    pl.semaphore_signal(barrier, inc=1, device_id=across, device_id_type=pl.DeviceIdType.MESH)
    pl.semaphore_wait(barrier, devices)

    def copy_to(source, target, send_sem, recv_sem, where):
        return pltpu.make_async_remote_copy(
            src_ref=source, dst_ref=target, send_sem=send_sem, recv_sem=recv_sem,
            device_id=where, device_id_type=pl.DeviceIdType.MESH,
        )

    def core_copy(by, chunk):
        other = jnp.int32(0)
        bit = 1
        while bit < group:
            mine = lax.rem(group_place // bit, 2)
            other = other + bit * ((1 - mine) if by & bit else mine)
            bit *= 2
        at = slice(chunk * lanes, (chunk + 1) * lanes)
        return copy_to(
            dpieces_far.at[by, :, :, at], core_got.at[by - 1, :, :, at],
            core_send.at[by - 1, chunk], core_recv.at[by - 1, chunk],
            {"seq": me - group_place + other},
        )

    def head_copy(step, chunk):
        where = lax.rem(me + step, devices)
        at = slice(chunk * lanes, (chunk + 1) * lanes)
        return copy_to(
            sent.at[where, :, at], got.at[me, :, at],
            head_send.at[step, chunk], head_recv.at[me, chunk], {"seq": where},
        )

    for chunk in range(chunks):
        for by in range(1, cores):
            core_copy(by, chunk).start()
    loads["piece"].wait()
    for chunk in range(chunks):
        at = slice(chunk * lanes, (chunk + 1) * lanes)
        for by in range(1, cores):
            core_copy(by, chunk).wait_recv()

        def gather(index, carry, at=at):
            piece = own_piece[index, :, at].astype(F32)
            for by in range(1, cores):
                piece = piece + core_got[by - 1, index, :, at].astype(F32)
            sent[index, HEAD_DIM:, at] = piece.astype(BF)
            sent[index, 0:HEAD_DIM, at] = dquery_ref[index, :, at]
            return carry

        lax.fori_loop(0, devices, gather, 0)

        def send(step, carry, chunk=chunk):
            head_copy(step, chunk).start()
            return carry

        lax.fori_loop(1, devices, send, 0)

    loads["z"].wait()
    loads["z_other"].wait()
    loads["mid"].wait()

    def add_last(index, carry):
        at = pl.ds(pl.multiple_of(index * lanes, lanes), lanes)
        both = z[at, :].astype(F32) + z_other[at, :].astype(F32)
        z[at, :] = (mid[at, :] + both).astype(BF)
        return carry

    lax.fori_loop(0, own_rows // lanes, add_last, 0)
    store_last = pltpu.make_async_copy(z, last_far, store_sem.at[0])
    store_last.start()
    for name in ("tokens", "weights", "normed", "dmid"):
        loads[name].wait()

    def part_rows(place_in_group, chunk):
        return slice(place_in_group * rows + chunk * lanes, place_in_group * rows + (chunk + 1) * lanes)

    def x_copy(place_in_group, chunk):
        at = part_rows(place_in_group, chunk)
        number = place_in_group * chunks + chunk
        return copy_to(
            partial_sent.at[at, :], partial_got.at[at, :], x_send.at[number], x_recv.at[number],
            across,
        )

    def unit_rows(at):
        stream = tokens[at, :].astype(F32)
        centred = stream - jnp.mean(stream, axis=-1, keepdims=True)
        spread = jnp.mean(centred * centred, axis=-1, keepdims=True)
        inverse = lax.rsqrt(spread + norm_eps)
        return centred * inverse, inverse

    def finish_norm(chunk):
        for place_in_group in range(group):
            at = part_rows(place_in_group, chunk)
            x_copy(place_in_group, chunk).wait_recv()
            dnormed = partial_sent[at, :].astype(F32) + partial_got[at, :].astype(F32)
            unit, inverse = unit_rows(at)
            dunit = dnormed * norms_ref[0:1, :]
            mean = jnp.mean(dunit, axis=-1, keepdims=True)
            along = jnp.mean(dunit * unit, axis=-1, keepdims=True)
            dmid[at, :] = dmid[at, :] + (dunit - mean - unit * along) * inverse

    gain_sum = jnp.zeros((1, width), F32)
    bias_sum = jnp.zeros((1, width), F32)
    lines = 256
    for chunk in range(chunks):
        at = slice(chunk * lanes, (chunk + 1) * lanes)

        def flatten(index, carry, chunk=chunk, at=at):
            head = index // group
            start = lax.rem(index, group) * rows + chunk * lanes
            to_rows = pl.ds(pl.multiple_of(start, lanes), lanes)

            def put(source):
                for which in range(3):
                    to = pl.ds(
                        pl.multiple_of(which * columns + head * HEAD_DIM, HEAD_DIM), HEAD_DIM
                    )
                    flat[to, to_rows] = source[index, which * HEAD_DIM : (which + 1) * HEAD_DIM, at]

            @pl.when(index == me)
            def _():
                put(sent)

            @pl.when(index != me)
            def _():
                copy_to(
                    sent.at[index, :, at], got.at[index, :, at],
                    head_send.at[0, chunk], head_recv.at[index, chunk], {"seq": index},
                ).wait_recv()
                put(got)

            return carry

        lax.fori_loop(0, devices, flatten, 0)
        ats = [part_rows(place_in_group, chunk) for place_in_group in range(group)]
        flat_chunk = jnp.concatenate([flat[:, part] for part in ats], axis=1)

        def sum_grads():
            normed_t = jnp.concatenate([normed[part, :] for part in ats], axis=0).T
            for line in range(width // lines):
                here = slice(line * lines, (line + 1) * lines)
                result = dot(normed_t[here, :], flat_chunk, 1, 1)
                if chunk > 0:
                    result = result + summed_grads[here, :]
                if chunk + 1 < chunks:
                    summed_grads[here, :] = result
                else:
                    partial[here, 0 : 3 * columns] = result.astype(BF)

        def send_dnormed(gain_sum, bias_sum):
            result = dot(flat_chunk.T, weights[...], 1, 1)
            for place_in_group in range(group):
                here = slice(place_in_group * lanes, (place_in_group + 1) * lanes)
                partial_sent[ats[place_in_group], :] = result[here, :].astype(BF)
                x_copy(place_in_group, chunk).start()
            for place_in_group in range(group):
                here = slice(place_in_group * lanes, (place_in_group + 1) * lanes)
                unit, _ = unit_rows(ats[place_in_group])
                gain_sum = gain_sum + jnp.sum(result[here, :] * unit, axis=0, keepdims=True)
                bias_sum = bias_sum + jnp.sum(result[here, :], axis=0, keepdims=True)
            return gain_sum, bias_sum

        gain_sum, bias_sum = send_dnormed(gain_sum, bias_sum)
        sum_grads()
        if chunk > 0 and chunk + 1 < chunks:
            finish_norm(chunk - 1)

    norm_rows = jnp.concatenate(
        [
            gain_sum, second_ref[0:1, :] * 0.5, bias_sum, second_ref[1:2, :] * 0.5,
            jnp.zeros((124, width), F32),
        ],
        axis=0,
    )
    partial[:, 3 * columns :] = norm_rows.T.astype(BF)

    order = []
    for step in range(chips // 2):
        for offset in (-step - 1, step + 1):
            if offset % chips not in order:
                order.append(offset % chips)
    order.append(0)

    def peer_copy(number):
        where = lax.rem(place + order[number], chips)
        theirs = seq_index(where) + 1 - 2 * core
        return copy_to(
            partial.at[pl.ds(pl.multiple_of(theirs * depth, depth), depth), :],
            from_peer.at[pl.ds(pl.multiple_of(where * depth, depth), depth), :],
            peer_send.at[number], peer_recv.at[number], peer,
        )

    for number in range(chips):
        peer_copy(number).start()

    waited = []

    def chip_block(offset, low, high):
        number = order.index(offset % chips)
        if number not in waited:
            peer_copy(number).wait_recv()
            waited.append(number)
        where = lax.rem(place + offset % chips, chips)
        own = pl.ds(pl.multiple_of(seq_index(where) * depth, depth), depth)
        there = pl.ds(pl.multiple_of(where * depth, depth), depth)
        return partial[own, low:high].astype(F32) + from_peer[there, low:high].astype(F32)

    steps = chips - 1

    def ring_copy(step, toward_right):
        if toward_right:
            source = first_right if step == 0 else ring_right.at[step - 1]
            return copy_to(
                source, ring_right.at[step], right_send.at[step], right_recv.at[step], right
            )
        source = first_left if step == 0 else ring_left.at[step - 1]
        return copy_to(source, ring_left.at[step], left_send.at[step], left_recv.at[step], left)

    first_right[...] = chip_block(-1, 0, cut).astype(BF)
    ring_copy(0, True).start()
    first_left[...] = chip_block(1, cut, wide).astype(BF)
    ring_copy(0, False).start()
    pending = list(range(max(chunks - 2, 0), chunks))
    for step in range(steps):
        if pending and step in (1, steps // 2):
            finish_norm(pending.pop(0))
        for toward_right, ring, low, high in (
            (True, ring_right, 0, cut), (False, ring_left, cut, wide),
        ):
            ring_copy(step, toward_right).wait_recv()
            offset = -step - 2 if toward_right else step + 2
            summed = ring[step].astype(F32) + chip_block(offset, low, high)
            if step + 1 < steps:
                ring[step] = summed.astype(BF)
                ring_copy(step + 1, toward_right).start()
            else:
                total[:, low:high] = summed
    few_sent[...] = total[:, 3 * columns :]
    few = copy_to(few_sent, few_got, few_send, few_recv, across)
    few.start()
    for chunk in pending:
        finish_norm(chunk)
    store_stream = pltpu.make_async_copy(dmid, dstream_far, store_sem.at[1])
    store_stream.start()
    dquery_w_ref[0] = total[:, 0:columns]
    dkey_w_ref[0] = total[:, columns : 2 * columns]
    dvalue_w_ref[0] = total[:, 2 * columns : 3 * columns]
    few.wait()
    norm_rows = (few_sent[...] + few_got[...]).T
    dgain_ref[0] = norm_rows[0:2, :]
    dbias_ref[0] = norm_rows[2:4, :]
    for chunk in range(chunks):
        for by in range(1, cores):
            core_copy(by, chunk).wait_send()
        for place_in_group in range(group):
            x_copy(place_in_group, chunk).wait_send()

        def wait_head(step, carry, chunk=chunk):
            head_copy(step, chunk).wait_send()
            return carry

        lax.fori_loop(1, devices, wait_head, 0)
    for number in range(chips):
        peer_copy(number).wait_send()
    for step in range(steps):
        ring_copy(step, True).wait_send()
        ring_copy(step, False).wait_send()
    store_last.wait()
    store_stream.wait()


def finish(
    dquery, dpieces, normed, weights, tokens, dmid, mid, z, z_other, norms, second, devices, group
):
    own_rows, width = tokens.shape
    cores, _, _, rows = dpieces.shape
    columns = weights.shape[1] // 3
    chips = devices // 2
    depth = width // devices
    wide = 3 * columns + 128
    cut = (wide // 128 + 1) // 2 * 128
    steps = chips - 1
    chunks = rows // 128
    whole = pl.BlockSpec(memory_space=pltpu.VMEM)
    far = pl.BlockSpec(memory_space=pl.ANY)
    dma = pltpu.SemaphoreType.DMA
    vmem = pltpu.VMEM
    return pl.pallas_call(
        functools.partial(
            finish_kernel, devices=devices, group=group, cores=cores, columns=columns, width=width
        ),
        in_specs=[whole] + [far] * 8 + [whole] * 2,
        out_specs=[far] * 2 + [whole] * 5,
        out_shape=[
            jax.ShapeDtypeStruct((own_rows, width), F32),
            jax.ShapeDtypeStruct((own_rows, width), BF),
        ]
        + [jax.ShapeDtypeStruct((1, depth, columns), F32)] * 3
        + [jax.ShapeDtypeStruct((1, 2, depth), F32)] * 2,
        scratch_shapes=[
            vmem((own_rows, width), BF), vmem((width, 3 * columns), BF),
            vmem((own_rows, width), BF), vmem((own_rows, width), F32),
            vmem((own_rows, width), F32), vmem((own_rows, width), BF),
            vmem((own_rows, width), BF), vmem((devices, 128, rows), BF),
            vmem((max(cores - 1, 1), devices, 128, rows), BF),
            vmem((devices, 3 * HEAD_DIM, rows), BF), vmem((devices, 3 * HEAD_DIM, rows), BF),
            vmem((3 * columns, own_rows), BF),
            vmem((own_rows, width), BF), vmem((own_rows, width), BF),
            vmem((width, 3 * columns), F32), vmem((width, wide), BF),
            vmem((chips * depth, wide), BF),
            vmem((depth, cut), BF), vmem((depth, wide - cut), BF),
            vmem((steps, depth, cut), BF), vmem((steps, depth, wide - cut), BF),
            vmem((depth, wide), F32),
            vmem((depth, 128), F32), vmem((depth, 128), F32),
            dma((8,)), dma((2,)),
            dma((max(cores - 1, 1), chunks)), dma((max(cores - 1, 1), chunks)),
            dma((devices, chunks)), dma((devices, chunks)),
            dma((group * chunks,)), dma((group * chunks,)),
            dma((chips,)), dma((chips,)),
            dma((steps,)), dma((steps,)), dma((steps,)), dma((steps,)),
            dma, dma,
        ],
        compiler_params=pltpu.CompilerParams(
            vmem_limit_bytes=60 * 2**20, collective_id=2, has_side_effects=True
        ),
        name="finish",
    )(dquery, dpieces, normed, weights, tokens, dmid, mid, z, z_other, norms, second)


def middle_kernel(
    mixed_ref, tokens_ref, dz_ref, second_ref, norms_ref,
    dout_ref, dmid_ref, mid_ref, z_ref, grads_ref, norm_grads_ref,
    weights, tokens, dz, flat, flat_other, normed, act, dup, mid, dmid, dsent, dgot, dy, z,
    out_t, dout, stage,
    load_sem, flat_send, flat_recv, x_send, x_recv, head_send, head_recv, store_sem, stage_sem,
    *, devices, group, columns, hidden,
):
    own_rows, width = tokens.shape
    rows = own_rows // group
    heads = columns // HEAD_DIM
    parts = x_send.shape[0]
    part_rows = own_rows // parts
    block = 512
    me = lax.axis_index("seq").astype(jnp.int32)
    core = lax.rem(me, group)
    half = lax.axis_index("tensor").astype(jnp.int32)
    across = {"tensor": 1 - half}

    loads = [
        pltpu.make_async_copy(second_ref.at[:, 0:width], weights.at[:, 0:width], load_sem.at[0]),
        pltpu.make_async_copy(tokens_ref, tokens, load_sem.at[1]),
        pltpu.make_async_copy(second_ref.at[:, width:], weights.at[:, width:], load_sem.at[2]),
        pltpu.make_async_copy(dz_ref, dz, load_sem.at[3]),
    ]
    for load in loads:
        load.start()

    barrier = pltpu.get_barrier_semaphore()
    for other in range(devices):
        @pl.when(me != other)
        def _(other=other):
            pl.semaphore_signal(
                barrier, inc=1, device_id={"seq": other}, device_id_type=pl.DeviceIdType.MESH
            )

    pl.semaphore_signal(
        barrier, inc=1, device_id=across, device_id_type=pl.DeviceIdType.MESH
    )
    pl.semaphore_wait(barrier, devices)

    def copy_to(source, target, send_sem, recv_sem, where):
        return pltpu.make_async_remote_copy(
            src_ref=source, dst_ref=target, send_sem=send_sem, recv_sem=recv_sem,
            device_id=where, device_id_type=pl.DeviceIdType.MESH,
        )

    def rows_of(part):
        return pl.ds(pl.multiple_of(part * part_rows, part_rows), part_rows)

    def flatten(index, carry):
        head = index // group
        at = pl.ds(pl.multiple_of(lax.rem(index, group) * rows, rows), rows)
        flat[pl.ds(pl.multiple_of(head * HEAD_DIM, HEAD_DIM), HEAD_DIM), at] = mixed_ref[index]
        return carry

    lax.fori_loop(0, devices, flatten, 0)

    def flat_copy(part):
        at = rows_of(part)
        return copy_to(
            flat.at[:, at], flat_other.at[:, at], flat_send.at[part], flat_recv.at[part], across
        )

    def x_copy(part):
        at = rows_of(part)
        return copy_to(dsent.at[at, :], dgot.at[at, :], x_send.at[part], x_recv.at[part], across)

    for part in range(parts):
        flat_copy(part).start()
    loads[0].wait()
    out_t[...] = weights[:, pl.ds(pl.multiple_of(half * columns, columns), columns)].T
    for load in loads[1:]:
        load.wait()
    first_half = half == 0

    def unit_rows(at):
        stream = mid[at, :]
        centred = stream - jnp.mean(stream, axis=-1, keepdims=True)
        spread = jnp.mean(centred * centred, axis=-1, keepdims=True)
        inverse = lax.rsqrt(spread + norm_eps)
        return centred * inverse, inverse

    def store_mid(part):
        at = rows_of(part)
        return pltpu.make_async_copy(mid.at[at, :], mid_ref.at[at, :], store_sem.at[0, part])

    def forward(part, carry):
        at = rows_of(part)
        flat_copy(part).wait_recv()
        own, other = flat[:, at], flat_other[:, at]
        low = jnp.where(first_half, own, other).T
        high = jnp.where(first_half, other, own).T
        projected = dot(low, weights[:, 0:columns], 1, 1) + dot(
            high, weights[:, columns:width], 1, 1
        )
        mid[at, :] = tokens[at, :].astype(F32) + projected
        store_mid(part).start()
        unit, _ = unit_rows(at)
        normed[at, :] = (unit * norms_ref[1:2, :] + norms_ref[3:4, :]).astype(BF)

        def hidden_block(index, total):
            cut = pl.ds(pl.multiple_of(index * block, block), block)
            up_cut = pl.ds(pl.multiple_of(width + index * block, block), block)
            down_cut = pl.ds(pl.multiple_of(width + hidden + index * block, block), block)
            up_w = weights[:, up_cut]
            up = dot(normed[at, :], up_w, 1, 0)
            dact = dot(dz[at, :], weights[:, down_cut], 1, 0)
            square = up * up
            bend = jnp.tanh(0.7978845608028654 * up * (1.0 + 0.044715 * square))
            grow = 0.5 + 0.5 * bend
            slope = grow + 0.5 * up * (1.0 - bend * bend) * (
                0.7978845608028654 + 0.10703222440890037 * square
            )
            act[at, cut] = (up * grow).astype(BF)
            dup_block = (dact * slope).astype(BF)
            dup[at, cut] = dup_block
            return total + dot(dup_block, up_w, 1, 1)

        total = lax.fori_loop(
            0, hidden // block, hidden_block, jnp.zeros((part_rows, width), F32)
        )
        dsent[at, :] = total.astype(BF)
        x_copy(part).start()
        return carry

    lax.fori_loop(0, parts, forward, 0)

    piece_rows = min(part_rows, rows)
    pieces = rows // piece_rows

    def head_copies(piece, head):
        start = piece * piece_rows
        owner = head * group + start // rows
        slot = lax.rem(piece, pieces)
        source = dout.at[
            pl.ds(pl.multiple_of(head * HEAD_DIM, HEAD_DIM), HEAD_DIM),
            pl.ds(pl.multiple_of(start, piece_rows), piece_rows),
        ]
        target = dout_ref.at[me, :, pl.ds(pl.multiple_of(slot * piece_rows, piece_rows), piece_rows)]
        away = copy_to(
            source, target, head_send.at[head, piece], head_recv.at[me, slot], {"seq": owner}
        )
        home = pltpu.make_async_copy(source, target, head_send.at[head, piece])
        return away, home, owner == me

    def send_heads(part):
        def send(index, carry):
            piece = part * (part_rows // piece_rows) + index // heads
            away, home, is_home = head_copies(piece, lax.rem(index, heads))

            @pl.when(is_home)
            def _():
                home.start()

            @pl.when(jnp.logical_not(is_home))
            def _():
                away.start()

            return carry

        lax.fori_loop(0, heads * (part_rows // piece_rows), send, 0)

    def store_dmid(part):
        at = rows_of(part)
        return pltpu.make_async_copy(dmid.at[at, :], dmid_ref.at[at, :], store_sem.at[1, part])

    def backward(part, sums):
        gain_sum, bias_sum = sums
        at = rows_of(part)
        x_copy(part).wait_recv()
        dnormed = dsent[at, :].astype(F32) + dgot[at, :].astype(F32)
        unit, inverse = unit_rows(at)
        dunit = dnormed * norms_ref[1:2, :]
        mean = jnp.mean(dunit, axis=-1, keepdims=True)
        along = jnp.mean(dunit * unit, axis=-1, keepdims=True)
        result = dz[at, :].astype(F32) + (dunit - mean - unit * along) * inverse
        dmid[at, :] = result
        store_dmid(part).start()
        low = result.astype(BF)
        dy[at, :] = low
        dout[:, at] = dot(out_t[...], low, 1, 1).astype(BF)
        send_heads(part)
        gain_sum = gain_sum + jnp.sum(dnormed * unit, axis=0, keepdims=True)
        bias_sum = bias_sum + jnp.sum(dnormed, axis=0, keepdims=True)
        return gain_sum, bias_sum

    def last_product(part, carry):
        at = rows_of(part)
        z[at, :] = dot(act[at, :], weights[:, width + hidden :], 1, 1).astype(BF)
        return carry

    lax.fori_loop(0, parts, last_product, 0)
    store_z = pltpu.make_async_copy(z, z_ref, load_sem.at[0])
    store_z.start()

    def grads_into(left_t, right_ref, first_column):
        blocks = right_ref.shape[1] // block

        def store(index, slot):
            cut = pl.ds(pl.multiple_of(first_column + index * block, block), block)
            return pltpu.make_async_copy(stage.at[slot], grads_ref.at[:, cut], stage_sem.at[slot])

        def one(index, carry):
            slot = lax.rem(index, 2)

            @pl.when(index >= 2)
            def _():
                store(index - 2, slot).wait()

            cut = pl.ds(pl.multiple_of(index * block, block), block)
            stage[slot] = dot(left_t, right_ref[:, cut], 1, 0).astype(BF)
            store(index, slot).start()
            return carry

        lax.fori_loop(0, blocks, one, 0)
        for index in range(blocks - 2, blocks):
            store(index, index % 2).wait()

    sums = (jnp.zeros((1, width), F32), jnp.zeros((1, width), F32))
    sums = backward(0, sums)
    grads_into(normed[...].T, dup, columns)
    sums = backward(1, sums)
    grads_into(dz[...].T, act, columns + hidden)
    for part in range(2, parts):
        sums = backward(part, sums)
    stage[0] = dot(dy[...].T, flat[...], 1, 1).astype(BF)
    store_out = pltpu.make_async_copy(stage.at[0], grads_ref.at[:, 0:columns], stage_sem.at[0])
    store_out.start()
    norm_grads_ref[...] = jnp.concatenate([*sums, jnp.zeros((6, width), F32)], axis=0)

    def wait_sent(index, carry):
        away, home, is_home = head_copies(index // heads, lax.rem(index, heads))

        @pl.when(is_home)
        def _():
            home.wait()

        @pl.when(jnp.logical_not(is_home))
        def _():
            away.wait_send()

        return carry

    lax.fori_loop(0, heads * (own_rows // piece_rows), wait_sent, 0)

    def wait_heads(index, carry):
        source = index // pieces
        slot = lax.rem(index, pieces)
        cut = pl.ds(pl.multiple_of(slot * piece_rows, piece_rows), piece_rows)

        @pl.when(source != me)
        def _():
            copy_to(
                dout.at[0:HEAD_DIM, 0:piece_rows], dout_ref.at[source, :, cut],
                head_send.at[0, 0], head_recv.at[source, slot], {"seq": source},
            ).wait_recv()

        return carry

    lax.fori_loop(0, devices * pieces, wait_heads, 0)
    for part in range(parts):
        flat_copy(part).wait_send()
        x_copy(part).wait_send()
        store_mid(part).wait()
        store_dmid(part).wait()
    store_z.wait()
    store_out.wait()


def middle(mixed, tokens, dz, second, norms, devices, group, columns):
    own_rows, width = tokens.shape
    rows = own_rows // group
    hidden = (second.shape[1] - width) // 2
    parts = 4
    piece_rows = min(own_rows // parts, rows)
    whole = pl.BlockSpec(memory_space=pltpu.VMEM)
    far = pl.BlockSpec(memory_space=pl.ANY)
    dma = pltpu.SemaphoreType.DMA
    vmem = pltpu.VMEM
    return pl.pallas_call(
        functools.partial(
            middle_kernel, devices=devices, group=group, columns=columns, hidden=hidden
        ),
        in_specs=[whole, far, far, far, whole],
        out_specs=[far] * 5 + [whole],
        out_shape=[
            jax.ShapeDtypeStruct((devices, HEAD_DIM, rows), BF),
            jax.ShapeDtypeStruct((own_rows, width), F32),
            jax.ShapeDtypeStruct((own_rows, width), F32),
            jax.ShapeDtypeStruct((own_rows, width), BF),
            jax.ShapeDtypeStruct((width, columns + 2 * hidden), BF),
            jax.ShapeDtypeStruct((8, width), F32),
        ],
        scratch_shapes=[
            vmem((width, width + 2 * hidden), BF),
            vmem((own_rows, width), BF), vmem((own_rows, width), BF),
            vmem((columns, own_rows), BF), vmem((columns, own_rows), BF),
            vmem((own_rows, width), BF),
            vmem((own_rows, hidden), BF), vmem((own_rows, hidden), BF),
            vmem((own_rows, width), F32), vmem((own_rows, width), F32),
            vmem((own_rows, width), BF), vmem((own_rows, width), BF),
            vmem((own_rows, width), BF), vmem((own_rows, width), BF),
            vmem((columns, width), BF), vmem((columns, own_rows), BF),
            vmem((2, width, 512), BF),
            dma((4,)), dma((parts,)), dma((parts,)), dma((parts,)), dma((parts,)),
            dma((columns // HEAD_DIM, own_rows // piece_rows)),
            dma((devices, rows // piece_rows)),
            dma((2, parts)), dma((2,)),
        ],
        compiler_params=pltpu.CompilerParams(
            vmem_limit_bytes=60 * 2**20, collective_id=3, has_side_effects=True
        ),
        name="middle",
    )(mixed, tokens, dz, second, norms)


def scene_span(ends_ref, scenes, first, last):
    low = jnp.int32(0)
    high = ends_ref[scenes - 1]
    for scene in range(scenes):
        low = jnp.where(first >= ends_ref[scene], ends_ref[scene], low)
    for scene in reversed(range(scenes)):
        high = jnp.where(last < ends_ref[scene], ends_ref[scene], high)
    return low, high


def scene_inside(ends_ref, scenes, row, position):
    start = jnp.zeros_like(row)
    end = jnp.zeros_like(row)
    before = jnp.int32(0)
    for scene in range(scenes):
        start = jnp.where(row == STAT_ROWS + scene, before, start)
        end = jnp.where(row == STAT_ROWS + scene, ends_ref[scene], end)
        before = ends_ref[scene]
    return (position >= start) & (position < end)


def key_extra(ends_ref, scenes, first, rows):
    row = lax.broadcasted_iota(jnp.int32, (64, rows), 0)
    position = first + lax.broadcasted_iota(jnp.int32, (64, rows), 1)
    inside = scene_inside(ends_ref, scenes, row, position)
    return jnp.where(row < STAT_ROWS, -1.0, jnp.where(inside, 1.0, 0.0)).astype(BF)


def query_extra(ends_ref, scenes, first, rows, stat):
    row = lax.broadcasted_iota(jnp.int32, (64, rows), 0)
    position = first + lax.broadcasted_iota(jnp.int32, (64, rows), 1)
    inside = scene_inside(ends_ref, scenes, row, position)
    is_scene = (row >= STAT_ROWS) & (row < STAT_ROWS + scenes)
    extra = jnp.where(is_scene & jnp.logical_not(inside), neg_large, 0.0)
    if stat is not None:
        extra = stat_rows(row, stat, extra)
    return extra.astype(BF)


def stat_rows(row, stat, extra):
    top = stat.astype(BF).astype(F32)
    middle = (stat - top).astype(BF).astype(F32)
    bottom = stat - top - middle
    extra = jnp.where(row == 0, top, extra)
    extra = jnp.where(row == 1, middle, extra)
    return jnp.where(row == 2, bottom, extra)


def walk_tiles(process, state, first, count, unit, sizes):
    at = first
    left = count
    for size in sizes:
        steps = left // size
        begin = at

        def step(index, carry, begin=begin, size=size):
            offset = pl.multiple_of((begin + index * size) * unit, unit)
            return process(offset, size * unit, carry)

        state = lax.fori_loop(0, steps, step, state)
        at = at + steps * size
        left = left - steps * size
    return state


def forward_kernel(
    ends_ref, me_ref, recv_ref, other_ref, out_ref, lse_ref, keys, values, key_top,
    *, scenes, group, total,
):
    block = pl.program_id(0)
    core = me_ref[0]
    sources = recv_ref.shape[0]
    rows = recv_ref.shape[2]

    @pl.when(block == 0)
    def _():
        values[64:80, :] = jnp.ones((16, total), BF)
        key_top[0] = 0.0
        for piece in range(group):
            place = core ^ piece

            def load(source, carry, piece=piece, place=place):
                first = pl.multiple_of((source * group + place) * rows, rows)
                if piece == 0:
                    key = recv_ref[source, 64:128, :]
                    value = recv_ref[source, 128:192, :]
                else:
                    key = other_ref[piece - 1, source, 0:64, :]
                    value = other_ref[piece - 1, source, 64:128, :]
                extra = key_extra(ends_ref, scenes, first, rows)
                keys[pl.ds(first, rows), :] = jnp.concatenate([key, extra], axis=0).T
                values[0:64, pl.ds(first, rows)] = value
                wide = key.astype(F32)
                key_top[0] = jnp.maximum(key_top[0], jnp.max(jnp.sum(wide * wide, axis=0)))
                return carry

            lax.fori_loop(0, sources, load, 0)

    first = (block * group + core) * rows
    low, high = scene_span(ends_ref, scenes, first, first + rows - 1)
    query = recv_ref[block, 0:64, :]
    wide = query.astype(F32)
    query_top = jnp.max(jnp.sum(wide * wide, axis=0))
    query = jnp.concatenate([query, query_extra(ends_ref, scenes, first, rows, None)], axis=0)
    unit = 256
    begin = low // unit
    count = (high + unit - 1) // unit - begin
    safe = query_top * key_top[0] <= SAFE_BOUND * SAFE_BOUND

    def scores_of(offset, size):
        return dot(keys[pl.ds(offset, size), :], query, 1, 0)

    def mix(offset, size, weights):
        return dot(values[:, pl.ds(offset, size)], weights.astype(BF), 1, 0)

    def write(total_mix, top):
        summed = total_mix[64:65, :]
        out_ref[0] = (total_mix[0:64, :] / summed).astype(BF)
        lse_ref[0] = top + jnp.log(summed) * log2_e

    @pl.when(safe)
    def _():
        def process(offset, size, carry):
            return carry + mix(offset, size, jnp.exp2(scores_of(offset, size)))

        write(
            walk_tiles(process, jnp.zeros((80, rows), F32), begin, count, unit, (8, 4, 2, 1)),
            0.0,
        )

    @pl.when(jnp.logical_not(safe))
    def _():
        def process(offset, size, carry):
            top, mixed = carry
            scores = scores_of(offset, size)
            new_top = jnp.maximum(top, jnp.max(scores, axis=0, keepdims=True))
            weights = jnp.exp2(scores - new_top)
            return new_top, mixed * jnp.exp2(top - new_top) + mix(offset, size, weights)

        start = (jnp.full((1, rows), neg_large, F32), jnp.zeros((80, rows), F32))
        top, mixed = walk_tiles(process, start, begin, count, unit, (1,))
        write(mixed, top)


def attention_forward(ends, me, recv, other, group):
    sources, _, rows = recv.shape
    total = sources * group * rows
    whole = pl.BlockSpec(memory_space=pltpu.VMEM)
    return pl.pallas_call(
        functools.partial(
            forward_kernel, scenes=ends.shape[0], group=group, total=total
        ),
        grid_spec=pltpu.PrefetchScalarGridSpec(
            num_scalar_prefetch=2,
            grid=(sources,),
            in_specs=[whole, whole],
            out_specs=[
                pl.BlockSpec((1, 64, rows), lambda b, *_: (b, 0, 0)),
                pl.BlockSpec((1, 1, rows), lambda b, *_: (b, 0, 0)),
            ],
            scratch_shapes=[
                pltpu.VMEM((total, 128), BF),
                pltpu.VMEM((80, total), BF),
                pltpu.SMEM((1,), F32),
            ],
        ),
        out_shape=[
            jax.ShapeDtypeStruct((sources, 64, rows), BF),
            jax.ShapeDtypeStruct((sources, 1, rows), F32),
        ],
        compiler_params=pltpu.CompilerParams(vmem_limit_bytes=VMEM_BYTES),
        cost_estimate=pl.CostEstimate(
            flops=60 * 10**9, bytes_accessed=8 * 10**6, transcendentals=45 * 10**6
        ),
        name="attention_forward",
    )(ends, me, recv, other)


def backward_kernel(ends_ref, me_ref, recv_ref, others_ref, *refs, scenes, group, parts):
    dout_refs = refs[:parts]
    out_ref, lse_ref, dquery_ref, dkeys_ref = refs[parts : parts + 4]
    queries, douts, queries_flat, douts_flat, dqueries = refs[parts + 4 :]
    block = pl.program_id(0)
    core = me_ref[0]
    sources = recv_ref.shape[0]
    rows = recv_ref.shape[2]
    span = group * rows

    @pl.when(block == 0)
    def _():
        dqueries[...] = jnp.zeros_like(dqueries)

        def load(source, carry):
            first = source * span + core * rows
            at = pl.ds(pl.multiple_of(source * rows, rows), rows)
            query = recv_ref[source, 0:64, :]
            dout = jnp.concatenate([ref[source] for ref in dout_refs], axis=1)
            delta = jnp.sum(
                dout.astype(F32) * out_ref[source].astype(F32), axis=0, keepdims=True
            )
            row = lax.broadcasted_iota(jnp.int32, (64, rows), 0)
            extra = query_extra(ends_ref, scenes, first, rows, lse_ref[source])
            queries[at, :] = jnp.concatenate([query, extra], axis=0).T
            extra = stat_rows(row, delta, jnp.zeros((64, rows), F32)).astype(BF)
            douts[at, :] = jnp.concatenate([dout, extra], axis=0).T
            queries_flat[:, at] = query
            douts_flat[:, at] = dout
            return carry

        lax.fori_loop(0, sources, load, 0)

    source = block // group
    place = block % group
    first = block * rows
    low, high = scene_span(ends_ref, scenes, first, first + rows - 1)
    extra = key_extra(ends_ref, scenes, first, rows)
    own = place == core
    key = jnp.where(own, recv_ref[source, 64:128, :], others_ref[0, 0, 0:64, :])
    value = jnp.where(own, recv_ref[source, 128:192, :], others_ref[0, 0, 64:128, :])
    key_wide = jnp.concatenate([key, extra], axis=0)
    value_wide = jnp.concatenate([value, extra], axis=0)
    key_rows = key_wide.T
    unit = min(256, rows)

    def local(position):
        inside = jnp.clip(lax.rem(position, span) - core * rows, 0, rows)
        return position // span * rows + inside

    begin = local(low) // unit
    count = (local(high) + unit - 1) // unit - begin

    def process(offset, size, carry):
        dkey, dvalue = carry
        at = pl.ds(offset, size)
        probs = jnp.exp2(dot(queries[at, :], key_wide, 1, 0))
        dprobs = dot(douts[at, :], value_wide, 1, 0)
        dscores = (probs * dprobs).astype(BF)
        dvalue = dvalue + dot(douts_flat[:, at], probs.astype(BF), 1, 0)
        dkey = dkey + dot(queries_flat[:, at], dscores, 1, 0)
        dqueries[at, :] += dot(dscores, key_rows, 1, 0)
        return dkey, dvalue

    zeros = jnp.zeros((64, rows), F32)
    dkey, dvalue = walk_tiles(process, (zeros, zeros), begin, count, unit, (8, 4, 2, 1))
    dkeys_ref[0, 0, 0:64, :] = (dkey * ln_2).astype(BF)
    dkeys_ref[0, 0, 64:128, :] = dvalue.astype(BF)

    @pl.when(block == sources * group - 1)
    def _():
        def store(source, carry):
            at = pl.ds(pl.multiple_of(source * rows, rows), rows)
            dquery_ref[source] = (dqueries[at, :].T[0:64, :] * HEAD_DIM**-0.5).astype(BF)
            return carry

        lax.fori_loop(0, sources, store, 0)


def attention_backward(ends, me, recv, others, dout, out, lse, group):
    sources, _, rows = recv.shape
    mine = sources * rows
    whole = pl.BlockSpec(memory_space=pltpu.VMEM)

    def other_map(block, ends_ref, me_ref):
        return (jnp.maximum((block % group) ^ me_ref[0], 1) - 1, block // group, 0, 0)

    def piece_map(block, ends_ref, me_ref):
        return ((block % group) ^ me_ref[0], block // group, 0, 0)

    return pl.pallas_call(
        functools.partial(
            backward_kernel, scenes=ends.shape[0], group=group, parts=len(dout)
        ),
        grid_spec=pltpu.PrefetchScalarGridSpec(
            num_scalar_prefetch=2,
            grid=(sources * group,),
            in_specs=[whole, pl.BlockSpec((1, 1, 128, rows), other_map)] + [whole] * (len(dout) + 2),
            out_specs=[whole, pl.BlockSpec((1, 1, 128, rows), piece_map)],
            scratch_shapes=[
                pltpu.VMEM((mine, 128), BF),
                pltpu.VMEM((mine, 128), BF),
                pltpu.VMEM((64, mine), BF),
                pltpu.VMEM((64, mine), BF),
                pltpu.VMEM((mine, 128), F32),
            ],
        ),
        out_shape=[
            jax.ShapeDtypeStruct((sources, 64, rows), BF),
            jax.ShapeDtypeStruct((group, sources, 128, rows), BF),
        ],
        compiler_params=pltpu.CompilerParams(vmem_limit_bytes=VMEM_BYTES),
        cost_estimate=pl.CostEstimate(
            flops=150 * 10**9, bytes_accessed=20 * 10**6, transcendentals=45 * 10**6
        ),
        name="attention_backward",
    )(ends, me, recv, others, *dout, out, lse)


def swap_tensor(part):
    return lax.ppermute(part, "tensor", [(0, 1), (1, 0)])


def per_device(
    tokens, scene_lengths, w_query, w_key, w_value, w_out, w_up, w_down,
    norm_gain, norm_bias, cotangent,
):
    own_rows, width = tokens.shape
    devices = lax.axis_size("seq")
    heads = w_query.shape[2] // HEAD_DIM
    columns = heads * HEAD_DIM
    hidden = w_up.shape[2]
    group = devices // heads
    rows = own_rows // group
    me = lax.rem(lax.axis_index("seq"), group).astype(jnp.int32).reshape(1)
    half = lax.axis_index("tensor")
    ends = jnp.cumsum(scene_lengths).astype(jnp.int32)

    def in_order(part):
        other = swap_tensor(part)
        return jnp.where(
            half == 0,
            jnp.concatenate([part, other], axis=-1),
            jnp.concatenate([other, part], axis=-1),
        )

    def to_owners(parts):
        return lax.all_to_all(parts, "seq", 0, 0, tiled=True)

    recv, others, normed_one, w_first, norms = project(
        tokens, w_query, w_key, w_value, norm_gain, norm_bias, devices, group
    )
    out_part = in_order(w_out[0].T)
    second_part = jnp.concatenate([out_part, w_up[0], w_down[0].T], axis=1)
    recv, second_part = lax.optimization_barrier((recv, second_part))
    second_all = lax.all_gather(second_part, "seq", axis=0, tiled=True)
    def swap_core(part, by):
        return lax.ppermute(part, "seq", [(i, i ^ by) for i in range(devices)])

    if group > 2:
        others = jnp.stack([swap_core(recv[:, HEAD_DIM:, :], by) for by in range(1, group)])
    out_head, lse = attention_forward(ends, me, recv, others, group)

    dout, dmid, mid, z, grads_second, second_norms = middle(
        to_owners(out_head), tokens, cotangent, second_all, norms, devices, group, columns
    )
    z_other = swap_tensor(z)
    grads_second = lax.psum_scatter(grads_second, "seq", scatter_dimension=0, tiled=True)
    grads_second = grads_second.astype(F32)

    dquery, dpieces = attention_backward(ends, me, recv, others, [dout], out_head, lse, group)
    if group > 2:
        dpieces = sum([dpieces[0].astype(F32)] + [
            swap_core(dpieces[by], by).astype(F32) for by in range(1, group)
        ]).astype(BF)[None]
    dstream, last, dquery_w, dkey_w, dvalue_w, dgain, dbias = finish(
        dquery, dpieces, normed_one, w_first, tokens, dmid, mid, z, z_other, norms, second_norms,
        devices, group,
    )
    return (
        last,
        dstream,
        dquery_w,
        dkey_w,
        dvalue_w,
        grads_second[:, :columns].T[None],
        grads_second[:, columns : columns + hidden][None],
        grads_second[:, columns + hidden :].T[None],
        dgain,
        dbias,
    )


def solution(mesh):
    placed = (
        P("seq", None),
        P(),
        P(None, "seq", "tensor"),
        P(None, "seq", "tensor"),
        P(None, "seq", "tensor"),
        P(None, "tensor", "seq"),
        P(None, "seq", "tensor"),
        P(None, "tensor", "seq"),
        P(None, None, "seq"),
        P(None, None, "seq"),
        P("seq", None),
    )
    return jax.shard_map(
        per_device,
        mesh=mesh,
        in_specs=placed,
        out_specs=(
            P("seq", None),
            P("seq", None),
            P(None, "seq", "tensor"),
            P(None, "seq", "tensor"),
            P(None, "seq", "tensor"),
            P(None, "tensor", "seq"),
            P(None, "seq", "tensor"),
            P(None, "tensor", "seq"),
            P(None, None, "seq"),
            P(None, None, "seq"),
        ),
        check_vma=False,
    )
```

```python
import functools

import jax
import jax.numpy as jnp
from jax import lax
from jax.experimental import pallas as pl
from jax.experimental.pallas import tpu as pltpu
from jax.sharding import PartitionSpec as P

HEAD_DIM = 64
BF = jnp.bfloat16
F32 = jnp.float32
norm_eps = 1e-06
neg_large = -1e30
log2_e = 1.4426950408889634
ln_2 = 0.6931471805599453
STAT_ROWS = 3
SAFE_BOUND = 60.0
VMEM_BYTES = 56 * 2**20


def dot(left, right, left_dim, right_dim):
    return lax.dot_general(
        left, right, (((left_dim,), (right_dim,)), ((), ())), preferred_element_type=F32
    )


def ring_of(devices):
    chips = devices // 2
    index = lax.axis_index("seq")
    core = lax.rem(index, 2)
    chip = index // 2
    if chips != 8:
        return chip, core, lambda place: 2 * place + core
    layer, column = chip // 2, lax.rem(chip, 2)
    place = layer + column * (7 - 2 * layer)

    def seq_index(place):
        side = place // 4
        depth = place + side * (7 - 2 * place)
        return depth * 4 + side * 2 + core

    return place, core, seq_index


def remote_copy(source, target, send_sem, recv_sem, seq):
    return pltpu.make_async_remote_copy(
        src_ref=source, dst_ref=target, send_sem=send_sem, recv_sem=recv_sem,
        device_id={"seq": seq}, device_id_type=pl.DeviceIdType.MESH,
    )


def meet(others):
    barrier = pltpu.get_barrier_semaphore()
    for other in others:
        pl.semaphore_signal(
            barrier, inc=1, device_id=other, device_id_type=pl.DeviceIdType.MESH
        )
    pl.semaphore_wait(barrier, len(others))


def project_kernel(
    tokens_ref, query_ref, key_ref, value_ref, out_ref, gain_ref, bias_ref,
    recv_ref, others_ref, normed_ref, weights_ref, out_w_ref, norms_ref,
    gathered, scaled, sent, send_right, recv_right, send_left, recv_left, send_peer, recv_peer,
    head_send, head_recv, home_sem, core_send, core_recv, out_sem,
    *, devices, group, columns, width,
):
    chips = devices // 2
    depth = width // devices
    rows = tokens_ref.shape[0] // group
    place, core, seq_index = ring_of(devices)
    me = seq_index(place)
    right = seq_index(lax.rem(place + 1, chips))
    left = seq_index(lax.rem(place + chips - 1, chips))
    peer = me + 1 - 2 * core
    heads = columns // HEAD_DIM
    meet([{"seq": lax.rem(me + step, devices)} for step in range(1, devices)])

    def slot(index):
        return gathered.at[pl.ds(pl.multiple_of(index * depth, depth), depth), :]

    mine = pl.ds(pl.multiple_of(me * depth, depth), depth)
    for which, ref in enumerate((query_ref, key_ref, value_ref)):
        gathered[mine, which * columns : (which + 1) * columns] = ref[0]
    norm_rows = jnp.concatenate(
        [gain_ref[0].astype(F32), bias_ref[0].astype(F32), jnp.zeros((124, depth), F32)], axis=0
    )
    gathered[mine, 3 * columns : 4 * columns] = out_ref[0].T
    gathered[mine, 4 * columns :] = norm_rows.T.astype(BF)

    to_right, to_left = chips // 2, chips - 1 - chips // 2

    def rightward(step):
        index = seq_index(lax.rem(place - step + chips, chips))
        return remote_copy(
            slot(index), slot(index), send_right.at[step], recv_right.at[step], right
        )

    def leftward(step):
        index = seq_index(lax.rem(place + step, chips))
        return remote_copy(slot(index), slot(index), send_left.at[step], recv_left.at[step], left)

    def across(distance):
        index = seq_index(lax.rem(place + distance + chips, chips))
        return remote_copy(
            slot(index), slot(index),
            send_peer.at[(distance + chips) % chips], recv_peer.at[(distance + chips) % chips], peer,
        )

    def arrive_right(step):
        index = seq_index(lax.rem(place - step - 1 + chips, chips))
        remote_copy(
            slot(index), slot(index), send_right.at[step], recv_right.at[step], right
        ).wait_recv()

    def arrive_left(step):
        index = seq_index(lax.rem(place + step + 1, chips))
        remote_copy(
            slot(index), slot(index), send_left.at[step], recv_left.at[step], left
        ).wait_recv()

    rightward(0).start()
    leftward(0).start()
    across(0).start()

    def normalize(index, carry):
        at = pl.ds(pl.multiple_of(index * 128, 128), 128)
        stream = tokens_ref[at, :].astype(F32)
        centred = stream - jnp.mean(stream, axis=-1, keepdims=True)
        spread = jnp.mean(centred * centred, axis=-1, keepdims=True)
        scaled[at, :] = centred * lax.rsqrt(spread + norm_eps)
        return carry

    lax.fori_loop(0, tokens_ref.shape[0] // 128, normalize, 0)

    for step in range(to_right):
        arrive_right(step)
        if step + 1 < to_right:
            rightward(step + 1).start()
        across(-step - 1).start()
        if step < to_left:
            arrive_left(step)
            if step + 1 < to_left:
                leftward(step + 1).start()
            across(step + 1).start()
    for distance in range(chips):
        index = seq_index(lax.rem(place + distance, chips)) + 1 - 2 * core
        remote_copy(
            slot(index), slot(index), send_peer.at[distance], recv_peer.at[distance], peer
        ).wait_recv()

    store = pltpu.make_async_copy(gathered.at[:, : 3 * columns], weights_ref, out_sem.at[0])
    store.start()
    store_out = pltpu.make_async_copy(
        gathered.at[:, 3 * columns : 4 * columns], out_w_ref, out_sem.at[1]
    )
    store_out.start()
    norms = gathered[:, 4 * columns :].astype(F32).T
    norms_ref[...] = norms[0:8]

    def apply_norm(index, carry):
        at = pl.ds(pl.multiple_of(index * 128, 128), 128)
        normed_ref[at, :] = (scaled[at, :] * norms[0:1] + norms[2:3]).astype(BF)
        return carry

    lax.fori_loop(0, tokens_ref.shape[0] // 128, apply_norm, 0)

    def head_copy(step, which):
        where = lax.rem(me + step, devices)
        at = slice(which * HEAD_DIM, (which + 1) * HEAD_DIM)
        return remote_copy(
            sent.at[where, at, :], recv_ref.at[me, at, :], head_send.at[step, which],
            head_recv.at[me, which], where,
        )

    def core_copy(source_ref, source):
        return remote_copy(
            source_ref.at[source, HEAD_DIM:, :], others_ref.at[0, source], core_send.at[source],
            core_recv.at[source], peer,
        )

    home = pltpu.make_async_copy(sent.at[me], recv_ref.at[me], home_sem)
    for which in (1, 2, 0):
        weights = gathered[:, which * columns : (which + 1) * columns].T
        factor = HEAD_DIM**-0.5 * log2_e if which == 0 else 1.0

        def project(core_index, carry, which=which, weights=weights, factor=factor):
            at = pl.ds(pl.multiple_of(core_index * rows, rows), rows)
            result = (dot(weights, normed_ref[at, :], 1, 1) * factor).astype(BF)
            for head in range(heads):
                sent[head * group + core_index, which * HEAD_DIM : (which + 1) * HEAD_DIM, :] = (
                    result[head * HEAD_DIM : (head + 1) * HEAD_DIM, :]
                )
            return carry

        lax.fori_loop(0, group, project, 0)

        def send(step, carry, which=which):
            head_copy(step, which).start()
            return carry

        lax.fori_loop(1, devices, send, 0)
        if which == 2 and group == 2:
            core_copy(sent, me).start()
    home.start()

    def wait_head(step, carry, which):
        source = lax.rem(me - step + devices, devices)
        at = slice(which * HEAD_DIM, (which + 1) * HEAD_DIM)
        remote_copy(
            sent.at[source, at, :], recv_ref.at[source, at, :], head_send.at[0, which],
            head_recv.at[source, which], source,
        ).wait_recv()
        return carry

    def forward(step, carry):
        wait_head(step, carry, 1)
        wait_head(step, carry, 2)
        if group == 2:
            core_copy(recv_ref, lax.rem(me - step + devices, devices)).start()
        return carry

    lax.fori_loop(1, devices, forward, 0)
    lax.fori_loop(1, devices, functools.partial(wait_head, which=0), 0)
    home.wait()

    def finish_core(source, carry):
        core_copy(recv_ref, source).wait()
        return carry

    if group == 2:
        lax.fori_loop(0, devices, finish_core, 0)

    def wait_sent(step, carry):
        for which in range(3):
            head_copy(step, which).wait_send()
        return carry

    lax.fori_loop(1, devices, wait_sent, 0)
    for step in range(to_right):
        rightward(step).wait_send()
    for step in range(to_left):
        leftward(step).wait_send()
    for distance in range(chips):
        across(distance).wait_send()
    store.wait()
    store_out.wait()


def project(tokens, w_query, w_key, w_value, w_out, norm_gain, norm_bias, devices, group):
    own_rows, width = tokens.shape
    columns = w_query.shape[2]
    chips = devices // 2
    rows = own_rows // group
    whole = pl.BlockSpec(memory_space=pltpu.VMEM)
    far = pl.BlockSpec(memory_space=pl.ANY)
    dma = pltpu.SemaphoreType.DMA
    return pl.pallas_call(
        functools.partial(
            project_kernel, devices=devices, group=group, columns=columns, width=width
        ),
        in_specs=[whole] * 7,
        out_specs=[far, far, whole, far, far, whole],
        out_shape=[
            jax.ShapeDtypeStruct((devices, 3 * HEAD_DIM, rows), BF),
            jax.ShapeDtypeStruct((1, devices, 2 * HEAD_DIM, rows), BF),
            jax.ShapeDtypeStruct((own_rows, width), BF),
            jax.ShapeDtypeStruct((width, 3 * columns), BF),
            jax.ShapeDtypeStruct((width, columns), BF),
            jax.ShapeDtypeStruct((8, width), F32),
        ],
        scratch_shapes=[
            pltpu.VMEM((width, 4 * columns + 128), BF),
            pltpu.VMEM((own_rows, width), F32),
            pltpu.VMEM((devices, 3 * HEAD_DIM, rows), BF),
            dma((chips // 2,)), dma((chips // 2,)),
            dma((chips // 2,)), dma((chips // 2,)),
            dma((chips,)), dma((chips,)),
            dma((devices, 3)), dma((devices, 3)), dma,
            dma((devices,)), dma((devices,)),
            dma((2,)),
        ],
        compiler_params=pltpu.CompilerParams(
            vmem_limit_bytes=VMEM_BYTES, collective_id=1, has_side_effects=True
        ),
        name="project",
    )(tokens, w_query, w_key, w_value, w_out, norm_gain, norm_bias)


def finish_kernel(
    dquery_ref, dpieces_far, normed_far, weights_far, tokens_far, dmid_far, mid_far, z_far,
    z_other_far, norms_ref, second_ref,
    dstream_far, last_far, dquery_w_ref, dkey_w_ref, dvalue_w_ref, dgain_ref, dbias_ref,
    normed, weights, tokens, dmid, mid, z, z_other, own_piece,
    core_got, sent, got, flat, partial_sent, partial_got, summed_grads, partial, from_peer,
    ring_first, ring, total, few_sent, few_got,
    load_sem, store_sem, core_send, core_recv, head_send, head_recv, x_send, x_recv,
    peer_send, peer_recv, ring_send, ring_recv, few_send, few_recv,
    *, devices, group, cores, columns, width,
):
    chips = devices // 2
    depth = width // devices
    own_rows = tokens.shape[0]
    rows = own_rows // group
    heads = columns // HEAD_DIM
    wide = 3 * columns + 128
    lanes = 128
    lines_wide = wide // lanes
    cuts = [(lines_wide * turn + 3) // 4 * lanes for turn in range(5)]
    chunks = rows // lanes
    place, core, seq_index = ring_of(devices)
    me = seq_index(place)
    right = {"seq": seq_index(lax.rem(place + 1, chips))}
    left = {"seq": seq_index(lax.rem(place + chips - 1, chips))}
    peer = {"seq": me + 1 - 2 * core}
    across = {"tensor": 1 - lax.axis_index("tensor")}
    group_place = lax.rem(me, group)

    loads = {}
    for number, (name, far, near) in enumerate((
        ("piece", dpieces_far.at[0], own_piece), ("tokens", tokens_far, tokens), ("weights", weights_far, weights),
        ("normed", normed_far, normed), ("z", z_far, z), ("z_other", z_other_far, z_other),
        ("mid", mid_far, mid), ("dmid", dmid_far, dmid),
    )):
        loads[name] = pltpu.make_async_copy(far, near, load_sem.at[number])
        loads[name].start()

    barrier = pltpu.get_barrier_semaphore()
    for step in range(1, devices):
        pl.semaphore_signal(
            barrier, inc=1, device_id={"seq": lax.rem(me + step, devices)},
            device_id_type=pl.DeviceIdType.MESH,
        )
    pl.semaphore_signal(barrier, inc=1, device_id=across, device_id_type=pl.DeviceIdType.MESH)
    pl.semaphore_wait(barrier, devices)

    def copy_to(source, target, send_sem, recv_sem, where):
        return pltpu.make_async_remote_copy(
            src_ref=source, dst_ref=target, send_sem=send_sem, recv_sem=recv_sem,
            device_id=where, device_id_type=pl.DeviceIdType.MESH,
        )

    def core_copy(by, chunk):
        other = jnp.int32(0)
        bit = 1
        while bit < group:
            mine = lax.rem(group_place // bit, 2)
            other = other + bit * ((1 - mine) if by & bit else mine)
            bit *= 2
        at = slice(chunk * lanes, (chunk + 1) * lanes)
        return copy_to(
            dpieces_far.at[by, :, :, at], core_got.at[by - 1, :, :, at],
            core_send.at[by - 1, chunk], core_recv.at[by - 1, chunk],
            {"seq": me - group_place + other},
        )

    def head_copy(step, chunk):
        where = lax.rem(me + step, devices)
        at = slice(chunk * lanes, (chunk + 1) * lanes)
        return copy_to(
            sent.at[where, :, at], got.at[me, :, at],
            head_send.at[step, chunk], head_recv.at[me, chunk], {"seq": where},
        )

    for chunk in range(chunks):
        for by in range(1, cores):
            core_copy(by, chunk).start()
    loads["piece"].wait()
    for chunk in range(chunks):
        at = slice(chunk * lanes, (chunk + 1) * lanes)
        for by in range(1, cores):
            core_copy(by, chunk).wait_recv()

        def gather(index, carry, at=at):
            piece = own_piece[index, :, at].astype(F32)
            for by in range(1, cores):
                piece = piece + core_got[by - 1, index, :, at].astype(F32)
            sent[index, HEAD_DIM:, at] = piece.astype(BF)
            sent[index, 0:HEAD_DIM, at] = dquery_ref[index, :, at]
            return carry

        lax.fori_loop(0, devices, gather, 0)

        def send(step, carry, chunk=chunk):
            head_copy(step, chunk).start()
            return carry

        lax.fori_loop(1, devices, send, 0)

    loads["z"].wait()
    loads["z_other"].wait()
    loads["mid"].wait()

    def add_last(index, carry):
        at = pl.ds(pl.multiple_of(index * lanes, lanes), lanes)
        both = z[at, :].astype(F32) + z_other[at, :].astype(F32)
        z[at, :] = (mid[at, :] + both).astype(BF)
        return carry

    lax.fori_loop(0, own_rows // lanes, add_last, 0)
    store_last = pltpu.make_async_copy(z, last_far, store_sem.at[0])
    store_last.start()
    for name in ("tokens", "weights", "normed", "dmid"):
        loads[name].wait()

    def part_rows(place_in_group, chunk):
        return slice(place_in_group * rows + chunk * lanes, place_in_group * rows + (chunk + 1) * lanes)

    def x_copy(place_in_group, chunk):
        at = part_rows(place_in_group, chunk)
        number = place_in_group * chunks + chunk
        return copy_to(
            partial_sent.at[at, :], partial_got.at[at, :], x_send.at[number], x_recv.at[number],
            across,
        )

    def unit_rows(at):
        stream = tokens[at, :].astype(F32)
        centred = stream - jnp.mean(stream, axis=-1, keepdims=True)
        spread = jnp.mean(centred * centred, axis=-1, keepdims=True)
        inverse = lax.rsqrt(spread + norm_eps)
        return centred * inverse, inverse

    def finish_norm(chunk):
        for place_in_group in range(group):
            at = part_rows(place_in_group, chunk)
            x_copy(place_in_group, chunk).wait_recv()
            dnormed = partial_sent[at, :].astype(F32) + partial_got[at, :].astype(F32)
            unit, inverse = unit_rows(at)
            dunit = dnormed * norms_ref[0:1, :]
            mean = jnp.mean(dunit, axis=-1, keepdims=True)
            along = jnp.mean(dunit * unit, axis=-1, keepdims=True)
            dmid[at, :] = dmid[at, :] + (dunit - mean - unit * along) * inverse

    gain_sum = jnp.zeros((1, width), F32)
    bias_sum = jnp.zeros((1, width), F32)
    lines = 256
    for chunk in range(chunks):
        at = slice(chunk * lanes, (chunk + 1) * lanes)

        def flatten(index, carry, chunk=chunk, at=at):
            head = index // group
            start = lax.rem(index, group) * rows + chunk * lanes
            to_rows = pl.ds(pl.multiple_of(start, lanes), lanes)

            def put(source):
                for which in range(3):
                    to = pl.ds(
                        pl.multiple_of(which * columns + head * HEAD_DIM, HEAD_DIM), HEAD_DIM
                    )
                    flat[to, to_rows] = source[index, which * HEAD_DIM : (which + 1) * HEAD_DIM, at]

            @pl.when(index == me)
            def _():
                put(sent)

            @pl.when(index != me)
            def _():
                copy_to(
                    sent.at[index, :, at], got.at[index, :, at],
                    head_send.at[0, chunk], head_recv.at[index, chunk], {"seq": index},
                ).wait_recv()
                put(got)

            return carry

        lax.fori_loop(0, devices, flatten, 0)
        ats = [part_rows(place_in_group, chunk) for place_in_group in range(group)]
        flat_chunk = jnp.concatenate([flat[:, part] for part in ats], axis=1)

        def sum_grads():
            normed_t = jnp.concatenate([normed[part, :] for part in ats], axis=0).T
            for line in range(width // lines):
                here = slice(line * lines, (line + 1) * lines)
                result = dot(normed_t[here, :], flat_chunk, 1, 1)
                if chunk > 0:
                    result = result + summed_grads[here, :]
                if chunk + 1 < chunks:
                    summed_grads[here, :] = result
                else:
                    partial[here, 0 : 3 * columns] = result.astype(BF)

        def send_dnormed(gain_sum, bias_sum):
            result = dot(flat_chunk.T, weights[...], 1, 1)
            for place_in_group in range(group):
                here = slice(place_in_group * lanes, (place_in_group + 1) * lanes)
                partial_sent[ats[place_in_group], :] = result[here, :].astype(BF)
                x_copy(place_in_group, chunk).start()
            for place_in_group in range(group):
                here = slice(place_in_group * lanes, (place_in_group + 1) * lanes)
                unit, _ = unit_rows(ats[place_in_group])
                gain_sum = gain_sum + jnp.sum(result[here, :] * unit, axis=0, keepdims=True)
                bias_sum = bias_sum + jnp.sum(result[here, :], axis=0, keepdims=True)
            return gain_sum, bias_sum

        gain_sum, bias_sum = send_dnormed(gain_sum, bias_sum)
        sum_grads()
        if chunk > 0 and chunk + 1 < chunks:
            finish_norm(chunk - 1)

    norm_rows = jnp.concatenate(
        [
            gain_sum, second_ref[0:1, :] * 0.5, bias_sum, second_ref[1:2, :] * 0.5,
            jnp.zeros((124, width), F32),
        ],
        axis=0,
    )
    partial[:, 3 * columns :] = norm_rows.T.astype(BF)

    order = []
    for step in range(chips // 2):
        for offset in (-step - 1, step + 1):
            if offset % chips not in order:
                order.append(offset % chips)
    order.append(0)

    def peer_copy(number):
        where = lax.rem(place + order[number], chips)
        theirs = seq_index(where) + 1 - 2 * core
        return copy_to(
            partial.at[pl.ds(pl.multiple_of(theirs * depth, depth), depth), :],
            from_peer.at[pl.ds(pl.multiple_of(where * depth, depth), depth), :],
            peer_send.at[number], peer_recv.at[number], peer,
        )

    for number in range(chips):
        peer_copy(number).start()

    waited = []

    def chip_block(offset, low, high):
        number = order.index(offset % chips)
        if number not in waited:
            peer_copy(number).wait_recv()
            waited.append(number)
        where = lax.rem(place + offset % chips, chips)
        own = pl.ds(pl.multiple_of(seq_index(where) * depth, depth), depth)
        there = pl.ds(pl.multiple_of(where * depth, depth), depth)
        return partial[own, low:high].astype(F32) + from_peer[there, low:high].astype(F32)

    steps = chips - 1

    rings = [(True, 0), (False, 2), (True, 1), (False, 3)]

    def ring_copy(step, toward_right, turn):
        low, high = cuts[turn], cuts[turn + 1]
        source = ring_first.at[:, low:high] if step == 0 else ring.at[step - 1, :, low:high]
        return copy_to(
            source, ring.at[step, :, low:high], ring_send.at[turn, step], ring_recv.at[turn, step],
            right if toward_right else left,
        )

    for toward_right, turn in rings:
        low, high = cuts[turn], cuts[turn + 1]
        ring_first[:, low:high] = chip_block(-1 if toward_right else 1, low, high).astype(BF)
        ring_copy(0, toward_right, turn).start()
    pending = list(range(max(chunks - 2, 0), chunks))
    for step in range(steps):
        if pending and step in (1, steps // 2):
            finish_norm(pending.pop(0))
        for toward_right, turn in rings:
            low, high = cuts[turn], cuts[turn + 1]
            ring_copy(step, toward_right, turn).wait_recv()
            offset = -step - 2 if toward_right else step + 2
            summed = ring[step, :, low:high].astype(F32) + chip_block(offset, low, high)
            if step + 1 < steps:
                ring[step, :, low:high] = summed.astype(BF)
                ring_copy(step + 1, toward_right, turn).start()
            else:
                total[:, low:high] = summed
    few_sent[...] = total[:, 3 * columns :]
    few = copy_to(few_sent, few_got, few_send, few_recv, across)
    few.start()
    for chunk in pending:
        finish_norm(chunk)
    store_stream = pltpu.make_async_copy(dmid, dstream_far, store_sem.at[1])
    store_stream.start()
    dquery_w_ref[0] = total[:, 0:columns]
    dkey_w_ref[0] = total[:, columns : 2 * columns]
    dvalue_w_ref[0] = total[:, 2 * columns : 3 * columns]
    few.wait()
    norm_rows = (few_sent[...] + few_got[...]).T
    dgain_ref[0] = norm_rows[0:2, :]
    dbias_ref[0] = norm_rows[2:4, :]
    for chunk in range(chunks):
        for by in range(1, cores):
            core_copy(by, chunk).wait_send()
        for place_in_group in range(group):
            x_copy(place_in_group, chunk).wait_send()

        def wait_head(step, carry, chunk=chunk):
            head_copy(step, chunk).wait_send()
            return carry

        lax.fori_loop(1, devices, wait_head, 0)
    for number in range(chips):
        peer_copy(number).wait_send()
    for step in range(steps):
        for toward_right, turn in rings:
            ring_copy(step, toward_right, turn).wait_send()
    store_last.wait()
    store_stream.wait()


def finish(
    dquery, dpieces, normed, weights, tokens, dmid, mid, z, z_other, norms, second, devices, group
):
    own_rows, width = tokens.shape
    cores, _, _, rows = dpieces.shape
    columns = weights.shape[1] // 3
    chips = devices // 2
    depth = width // devices
    wide = 3 * columns + 128
    steps = chips - 1
    chunks = rows // 128
    whole = pl.BlockSpec(memory_space=pltpu.VMEM)
    far = pl.BlockSpec(memory_space=pl.ANY)
    dma = pltpu.SemaphoreType.DMA
    vmem = pltpu.VMEM
    return pl.pallas_call(
        functools.partial(
            finish_kernel, devices=devices, group=group, cores=cores, columns=columns, width=width
        ),
        in_specs=[whole] + [far] * 8 + [whole] * 2,
        out_specs=[far] * 2 + [whole] * 5,
        out_shape=[
            jax.ShapeDtypeStruct((own_rows, width), F32),
            jax.ShapeDtypeStruct((own_rows, width), BF),
        ]
        + [jax.ShapeDtypeStruct((1, depth, columns), F32)] * 3
        + [jax.ShapeDtypeStruct((1, 2, depth), F32)] * 2,
        scratch_shapes=[
            vmem((own_rows, width), BF), vmem((width, 3 * columns), BF),
            vmem((own_rows, width), BF), vmem((own_rows, width), F32),
            vmem((own_rows, width), F32), vmem((own_rows, width), BF),
            vmem((own_rows, width), BF), vmem((devices, 128, rows), BF),
            vmem((max(cores - 1, 1), devices, 128, rows), BF),
            vmem((devices, 3 * HEAD_DIM, rows), BF), vmem((devices, 3 * HEAD_DIM, rows), BF),
            vmem((3 * columns, own_rows), BF),
            vmem((own_rows, width), BF), vmem((own_rows, width), BF),
            vmem((width, 3 * columns), F32), vmem((width, wide), BF),
            vmem((chips * depth, wide), BF),
            vmem((depth, wide), BF), vmem((steps, depth, wide), BF),
            vmem((depth, wide), F32),
            vmem((depth, 128), F32), vmem((depth, 128), F32),
            dma((8,)), dma((2,)),
            dma((max(cores - 1, 1), chunks)), dma((max(cores - 1, 1), chunks)),
            dma((devices, chunks)), dma((devices, chunks)),
            dma((group * chunks,)), dma((group * chunks,)),
            dma((chips,)), dma((chips,)),
            dma((4, steps)), dma((4, steps)),
            dma, dma,
        ],
        compiler_params=pltpu.CompilerParams(
            vmem_limit_bytes=60 * 2**20, collective_id=2, has_side_effects=True
        ),
        name="finish",
    )(dquery, dpieces, normed, weights, tokens, dmid, mid, z, z_other, norms, second)


def middle_kernel(
    mixed_far, tokens_ref, dz_ref, out_own_ref, out_other_ref, second_ref, norms_ref,
    dout_ref, dmid_ref, mid_ref, z_ref, grads_ref, norm_grads_ref,
    weights, tokens, dz, flat, flat_other, normed, act, dup, mid, dmid, dsent, dgot, dy, z,
    out_t, dout, stage,
    load_sem, mixed_send, mixed_recv, flat_send, flat_recv, x_send, x_recv, head_send, head_recv, store_sem, stage_sem,
    *, devices, group, columns, hidden,
):
    own_rows, width = tokens.shape
    rows = own_rows // group
    heads = columns // HEAD_DIM
    parts = x_send.shape[0]
    part_rows = own_rows // parts
    block = 512
    me = lax.axis_index("seq").astype(jnp.int32)
    core = lax.rem(me, group)
    half = lax.axis_index("tensor").astype(jnp.int32)
    across = {"tensor": 1 - half}

    own_cut = pl.ds(pl.multiple_of(half * columns, columns), columns)
    other_cut = pl.ds(pl.multiple_of((1 - half) * columns, columns), columns)
    loads = [
        pltpu.make_async_copy(out_own_ref, weights.at[:, own_cut], load_sem.at[0]),
        pltpu.make_async_copy(tokens_ref, tokens, load_sem.at[1]),
        pltpu.make_async_copy(second_ref, weights.at[:, width:], load_sem.at[2]),
        pltpu.make_async_copy(dz_ref, dz, load_sem.at[3]),
        pltpu.make_async_copy(out_other_ref, weights.at[:, other_cut], load_sem.at[4]),
    ]
    for load in loads:
        load.start()

    barrier = pltpu.get_barrier_semaphore()
    for other in range(devices):
        @pl.when(me != other)
        def _(other=other):
            pl.semaphore_signal(
                barrier, inc=1, device_id={"seq": other}, device_id_type=pl.DeviceIdType.MESH
            )

    pl.semaphore_signal(
        barrier, inc=1, device_id=across, device_id_type=pl.DeviceIdType.MESH
    )
    pl.semaphore_wait(barrier, devices)

    def copy_to(source, target, send_sem, recv_sem, where):
        return pltpu.make_async_remote_copy(
            src_ref=source, dst_ref=target, send_sem=send_sem, recv_sem=recv_sem,
            device_id=where, device_id_type=pl.DeviceIdType.MESH,
        )

    def rows_of(part):
        return pl.ds(pl.multiple_of(part * part_rows, part_rows), part_rows)

    piece_rows = min(part_rows, rows)
    pieces = rows // piece_rows
    my_head = me // group

    def mixed_copy(step, piece):
        where = lax.rem(me + step, devices)
        cut = slice(piece * piece_rows, (piece + 1) * piece_rows)
        to = pl.ds(pl.multiple_of(core * rows + piece * piece_rows, piece_rows), piece_rows)
        return copy_to(
            mixed_far.at[where, :, cut],
            flat.at[pl.ds(pl.multiple_of(my_head * HEAD_DIM, HEAD_DIM), HEAD_DIM), to],
            mixed_send.at[step, piece], mixed_recv.at[me, piece], {"seq": where},
        )

    def mixed_home(piece):
        cut = slice(piece * piece_rows, (piece + 1) * piece_rows)
        to = pl.ds(pl.multiple_of(core * rows + piece * piece_rows, piece_rows), piece_rows)
        return pltpu.make_async_copy(
            mixed_far.at[me, :, cut],
            flat.at[pl.ds(pl.multiple_of(my_head * HEAD_DIM, HEAD_DIM), HEAD_DIM), to],
            mixed_send.at[0, piece],
        )

    for piece in range(pieces):
        mixed_home(piece).start()

        def send_mixed(step, carry, piece=piece):
            mixed_copy(step, piece).start()
            return carry

        lax.fori_loop(1, devices, send_mixed, 0)

    def wait_mixed(place, piece):
        to = pl.ds(place * rows + piece * piece_rows, piece_rows)

        def one(head, carry):
            source = head * group + place
            at = pl.ds(pl.multiple_of(head * HEAD_DIM, HEAD_DIM), HEAD_DIM)

            @pl.when(source != me)
            def _():
                copy_to(
                    flat.at[at, to], flat.at[at, to], mixed_send.at[0, piece],
                    mixed_recv.at[source, piece], {"seq": source},
                ).wait_recv()

            return carry

        lax.fori_loop(0, heads, one, 0)

    def flat_copy(part):
        at = rows_of(part)
        return copy_to(
            flat.at[:, at], flat_other.at[:, at], flat_send.at[part], flat_recv.at[part], across
        )

    def x_copy(part):
        at = rows_of(part)
        return copy_to(dsent.at[at, :], dgot.at[at, :], x_send.at[part], x_recv.at[part], across)

    span = part_rows // piece_rows
    turns = [
        (place * rows + piece * piece_rows) // part_rows
        for piece in range(pieces) for place in range(0, group, span)
    ]
    for piece in range(pieces):
        mixed_home(piece).wait()
    for turn, part in enumerate(turns):
        for place in range(group):
            for piece in range(pieces):
                if (place * rows + piece * piece_rows) // part_rows == part:
                    wait_mixed(place, piece)
        flat_copy(part).start()
    loads[0].wait()
    out_t[...] = weights[:, own_cut].T
    for load in loads[1:]:
        load.wait()
    first_half = half == 0

    def unit_rows(at):
        stream = mid[at, :]
        centred = stream - jnp.mean(stream, axis=-1, keepdims=True)
        spread = jnp.mean(centred * centred, axis=-1, keepdims=True)
        inverse = lax.rsqrt(spread + norm_eps)
        return centred * inverse, inverse

    def store_mid(part):
        at = rows_of(part)
        return pltpu.make_async_copy(mid.at[at, :], mid_ref.at[at, :], store_sem.at[0, part])

    def forward(part, carry):
        at = rows_of(part)
        flat_copy(part).wait_recv()
        own, other = flat[:, at], flat_other[:, at]
        low = jnp.where(first_half, own, other).T
        high = jnp.where(first_half, other, own).T
        projected = dot(low, weights[:, 0:columns], 1, 1) + dot(
            high, weights[:, columns:width], 1, 1
        )
        mid[at, :] = tokens[at, :].astype(F32) + projected
        store_mid(part).start()
        unit, _ = unit_rows(at)
        normed[at, :] = (unit * norms_ref[1:2, :] + norms_ref[3:4, :]).astype(BF)

        def hidden_block(index, total):
            cut = pl.ds(pl.multiple_of(index * block, block), block)
            up_cut = pl.ds(pl.multiple_of(width + index * block, block), block)
            down_cut = pl.ds(pl.multiple_of(width + hidden + index * block, block), block)
            up_w = weights[:, up_cut]
            up = dot(normed[at, :], up_w, 1, 0)
            dact = dot(dz[at, :], weights[:, down_cut], 1, 0)
            square = up * up
            bend = jnp.tanh(0.7978845608028654 * up * (1.0 + 0.044715 * square))
            grow = 0.5 + 0.5 * bend
            slope = grow + 0.5 * up * (1.0 - bend * bend) * (
                0.7978845608028654 + 0.10703222440890037 * square
            )
            act[at, cut] = (up * grow).astype(BF)
            dup_block = (dact * slope).astype(BF)
            dup[at, cut] = dup_block
            return total + dot(dup_block, up_w, 1, 1)

        total = lax.fori_loop(
            0, hidden // block, hidden_block, jnp.zeros((part_rows, width), F32)
        )
        dsent[at, :] = total.astype(BF)
        x_copy(part).start()
        return carry

    def forward_turn(turn, carry):
        return forward(lax.rem(turn, group) * (parts // group) + turn // group, carry)

    lax.fori_loop(0, parts, forward_turn if pieces > 1 else forward, 0)

    def head_copies(piece, head):
        start = piece * piece_rows
        owner = head * group + start // rows
        slot = lax.rem(piece, pieces)
        source = dout.at[
            pl.ds(pl.multiple_of(head * HEAD_DIM, HEAD_DIM), HEAD_DIM),
            pl.ds(pl.multiple_of(start, piece_rows), piece_rows),
        ]
        target = dout_ref.at[me, :, pl.ds(pl.multiple_of(slot * piece_rows, piece_rows), piece_rows)]
        away = copy_to(
            source, target, head_send.at[head, piece], head_recv.at[me, slot], {"seq": owner}
        )
        home = pltpu.make_async_copy(source, target, head_send.at[head, piece])
        return away, home, owner == me

    def send_heads(part):
        def send(index, carry):
            piece = part * (part_rows // piece_rows) + index // heads
            away, home, is_home = head_copies(piece, lax.rem(index, heads))

            @pl.when(is_home)
            def _():
                home.start()

            @pl.when(jnp.logical_not(is_home))
            def _():
                away.start()

            return carry

        lax.fori_loop(0, heads * (part_rows // piece_rows), send, 0)

    def store_dmid(part):
        at = rows_of(part)
        return pltpu.make_async_copy(dmid.at[at, :], dmid_ref.at[at, :], store_sem.at[1, part])

    def backward(part, sums):
        gain_sum, bias_sum = sums
        at = rows_of(part)
        x_copy(part).wait_recv()
        dnormed = dsent[at, :].astype(F32) + dgot[at, :].astype(F32)
        unit, inverse = unit_rows(at)
        dunit = dnormed * norms_ref[1:2, :]
        mean = jnp.mean(dunit, axis=-1, keepdims=True)
        along = jnp.mean(dunit * unit, axis=-1, keepdims=True)
        result = dz[at, :].astype(F32) + (dunit - mean - unit * along) * inverse
        dmid[at, :] = result
        store_dmid(part).start()
        low = result.astype(BF)
        dy[at, :] = low
        dout[:, at] = dot(out_t[...], low, 1, 1).astype(BF)
        send_heads(part)
        gain_sum = gain_sum + jnp.sum(dnormed * unit, axis=0, keepdims=True)
        bias_sum = bias_sum + jnp.sum(dnormed, axis=0, keepdims=True)
        return gain_sum, bias_sum

    def last_product(part, carry):
        at = rows_of(part)
        z[at, :] = dot(act[at, :], weights[:, width + hidden :], 1, 1).astype(BF)
        return carry

    lax.fori_loop(0, parts, last_product, 0)
    store_z = pltpu.make_async_copy(z, z_ref, load_sem.at[0])
    store_z.start()

    def grads_into(left_t, right_ref, first_column):
        blocks = right_ref.shape[1] // block

        def store(index, slot):
            cut = pl.ds(pl.multiple_of(first_column + index * block, block), block)
            return pltpu.make_async_copy(stage.at[slot], grads_ref.at[:, cut], stage_sem.at[slot])

        def one(index, carry):
            slot = lax.rem(index, 2)

            @pl.when(index >= 2)
            def _():
                store(index - 2, slot).wait()

            cut = pl.ds(pl.multiple_of(index * block, block), block)
            stage[slot] = dot(left_t, right_ref[:, cut], 1, 0).astype(BF)
            store(index, slot).start()
            return carry

        lax.fori_loop(0, blocks, one, 0)
        for index in range(blocks - 2, blocks):
            store(index, index % 2).wait()

    sums = (jnp.zeros((1, width), F32), jnp.zeros((1, width), F32))
    sums = backward(turns[0], sums)
    grads_into(normed[...].T, dup, columns)
    sums = backward(turns[1], sums)
    grads_into(dz[...].T, act, columns + hidden)
    for part in turns[2:]:
        sums = backward(part, sums)
    stage[0] = dot(dy[...].T, flat[...], 1, 1).astype(BF)
    store_out = pltpu.make_async_copy(stage.at[0], grads_ref.at[:, 0:columns], stage_sem.at[0])
    store_out.start()
    norm_grads_ref[...] = jnp.concatenate([*sums, jnp.zeros((6, width), F32)], axis=0)

    def wait_sent(index, carry):
        away, home, is_home = head_copies(index // heads, lax.rem(index, heads))

        @pl.when(is_home)
        def _():
            home.wait()

        @pl.when(jnp.logical_not(is_home))
        def _():
            away.wait_send()

        return carry

    lax.fori_loop(0, heads * (own_rows // piece_rows), wait_sent, 0)

    def wait_heads(index, carry):
        source = index // pieces
        slot = lax.rem(index, pieces)
        cut = pl.ds(pl.multiple_of(slot * piece_rows, piece_rows), piece_rows)

        @pl.when(source != me)
        def _():
            copy_to(
                dout.at[0:HEAD_DIM, 0:piece_rows], dout_ref.at[source, :, cut],
                head_send.at[0, 0], head_recv.at[source, slot], {"seq": source},
            ).wait_recv()

        return carry

    lax.fori_loop(0, devices * pieces, wait_heads, 0)
    for piece in range(pieces):
        def sent_mixed(step, carry, piece=piece):
            mixed_copy(step, piece).wait_send()
            return carry

        lax.fori_loop(1, devices, sent_mixed, 0)
    for part in range(parts):
        flat_copy(part).wait_send()
        x_copy(part).wait_send()
        store_mid(part).wait()
        store_dmid(part).wait()
    store_z.wait()
    store_out.wait()


def middle(mixed, tokens, dz, out_own, out_other, second, norms, devices, group):
    own_rows, width = tokens.shape
    rows = own_rows // group
    columns = out_own.shape[1]
    hidden = second.shape[1] // 2
    parts = 4
    piece_rows = min(own_rows // parts, rows)
    whole = pl.BlockSpec(memory_space=pltpu.VMEM)
    far = pl.BlockSpec(memory_space=pl.ANY)
    dma = pltpu.SemaphoreType.DMA
    vmem = pltpu.VMEM
    return pl.pallas_call(
        functools.partial(
            middle_kernel, devices=devices, group=group, columns=columns, hidden=hidden
        ),
        in_specs=[far] * 6 + [whole],
        out_specs=[far] * 5 + [whole],
        out_shape=[
            jax.ShapeDtypeStruct((devices, HEAD_DIM, rows), BF),
            jax.ShapeDtypeStruct((own_rows, width), F32),
            jax.ShapeDtypeStruct((own_rows, width), F32),
            jax.ShapeDtypeStruct((own_rows, width), BF),
            jax.ShapeDtypeStruct((width, columns + 2 * hidden), BF),
            jax.ShapeDtypeStruct((8, width), F32),
        ],
        scratch_shapes=[
            vmem((width, width + 2 * hidden), BF),
            vmem((own_rows, width), BF), vmem((own_rows, width), BF),
            vmem((columns, own_rows), BF), vmem((columns, own_rows), BF),
            vmem((own_rows, width), BF),
            vmem((own_rows, hidden), BF), vmem((own_rows, hidden), BF),
            vmem((own_rows, width), F32), vmem((own_rows, width), F32),
            vmem((own_rows, width), BF), vmem((own_rows, width), BF),
            vmem((own_rows, width), BF), vmem((own_rows, width), BF),
            vmem((columns, width), BF), vmem((columns, own_rows), BF),
            vmem((2, width, 512), BF),
            dma((5,)), dma((devices, rows // piece_rows)), dma((devices, rows // piece_rows)),
            dma((parts,)), dma((parts,)), dma((parts,)), dma((parts,)),
            dma((columns // HEAD_DIM, own_rows // piece_rows)),
            dma((devices, rows // piece_rows)),
            dma((2, parts)), dma((2,)),
        ],
        compiler_params=pltpu.CompilerParams(
            vmem_limit_bytes=60 * 2**20, collective_id=3, has_side_effects=True
        ),
        name="middle",
    )(mixed, tokens, dz, out_own, out_other, second, norms)


def scene_span(ends_ref, scenes, first, last):
    low = jnp.int32(0)
    high = ends_ref[scenes - 1]
    for scene in range(scenes):
        low = jnp.where(first >= ends_ref[scene], ends_ref[scene], low)
    for scene in reversed(range(scenes)):
        high = jnp.where(last < ends_ref[scene], ends_ref[scene], high)
    return low, high


def scene_inside(ends_ref, scenes, row, position):
    start = jnp.zeros_like(row)
    end = jnp.zeros_like(row)
    before = jnp.int32(0)
    for scene in range(scenes):
        start = jnp.where(row == STAT_ROWS + scene, before, start)
        end = jnp.where(row == STAT_ROWS + scene, ends_ref[scene], end)
        before = ends_ref[scene]
    return (position >= start) & (position < end)


def key_extra(ends_ref, scenes, first, rows):
    row = lax.broadcasted_iota(jnp.int32, (64, rows), 0)
    position = first + lax.broadcasted_iota(jnp.int32, (64, rows), 1)
    inside = scene_inside(ends_ref, scenes, row, position)
    return jnp.where(row < STAT_ROWS, -1.0, jnp.where(inside, 1.0, 0.0)).astype(BF)


def query_extra(ends_ref, scenes, first, rows, stat):
    row = lax.broadcasted_iota(jnp.int32, (64, rows), 0)
    position = first + lax.broadcasted_iota(jnp.int32, (64, rows), 1)
    inside = scene_inside(ends_ref, scenes, row, position)
    is_scene = (row >= STAT_ROWS) & (row < STAT_ROWS + scenes)
    extra = jnp.where(is_scene & jnp.logical_not(inside), neg_large, 0.0)
    if stat is not None:
        extra = stat_rows(row, stat, extra)
    return extra.astype(BF)


def stat_rows(row, stat, extra):
    top = stat.astype(BF).astype(F32)
    middle = (stat - top).astype(BF).astype(F32)
    bottom = stat - top - middle
    extra = jnp.where(row == 0, top, extra)
    extra = jnp.where(row == 1, middle, extra)
    return jnp.where(row == 2, bottom, extra)


def walk_tiles(process, first, count, unit, long_tiles):
    sizes = list(range(1, 9))
    steps = (count + 7) // 8
    if long_tiles:
        sizes += [14, 15]
        steps = jnp.where((count >= 28) & (count <= 30), 2, steps)
        steps = jnp.where((count == 14) | (count == 15), 1, steps)

    def step(index, carry):
        start = lax.div(count * index, steps)
        size = lax.div(count * (index + 1), steps) - start
        offset = pl.multiple_of((first + start) * unit, unit)
        choice = jnp.where(size <= 8, size - 1, size - 6)
        lax.switch(choice, [functools.partial(process, offset, units * unit) for units in sizes])
        return carry

    lax.fori_loop(0, steps, step, 0)


def walk_units(process, state, first, count, unit):
    def step(index, carry):
        return process(pl.multiple_of((first + index) * unit, unit), unit, carry)

    return lax.fori_loop(0, count, step, state)


def forward_kernel(
    ends_ref, me_ref, recv_ref, other_ref, out_ref, lse_ref, keys, values, total_mix, key_top,
    *, scenes, group, total,
):
    block = pl.program_id(0)
    core = me_ref[0]
    sources = recv_ref.shape[0]
    rows = recv_ref.shape[2]

    @pl.when(block == 0)
    def _():
        values[64:80, :] = jnp.ones((16, total), BF)
        key_top[0] = 0.0
        for piece in range(group):
            place = core ^ piece

            def load(source, carry, piece=piece, place=place):
                first = pl.multiple_of((source * group + place) * rows, rows)
                if piece == 0:
                    key = recv_ref[source, 64:128, :]
                    value = recv_ref[source, 128:192, :]
                else:
                    key = other_ref[piece - 1, source, 0:64, :]
                    value = other_ref[piece - 1, source, 64:128, :]
                extra = key_extra(ends_ref, scenes, first, rows)
                keys[pl.ds(first, rows), :] = jnp.concatenate([key, extra], axis=0).T
                values[0:64, pl.ds(first, rows)] = value
                wide = key.astype(F32)
                key_top[0] = jnp.maximum(key_top[0], jnp.max(jnp.sum(wide * wide, axis=0)))
                return carry

            lax.fori_loop(0, sources, load, 0)

    first = (block * group + core) * rows
    low, high = scene_span(ends_ref, scenes, first, first + rows - 1)
    query = recv_ref[block, 0:64, :]
    wide = query.astype(F32)
    query_top = jnp.max(jnp.sum(wide * wide, axis=0))
    query = jnp.concatenate([query, query_extra(ends_ref, scenes, first, rows, None)], axis=0)
    unit = 256
    begin = low // unit
    count = (high + unit - 1) // unit - begin
    safe = query_top * key_top[0] <= SAFE_BOUND * SAFE_BOUND

    def scores_of(offset, size):
        return dot(keys[pl.ds(offset, size), :], query, 1, 0)

    def mix(offset, size, weights):
        return dot(values[:, pl.ds(offset, size)], weights.astype(BF), 1, 0)

    def write(mixed, top):
        summed = mixed[64:65, :]
        out_ref[0] = (mixed[0:64, :] / summed).astype(BF)
        lse_ref[0] = top + jnp.log(summed) * log2_e

    @pl.when(safe)
    def _():
        def process(offset, size):
            total_mix[...] += mix(offset, size, jnp.exp2(scores_of(offset, size)))

        total_mix[...] = jnp.zeros_like(total_mix)
        walk_tiles(process, begin, count, unit, True)
        write(total_mix[...], 0.0)

    @pl.when(jnp.logical_not(safe))
    def _():
        def process(offset, size, carry):
            top, mixed = carry
            scores = scores_of(offset, size)
            new_top = jnp.maximum(top, jnp.max(scores, axis=0, keepdims=True))
            weights = jnp.exp2(scores - new_top)
            return new_top, mixed * jnp.exp2(top - new_top) + mix(offset, size, weights)

        start = (jnp.full((1, rows), neg_large, F32), jnp.zeros((80, rows), F32))
        top, mixed = walk_units(process, start, begin, count, unit)
        write(mixed, top)


def attention_forward(ends, me, recv, other, group):
    sources, _, rows = recv.shape
    total = sources * group * rows
    whole = pl.BlockSpec(memory_space=pltpu.VMEM)
    return pl.pallas_call(
        functools.partial(
            forward_kernel, scenes=ends.shape[0], group=group, total=total
        ),
        grid_spec=pltpu.PrefetchScalarGridSpec(
            num_scalar_prefetch=2,
            grid=(sources,),
            in_specs=[whole, whole],
            out_specs=[
                pl.BlockSpec((1, 64, rows), lambda b, *_: (b, 0, 0)),
                pl.BlockSpec((1, 1, rows), lambda b, *_: (b, 0, 0)),
            ],
            scratch_shapes=[
                pltpu.VMEM((total, 128), BF),
                pltpu.VMEM((80, total), BF),
                pltpu.VMEM((80, rows), F32),
                pltpu.SMEM((1,), F32),
            ],
        ),
        out_shape=[
            jax.ShapeDtypeStruct((sources, 64, rows), BF),
            jax.ShapeDtypeStruct((sources, 1, rows), F32),
        ],
        compiler_params=pltpu.CompilerParams(vmem_limit_bytes=VMEM_BYTES),
        cost_estimate=pl.CostEstimate(
            flops=60 * 10**9, bytes_accessed=8 * 10**6, transcendentals=45 * 10**6
        ),
        name="attention_forward",
    )(ends, me, recv, other)


def backward_kernel(ends_ref, me_ref, recv_ref, others_ref, *refs, scenes, group, parts):
    dout_refs = refs[:parts]
    out_ref, lse_ref, dquery_ref, dkeys_ref = refs[parts : parts + 4]
    queries, douts, queries_flat, douts_flat, dqueries, dkey, dvalue = refs[parts + 4 :]
    block = pl.program_id(0)
    core = me_ref[0]
    sources = recv_ref.shape[0]
    rows = recv_ref.shape[2]
    span = group * rows

    @pl.when(block == 0)
    def _():
        dqueries[...] = jnp.zeros_like(dqueries)

        def load(source, carry):
            first = source * span + core * rows
            at = pl.ds(pl.multiple_of(source * rows, rows), rows)
            query = recv_ref[source, 0:64, :]
            dout = jnp.concatenate([ref[source] for ref in dout_refs], axis=1)
            delta = jnp.sum(
                dout.astype(F32) * out_ref[source].astype(F32), axis=0, keepdims=True
            )
            row = lax.broadcasted_iota(jnp.int32, (64, rows), 0)
            extra = query_extra(ends_ref, scenes, first, rows, lse_ref[source])
            queries[at, :] = jnp.concatenate([query, extra], axis=0).T
            extra = stat_rows(row, delta, jnp.zeros((64, rows), F32)).astype(BF)
            douts[at, :] = jnp.concatenate([dout, extra], axis=0).T
            queries_flat[:, at] = query
            douts_flat[:, at] = dout
            return carry

        lax.fori_loop(0, sources, load, 0)

    source = block // group
    place = block % group
    first = block * rows
    low, high = scene_span(ends_ref, scenes, first, first + rows - 1)
    extra = key_extra(ends_ref, scenes, first, rows)
    own = place == core
    key = jnp.where(own, recv_ref[source, 64:128, :], others_ref[0, 0, 0:64, :])
    value = jnp.where(own, recv_ref[source, 128:192, :], others_ref[0, 0, 64:128, :])
    key_wide = jnp.concatenate([key, extra], axis=0)
    value_wide = jnp.concatenate([value, extra], axis=0)
    key_rows = key_wide.T
    unit = min(256, rows)

    def local(position):
        inside = jnp.clip(lax.rem(position, span) - core * rows, 0, rows)
        return position // span * rows + inside

    begin = local(low) // unit
    count = (local(high) + unit - 1) // unit - begin

    def process(offset, size):
        at = pl.ds(offset, size)
        probs = jnp.exp2(dot(queries[at, :], key_wide, 1, 0))
        dprobs = dot(douts[at, :], value_wide, 1, 0)
        dscores = (probs * dprobs).astype(BF)
        dvalue[...] += dot(douts_flat[:, at], probs.astype(BF), 1, 0)
        dkey[...] += dot(queries_flat[:, at], dscores, 1, 0)
        dqueries[at, :] += dot(dscores, key_rows, 1, 0)

    dkey[...] = jnp.zeros_like(dkey)
    dvalue[...] = jnp.zeros_like(dvalue)
    walk_tiles(process, begin, count, unit, False)
    dkeys_ref[0, 0, 0:64, :] = (dkey[...] * ln_2).astype(BF)
    dkeys_ref[0, 0, 64:128, :] = dvalue[...].astype(BF)

    @pl.when(block == sources * group - 1)
    def _():
        def store(source, carry):
            at = pl.ds(pl.multiple_of(source * rows, rows), rows)
            dquery_ref[source] = (dqueries[at, :].T[0:64, :] * HEAD_DIM**-0.5).astype(BF)
            return carry

        lax.fori_loop(0, sources, store, 0)


def attention_backward(ends, me, recv, others, dout, out, lse, group):
    sources, _, rows = recv.shape
    mine = sources * rows
    whole = pl.BlockSpec(memory_space=pltpu.VMEM)

    def other_map(block, ends_ref, me_ref):
        return (jnp.maximum((block % group) ^ me_ref[0], 1) - 1, block // group, 0, 0)

    def piece_map(block, ends_ref, me_ref):
        return ((block % group) ^ me_ref[0], block // group, 0, 0)

    return pl.pallas_call(
        functools.partial(
            backward_kernel, scenes=ends.shape[0], group=group, parts=len(dout)
        ),
        grid_spec=pltpu.PrefetchScalarGridSpec(
            num_scalar_prefetch=2,
            grid=(sources * group,),
            in_specs=[whole, pl.BlockSpec((1, 1, 128, rows), other_map)] + [whole] * (len(dout) + 2),
            out_specs=[whole, pl.BlockSpec((1, 1, 128, rows), piece_map)],
            scratch_shapes=[
                pltpu.VMEM((mine, 128), BF),
                pltpu.VMEM((mine, 128), BF),
                pltpu.VMEM((64, mine), BF),
                pltpu.VMEM((64, mine), BF),
                pltpu.VMEM((mine, 128), F32),
                pltpu.VMEM((64, rows), F32),
                pltpu.VMEM((64, rows), F32),
            ],
        ),
        out_shape=[
            jax.ShapeDtypeStruct((sources, 64, rows), BF),
            jax.ShapeDtypeStruct((group, sources, 128, rows), BF),
        ],
        compiler_params=pltpu.CompilerParams(vmem_limit_bytes=VMEM_BYTES),
        cost_estimate=pl.CostEstimate(
            flops=150 * 10**9, bytes_accessed=20 * 10**6, transcendentals=45 * 10**6
        ),
        name="attention_backward",
    )(ends, me, recv, others, *dout, out, lse)


def swap_tensor(part):
    return lax.ppermute(part, "tensor", [(0, 1), (1, 0)])


def per_device(
    tokens, scene_lengths, w_query, w_key, w_value, w_out, w_up, w_down,
    norm_gain, norm_bias, cotangent,
):
    own_rows, width = tokens.shape
    devices = lax.axis_size("seq")
    heads = w_query.shape[2] // HEAD_DIM
    columns = heads * HEAD_DIM
    hidden = w_up.shape[2]
    group = devices // heads
    rows = own_rows // group
    me = lax.rem(lax.axis_index("seq"), group).astype(jnp.int32).reshape(1)
    half = lax.axis_index("tensor")
    ends = jnp.cumsum(scene_lengths).astype(jnp.int32)

    recv, others, normed_one, w_first, out_own, norms = project(
        tokens, w_query, w_key, w_value, w_out, norm_gain, norm_bias, devices, group
    )
    out_other = swap_tensor(out_own)
    second_part = jnp.concatenate([w_up[0], w_down[0].T], axis=1)
    recv, second_part = lax.optimization_barrier((recv, second_part))
    second_all = lax.all_gather(second_part, "seq", axis=0, tiled=True)
    def swap_core(part, by):
        return lax.ppermute(part, "seq", [(i, i ^ by) for i in range(devices)])

    if group > 2:
        others = jnp.stack([swap_core(recv[:, HEAD_DIM:, :], by) for by in range(1, group)])
    out_head, lse = attention_forward(ends, me, recv, others, group)

    dout, dmid, mid, z, grads_second, second_norms = middle(
        out_head, tokens, cotangent, out_own, out_other, second_all, norms, devices, group
    )
    z_other = swap_tensor(z)
    grads_second = lax.psum_scatter(grads_second, "seq", scatter_dimension=0, tiled=True)
    grads_second = grads_second.astype(F32)

    dquery, dpieces = attention_backward(ends, me, recv, others, [dout], out_head, lse, group)
    if group > 2:
        dpieces = sum([dpieces[0].astype(F32)] + [
            swap_core(dpieces[by], by).astype(F32) for by in range(1, group)
        ]).astype(BF)[None]
    dstream, last, dquery_w, dkey_w, dvalue_w, dgain, dbias = finish(
        dquery, dpieces, normed_one, w_first, tokens, dmid, mid, z, z_other, norms, second_norms,
        devices, group,
    )
    return (
        last,
        dstream,
        dquery_w,
        dkey_w,
        dvalue_w,
        grads_second[:, :columns].T[None],
        grads_second[:, columns : columns + hidden][None],
        grads_second[:, columns + hidden :].T[None],
        dgain,
        dbias,
    )


def solution(mesh):
    placed = (
        P("seq", None),
        P(),
        P(None, "seq", "tensor"),
        P(None, "seq", "tensor"),
        P(None, "seq", "tensor"),
        P(None, "tensor", "seq"),
        P(None, "seq", "tensor"),
        P(None, "tensor", "seq"),
        P(None, None, "seq"),
        P(None, None, "seq"),
        P("seq", None),
    )
    return jax.shard_map(
        per_device,
        mesh=mesh,
        in_specs=placed,
        out_specs=(
            P("seq", None),
            P("seq", None),
            P(None, "seq", "tensor"),
            P(None, "seq", "tensor"),
            P(None, "seq", "tensor"),
            P(None, "tensor", "seq"),
            P(None, "seq", "tensor"),
            P(None, "tensor", "seq"),
            P(None, None, "seq"),
            P(None, None, "seq"),
        ),
        check_vma=False,
    )
```

```python
import functools

import jax
import jax.numpy as jnp
from jax import lax
from jax.experimental import pallas as pl
from jax.experimental.pallas import tpu as pltpu
from jax.sharding import PartitionSpec as P

HEAD_DIM = 64
SCENE_MAX = 7168
BF = jnp.bfloat16
F32 = jnp.float32
norm_eps = 1e-06
neg_large = -1e30
log2_e = 1.4426950408889634
ln_2 = 0.6931471805599453
STAT_ROWS = 3
SAFE_BOUND = 60.0
VMEM_BYTES = 56 * 2**20


def dot(left, right, left_dim, right_dim):
    return lax.dot_general(
        left, right, (((left_dim,), (right_dim,)), ((), ())), preferred_element_type=F32
    )


def ring_of(devices):
    chips = devices // 2
    index = lax.axis_index("seq")
    core = lax.rem(index, 2)
    chip = index // 2
    if chips != 8:
        return chip, core, lambda place: 2 * place + core
    layer, column = chip // 2, lax.rem(chip, 2)
    place = layer + column * (7 - 2 * layer)

    def seq_index(place):
        side = place // 4
        depth = place + side * (7 - 2 * place)
        return depth * 4 + side * 2 + core

    return place, core, seq_index


def remote_copy(source, target, send_sem, recv_sem, seq):
    return pltpu.make_async_remote_copy(
        src_ref=source, dst_ref=target, send_sem=send_sem, recv_sem=recv_sem,
        device_id={"seq": seq}, device_id_type=pl.DeviceIdType.MESH,
    )


def meet(others):
    barrier = pltpu.get_barrier_semaphore()
    for other in others:
        pl.semaphore_signal(
            barrier, inc=1, device_id=other, device_id_type=pl.DeviceIdType.MESH
        )
    pl.semaphore_wait(barrier, len(others))


def project_kernel(
    tokens_ref, query_ref, key_ref, value_ref, out_ref, gain_ref, bias_ref, up_ref, down_ref,
    recv_ref, others_ref, normed_ref, weights_ref, out_w_ref, norms_ref, second_ref,
    gathered, scaled, sent, send_right, recv_right, send_left, recv_left, send_peer, recv_peer,
    head_send, head_recv, home_sem, core_send, core_recv, out_sem,
    *, devices, group, columns, width,
):
    chips = devices // 2
    depth = width // devices
    rows = tokens_ref.shape[0] // group
    place, core, seq_index = ring_of(devices)
    me = seq_index(place)
    right = seq_index(lax.rem(place + 1, chips))
    left = seq_index(lax.rem(place + chips - 1, chips))
    peer = me + 1 - 2 * core
    heads = columns // HEAD_DIM
    meet([{"seq": lax.rem(me + step, devices)} for step in range(1, devices)])

    def slot(index):
        return gathered.at[pl.ds(pl.multiple_of(index * depth, depth), depth), :]

    mine = pl.ds(pl.multiple_of(me * depth, depth), depth)
    for which, ref in enumerate((query_ref, key_ref, value_ref)):
        gathered[mine, which * columns : (which + 1) * columns] = ref[0]
    norm_rows = jnp.concatenate(
        [gain_ref[0].astype(F32), bias_ref[0].astype(F32), jnp.zeros((124, depth), F32)], axis=0
    )
    gathered[mine, 3 * columns : 4 * columns] = out_ref[...]
    gathered[mine, 4 * columns :] = norm_rows.T.astype(BF)

    to_right, to_left = chips // 2, chips - 1 - chips // 2

    def rightward(step):
        index = seq_index(lax.rem(place - step + chips, chips))
        return remote_copy(
            slot(index), slot(index), send_right.at[step], recv_right.at[step], right
        )

    def leftward(step):
        index = seq_index(lax.rem(place + step, chips))
        return remote_copy(slot(index), slot(index), send_left.at[step], recv_left.at[step], left)

    def across(distance):
        index = seq_index(lax.rem(place + distance + chips, chips))
        return remote_copy(
            slot(index), slot(index),
            send_peer.at[(distance + chips) % chips], recv_peer.at[(distance + chips) % chips], peer,
        )

    def arrive_right(step):
        index = seq_index(lax.rem(place - step - 1 + chips, chips))
        remote_copy(
            slot(index), slot(index), send_right.at[step], recv_right.at[step], right
        ).wait_recv()

    def arrive_left(step):
        index = seq_index(lax.rem(place + step + 1, chips))
        remote_copy(
            slot(index), slot(index), send_left.at[step], recv_left.at[step], left
        ).wait_recv()

    rightward(0).start()
    leftward(0).start()
    across(0).start()

    def normalize(index, carry):
        at = pl.ds(pl.multiple_of(index * 128, 128), 128)
        stream = tokens_ref[at, :].astype(F32)
        centred = stream - jnp.mean(stream, axis=-1, keepdims=True)
        spread = jnp.mean(centred * centred, axis=-1, keepdims=True)
        scaled[at, :] = centred * lax.rsqrt(spread + norm_eps)
        return carry

    lax.fori_loop(0, tokens_ref.shape[0] // 128, normalize, 0)

    hidden = up_ref.shape[2]
    second_ref[:, 0:hidden] = up_ref[0]
    second_ref[:, hidden:] = down_ref[...]
    for step in range(to_right):
        arrive_right(step)
        if step + 1 < to_right:
            rightward(step + 1).start()
        across(-step - 1).start()
        if step < to_left:
            arrive_left(step)
            if step + 1 < to_left:
                leftward(step + 1).start()
            across(step + 1).start()
    for distance in range(chips):
        index = seq_index(lax.rem(place + distance, chips)) + 1 - 2 * core
        remote_copy(
            slot(index), slot(index), send_peer.at[distance], recv_peer.at[distance], peer
        ).wait_recv()

    store = pltpu.make_async_copy(gathered.at[:, : 3 * columns], weights_ref, out_sem.at[0])
    store.start()
    store_out = pltpu.make_async_copy(
        gathered.at[:, 3 * columns : 4 * columns], out_w_ref, out_sem.at[1]
    )
    store_out.start()
    norms = gathered[:, 4 * columns :].astype(F32).T
    norms_ref[...] = norms[0:8]

    def apply_norm(index, carry):
        at = pl.ds(pl.multiple_of(index * 128, 128), 128)
        normed_ref[at, :] = (scaled[at, :] * norms[0:1] + norms[2:3]).astype(BF)
        return carry

    lax.fori_loop(0, tokens_ref.shape[0] // 128, apply_norm, 0)

    def head_copy(step, which):
        where = lax.rem(me + step, devices)
        at = slice(which * HEAD_DIM, (which + 1) * HEAD_DIM)
        return remote_copy(
            sent.at[where, at, :], recv_ref.at[me, at, :], head_send.at[step, which],
            head_recv.at[me, which], where,
        )

    def core_copy(source_ref, source):
        return remote_copy(
            source_ref.at[source, HEAD_DIM:, :], others_ref.at[0, source], core_send.at[source],
            core_recv.at[source], peer,
        )

    home = pltpu.make_async_copy(sent.at[me], recv_ref.at[me], home_sem)
    for which in (1, 2, 0):
        weights = gathered[:, which * columns : (which + 1) * columns].T
        factor = HEAD_DIM**-0.5 * log2_e if which == 0 else 1.0

        def project(core_index, carry, which=which, weights=weights, factor=factor):
            at = pl.ds(pl.multiple_of(core_index * rows, rows), rows)
            result = (dot(weights, normed_ref[at, :], 1, 1) * factor).astype(BF)
            for head in range(heads):
                sent[head * group + core_index, which * HEAD_DIM : (which + 1) * HEAD_DIM, :] = (
                    result[head * HEAD_DIM : (head + 1) * HEAD_DIM, :]
                )
            return carry

        lax.fori_loop(0, group, project, 0)

        def send(step, carry, which=which):
            head_copy(step, which).start()
            return carry

        lax.fori_loop(1, devices, send, 0)
        if which == 2 and group == 2:
            core_copy(sent, me).start()
    home.start()

    def wait_head(step, carry, which):
        source = lax.rem(me - step + devices, devices)
        at = slice(which * HEAD_DIM, (which + 1) * HEAD_DIM)
        remote_copy(
            sent.at[source, at, :], recv_ref.at[source, at, :], head_send.at[0, which],
            head_recv.at[source, which], source,
        ).wait_recv()
        return carry

    def forward(step, carry):
        wait_head(step, carry, 1)
        wait_head(step, carry, 2)
        if group == 2:
            core_copy(recv_ref, lax.rem(me - step + devices, devices)).start()
        return carry

    lax.fori_loop(1, devices, forward, 0)
    lax.fori_loop(1, devices, functools.partial(wait_head, which=0), 0)
    home.wait()

    def finish_core(source, carry):
        core_copy(recv_ref, source).wait()
        return carry

    if group == 2:
        lax.fori_loop(0, devices, finish_core, 0)

    def wait_sent(step, carry):
        for which in range(3):
            head_copy(step, which).wait_send()
        return carry

    lax.fori_loop(1, devices, wait_sent, 0)
    for step in range(to_right):
        rightward(step).wait_send()
    for step in range(to_left):
        leftward(step).wait_send()
    for distance in range(chips):
        across(distance).wait_send()
    store.wait()
    store_out.wait()


def project(
    tokens, w_query, w_key, w_value, w_out, norm_gain, norm_bias, w_up, w_down, devices, group
):
    own_rows, width = tokens.shape
    columns = w_query.shape[2]
    chips = devices // 2
    rows = own_rows // group
    whole = pl.BlockSpec(memory_space=pltpu.VMEM)
    far = pl.BlockSpec(memory_space=pl.ANY)
    dma = pltpu.SemaphoreType.DMA
    return pl.pallas_call(
        functools.partial(
            project_kernel, devices=devices, group=group, columns=columns, width=width
        ),
        in_specs=[whole] * 9,
        out_specs=[far, far, whole, far, far, whole, whole],
        out_shape=[
            jax.ShapeDtypeStruct((devices, 3 * HEAD_DIM, rows), BF),
            jax.ShapeDtypeStruct((1, devices, 2 * HEAD_DIM, rows), BF),
            jax.ShapeDtypeStruct((own_rows, width), BF),
            jax.ShapeDtypeStruct((width, 3 * columns), BF),
            jax.ShapeDtypeStruct((width, columns), BF),
            jax.ShapeDtypeStruct((8, width), F32),
            jax.ShapeDtypeStruct((width // devices, 2 * w_up.shape[2]), BF),
        ],
        scratch_shapes=[
            pltpu.VMEM((width, 4 * columns + 128), BF),
            pltpu.VMEM((own_rows, width), F32),
            pltpu.VMEM((devices, 3 * HEAD_DIM, rows), BF),
            dma((chips // 2,)), dma((chips // 2,)),
            dma((chips // 2,)), dma((chips // 2,)),
            dma((chips,)), dma((chips,)),
            dma((devices, 3)), dma((devices, 3)), dma,
            dma((devices,)), dma((devices,)),
            dma((2,)),
        ],
        compiler_params=pltpu.CompilerParams(
            vmem_limit_bytes=VMEM_BYTES, collective_id=1, has_side_effects=True
        ),
        name="project",
    )(tokens, w_query, w_key, w_value, w_out[0].T, norm_gain, norm_bias, w_up, w_down[0].T)


def finish_kernel(
    dquery_ref, dpieces_far, normed_far, weights_far, tokens_far, dmid_far, mid_far, z_far,
    z_other_far, norms_ref, second_ref,
    dstream_far, last_far, dquery_w_ref, dkey_w_ref, dvalue_w_ref, dgain_ref, dbias_ref,
    normed, weights, tokens, dmid, mid, z, z_other, own_piece,
    core_got, sent, got, flat, partial_sent, partial_got, summed_grads, partial, from_peer,
    ring_first, ring, total, few_sent, few_got,
    load_sem, store_sem, core_send, core_recv, head_send, head_recv, x_send, x_recv,
    peer_send, peer_recv, ring_send, ring_recv, few_send, few_recv,
    *, devices, group, cores, columns, width,
):
    chips = devices // 2
    depth = width // devices
    own_rows = tokens.shape[0]
    rows = own_rows // group
    heads = columns // HEAD_DIM
    wide = 3 * columns + 128
    lanes = 128
    lines_wide = wide // lanes
    cuts = [(lines_wide * turn + 3) // 4 * lanes for turn in range(5)]
    chunks = rows // lanes
    place, core, seq_index = ring_of(devices)
    me = seq_index(place)
    right = {"seq": seq_index(lax.rem(place + 1, chips))}
    left = {"seq": seq_index(lax.rem(place + chips - 1, chips))}
    peer = {"seq": me + 1 - 2 * core}
    across = {"tensor": 1 - lax.axis_index("tensor")}
    group_place = lax.rem(me, group)

    loads = {}
    for number, (name, far, near) in enumerate((
        ("piece", dpieces_far.at[0], own_piece), ("tokens", tokens_far, tokens), ("weights", weights_far, weights),
        ("normed", normed_far, normed), ("z", z_far, z), ("z_other", z_other_far, z_other),
        ("mid", mid_far, mid), ("dmid", dmid_far, dmid),
    )):
        loads[name] = pltpu.make_async_copy(far, near, load_sem.at[number])
        loads[name].start()

    barrier = pltpu.get_barrier_semaphore()
    for step in range(1, devices):
        pl.semaphore_signal(
            barrier, inc=1, device_id={"seq": lax.rem(me + step, devices)},
            device_id_type=pl.DeviceIdType.MESH,
        )
    pl.semaphore_signal(barrier, inc=1, device_id=across, device_id_type=pl.DeviceIdType.MESH)
    pl.semaphore_wait(barrier, devices)

    def copy_to(source, target, send_sem, recv_sem, where):
        return pltpu.make_async_remote_copy(
            src_ref=source, dst_ref=target, send_sem=send_sem, recv_sem=recv_sem,
            device_id=where, device_id_type=pl.DeviceIdType.MESH,
        )

    def core_copy(by, chunk):
        other = jnp.int32(0)
        bit = 1
        while bit < group:
            mine = lax.rem(group_place // bit, 2)
            other = other + bit * ((1 - mine) if by & bit else mine)
            bit *= 2
        at = slice(chunk * lanes, (chunk + 1) * lanes)
        return copy_to(
            dpieces_far.at[by, :, :, at], core_got.at[by - 1, :, :, at],
            core_send.at[by - 1, chunk], core_recv.at[by - 1, chunk],
            {"seq": me - group_place + other},
        )

    def head_copy(step, chunk):
        where = lax.rem(me + step, devices)
        at = slice(chunk * lanes, (chunk + 1) * lanes)
        return copy_to(
            sent.at[where, :, at], got.at[me, :, at],
            head_send.at[step, chunk], head_recv.at[me, chunk], {"seq": where},
        )

    for chunk in range(chunks):
        for by in range(1, cores):
            core_copy(by, chunk).start()
    loads["piece"].wait()
    for chunk in range(chunks):
        at = slice(chunk * lanes, (chunk + 1) * lanes)
        for by in range(1, cores):
            core_copy(by, chunk).wait_recv()

        def gather(index, carry, at=at):
            piece = own_piece[index, :, at].astype(F32)
            for by in range(1, cores):
                piece = piece + core_got[by - 1, index, :, at].astype(F32)
            sent[index, HEAD_DIM:, at] = piece.astype(BF)
            sent[index, 0:HEAD_DIM, at] = dquery_ref[index, :, at]
            return carry

        lax.fori_loop(0, devices, gather, 0)

        def send(step, carry, chunk=chunk):
            head_copy(step, chunk).start()
            return carry

        lax.fori_loop(1, devices, send, 0)

    loads["z"].wait()
    loads["z_other"].wait()
    loads["mid"].wait()

    def add_last(index, carry):
        at = pl.ds(pl.multiple_of(index * lanes, lanes), lanes)
        both = z[at, :].astype(F32) + z_other[at, :].astype(F32)
        z[at, :] = (mid[at, :] + both).astype(BF)
        return carry

    lax.fori_loop(0, own_rows // lanes, add_last, 0)
    store_last = pltpu.make_async_copy(z, last_far, store_sem.at[0])
    store_last.start()
    for name in ("tokens", "weights", "normed", "dmid"):
        loads[name].wait()

    def part_rows(place_in_group, chunk):
        return slice(place_in_group * rows + chunk * lanes, place_in_group * rows + (chunk + 1) * lanes)

    def x_copy(place_in_group, chunk):
        at = part_rows(place_in_group, chunk)
        number = place_in_group * chunks + chunk
        return copy_to(
            partial_sent.at[at, :], partial_got.at[at, :], x_send.at[number], x_recv.at[number],
            across,
        )

    def unit_rows(at):
        stream = tokens[at, :].astype(F32)
        centred = stream - jnp.mean(stream, axis=-1, keepdims=True)
        spread = jnp.mean(centred * centred, axis=-1, keepdims=True)
        inverse = lax.rsqrt(spread + norm_eps)
        return centred * inverse, inverse

    def finish_norm(chunk):
        for place_in_group in range(group):
            at = part_rows(place_in_group, chunk)
            x_copy(place_in_group, chunk).wait_recv()
            dnormed = partial_sent[at, :].astype(F32) + partial_got[at, :].astype(F32)
            unit, inverse = unit_rows(at)
            dunit = dnormed * norms_ref[0:1, :]
            mean = jnp.mean(dunit, axis=-1, keepdims=True)
            along = jnp.mean(dunit * unit, axis=-1, keepdims=True)
            dmid[at, :] = dmid[at, :] + (dunit - mean - unit * along) * inverse

    gain_sum = jnp.zeros((1, width), F32)
    bias_sum = jnp.zeros((1, width), F32)
    lines = 256
    for chunk in range(chunks):
        at = slice(chunk * lanes, (chunk + 1) * lanes)

        def flatten(index, carry, chunk=chunk, at=at):
            head = index // group
            start = lax.rem(index, group) * rows + chunk * lanes
            to_rows = pl.ds(pl.multiple_of(start, lanes), lanes)

            def put(source):
                for which in range(3):
                    to = pl.ds(
                        pl.multiple_of(which * columns + head * HEAD_DIM, HEAD_DIM), HEAD_DIM
                    )
                    flat[to, to_rows] = source[index, which * HEAD_DIM : (which + 1) * HEAD_DIM, at]

            @pl.when(index == me)
            def _():
                put(sent)

            @pl.when(index != me)
            def _():
                copy_to(
                    sent.at[index, :, at], got.at[index, :, at],
                    head_send.at[0, chunk], head_recv.at[index, chunk], {"seq": index},
                ).wait_recv()
                put(got)

            return carry

        lax.fori_loop(0, devices, flatten, 0)
        ats = [part_rows(place_in_group, chunk) for place_in_group in range(group)]
        flat_chunk = jnp.concatenate([flat[:, part] for part in ats], axis=1)

        def sum_grads():
            normed_t = jnp.concatenate([normed[part, :] for part in ats], axis=0).T
            for line in range(width // lines):
                here = slice(line * lines, (line + 1) * lines)
                result = dot(normed_t[here, :], flat_chunk, 1, 1)
                if chunk > 0:
                    result = result + summed_grads[here, :]
                if chunk + 1 < chunks:
                    summed_grads[here, :] = result
                else:
                    partial[here, 0 : 3 * columns] = result.astype(BF)

        def send_dnormed(gain_sum, bias_sum):
            result = dot(flat_chunk.T, weights[...], 1, 1)
            for place_in_group in range(group):
                here = slice(place_in_group * lanes, (place_in_group + 1) * lanes)
                partial_sent[ats[place_in_group], :] = result[here, :].astype(BF)
                x_copy(place_in_group, chunk).start()
            if chunk + 1 == chunks:
                sum_grads()
            for place_in_group in range(group):
                here = slice(place_in_group * lanes, (place_in_group + 1) * lanes)
                unit, _ = unit_rows(ats[place_in_group])
                gain_sum = gain_sum + jnp.sum(result[here, :] * unit, axis=0, keepdims=True)
                bias_sum = bias_sum + jnp.sum(result[here, :], axis=0, keepdims=True)
            return gain_sum, bias_sum

        gain_sum, bias_sum = send_dnormed(gain_sum, bias_sum)
        if chunk + 1 < chunks:
            sum_grads()
        if chunk > 0 and chunk + 1 < chunks:
            finish_norm(chunk - 1)

    norm_rows = jnp.concatenate(
        [
            gain_sum, second_ref[0:1, :] * 0.5, bias_sum, second_ref[1:2, :] * 0.5,
            jnp.zeros((124, width), F32),
        ],
        axis=0,
    )
    partial[:, 3 * columns :] = norm_rows.T.astype(BF)

    order = []
    for step in range(chips // 2):
        for offset in (-step - 1, step + 1):
            if offset % chips not in order:
                order.append(offset % chips)
    order.append(0)

    def peer_copy(number):
        where = lax.rem(place + order[number], chips)
        theirs = seq_index(where) + 1 - 2 * core
        return copy_to(
            partial.at[pl.ds(pl.multiple_of(theirs * depth, depth), depth), :],
            from_peer.at[pl.ds(pl.multiple_of(where * depth, depth), depth), :],
            peer_send.at[number], peer_recv.at[number], peer,
        )

    for number in range(chips):
        peer_copy(number).start()

    waited = []

    def chip_block(offset, low, high):
        number = order.index(offset % chips)
        if number not in waited:
            peer_copy(number).wait_recv()
            waited.append(number)
        where = lax.rem(place + offset % chips, chips)
        own = pl.ds(pl.multiple_of(seq_index(where) * depth, depth), depth)
        there = pl.ds(pl.multiple_of(where * depth, depth), depth)
        return partial[own, low:high].astype(F32) + from_peer[there, low:high].astype(F32)

    steps = chips - 1

    rings = [(True, 0), (False, 2), (True, 1), (False, 3)]

    def ring_copy(step, toward_right, turn):
        low, high = cuts[turn], cuts[turn + 1]
        source = ring_first.at[:, low:high] if step == 0 else ring.at[step - 1, :, low:high]
        return copy_to(
            source, ring.at[step, :, low:high], ring_send.at[turn, step], ring_recv.at[turn, step],
            right if toward_right else left,
        )

    for toward_right, turn in rings:
        low, high = cuts[turn], cuts[turn + 1]
        ring_first[:, low:high] = chip_block(-1 if toward_right else 1, low, high).astype(BF)
        ring_copy(0, toward_right, turn).start()
    pending = list(range(max(chunks - 2, 0), chunks))
    for step in range(steps):
        if pending and step in (1, steps // 2):
            finish_norm(pending.pop(0))
        for toward_right, turn in rings:
            low, high = cuts[turn], cuts[turn + 1]
            ring_copy(step, toward_right, turn).wait_recv()
            offset = -step - 2 if toward_right else step + 2
            summed = ring[step, :, low:high].astype(F32) + chip_block(offset, low, high)
            if step + 1 < steps:
                ring[step, :, low:high] = summed.astype(BF)
                ring_copy(step + 1, toward_right, turn).start()
            else:
                total[:, low:high] = summed
    few_sent[...] = total[:, 3 * columns :]
    few = copy_to(few_sent, few_got, few_send, few_recv, across)
    few.start()
    for chunk in pending:
        finish_norm(chunk)
    store_stream = pltpu.make_async_copy(dmid, dstream_far, store_sem.at[1])
    store_stream.start()
    dquery_w_ref[0] = total[:, 0:columns]
    dkey_w_ref[0] = total[:, columns : 2 * columns]
    dvalue_w_ref[0] = total[:, 2 * columns : 3 * columns]
    few.wait()
    norm_rows = (few_sent[...] + few_got[...]).T
    dgain_ref[0] = norm_rows[0:2, :]
    dbias_ref[0] = norm_rows[2:4, :]
    for chunk in range(chunks):
        for by in range(1, cores):
            core_copy(by, chunk).wait_send()
        for place_in_group in range(group):
            x_copy(place_in_group, chunk).wait_send()

        def wait_head(step, carry, chunk=chunk):
            head_copy(step, chunk).wait_send()
            return carry

        lax.fori_loop(1, devices, wait_head, 0)
    for number in range(chips):
        peer_copy(number).wait_send()
    for step in range(steps):
        for toward_right, turn in rings:
            ring_copy(step, toward_right, turn).wait_send()
    store_last.wait()
    store_stream.wait()


def finish(
    dquery, dpieces, normed, weights, tokens, dmid, mid, z, z_other, norms, second, devices, group
):
    own_rows, width = tokens.shape
    cores, _, _, rows = dpieces.shape
    columns = weights.shape[1] // 3
    chips = devices // 2
    depth = width // devices
    wide = 3 * columns + 128
    steps = chips - 1
    chunks = rows // 128
    whole = pl.BlockSpec(memory_space=pltpu.VMEM)
    far = pl.BlockSpec(memory_space=pl.ANY)
    dma = pltpu.SemaphoreType.DMA
    vmem = pltpu.VMEM
    return pl.pallas_call(
        functools.partial(
            finish_kernel, devices=devices, group=group, cores=cores, columns=columns, width=width
        ),
        in_specs=[whole] + [far] * 8 + [whole] * 2,
        out_specs=[far] * 2 + [whole] * 5,
        out_shape=[
            jax.ShapeDtypeStruct((own_rows, width), F32),
            jax.ShapeDtypeStruct((own_rows, width), BF),
        ]
        + [jax.ShapeDtypeStruct((1, depth, columns), F32)] * 3
        + [jax.ShapeDtypeStruct((1, 2, depth), F32)] * 2,
        scratch_shapes=[
            vmem((own_rows, width), BF), vmem((width, 3 * columns), BF),
            vmem((own_rows, width), BF), vmem((own_rows, width), F32),
            vmem((own_rows, width), F32), vmem((own_rows, width), BF),
            vmem((own_rows, width), BF), vmem((devices, 128, rows), BF),
            vmem((max(cores - 1, 1), devices, 128, rows), BF),
            vmem((devices, 3 * HEAD_DIM, rows), BF), vmem((devices, 3 * HEAD_DIM, rows), BF),
            vmem((3 * columns, own_rows), BF),
            vmem((own_rows, width), BF), vmem((own_rows, width), BF),
            vmem((width, 3 * columns), F32), vmem((width, wide), BF),
            vmem((chips * depth, wide), BF),
            vmem((depth, wide), BF), vmem((steps, depth, wide), BF),
            vmem((depth, wide), F32),
            vmem((depth, 128), F32), vmem((depth, 128), F32),
            dma((8,)), dma((2,)),
            dma((max(cores - 1, 1), chunks)), dma((max(cores - 1, 1), chunks)),
            dma((devices, chunks)), dma((devices, chunks)),
            dma((group * chunks,)), dma((group * chunks,)),
            dma((chips,)), dma((chips,)),
            dma((4, steps)), dma((4, steps)),
            dma, dma,
        ],
        compiler_params=pltpu.CompilerParams(
            vmem_limit_bytes=60 * 2**20, collective_id=2, has_side_effects=True
        ),
        name="finish",
    )(dquery, dpieces, normed, weights, tokens, dmid, mid, z, z_other, norms, second)


def middle_kernel(
    mixed_far, tokens_ref, dz_ref, out_own_ref, out_other_ref, second_ref, norms_ref,
    dout_ref, dmid_ref, mid_ref, z_ref, grads_ref, norm_grads_ref,
    weights, tokens, dz, flat, flat_other, normed, act, dup, mid, dmid, dsent, dgot, dy, z,
    out_t, dout, stage,
    load_sem, mixed_send, mixed_recv, flat_send, flat_recv, x_send, x_recv, head_send, head_recv, store_sem, stage_sem,
    *, devices, group, columns, hidden,
):
    own_rows, width = tokens.shape
    rows = own_rows // group
    heads = columns // HEAD_DIM
    parts = x_send.shape[0]
    part_rows = own_rows // parts
    block = 512
    me = lax.axis_index("seq").astype(jnp.int32)
    core = lax.rem(me, group)
    half = lax.axis_index("tensor").astype(jnp.int32)
    across = {"tensor": 1 - half}

    own_cut = pl.ds(pl.multiple_of(half * columns, columns), columns)
    other_cut = pl.ds(pl.multiple_of((1 - half) * columns, columns), columns)
    loads = [
        pltpu.make_async_copy(out_own_ref, weights.at[:, own_cut], load_sem.at[0]),
        pltpu.make_async_copy(tokens_ref, tokens, load_sem.at[1]),
        pltpu.make_async_copy(second_ref, weights.at[:, width:], load_sem.at[2]),
        pltpu.make_async_copy(dz_ref, dz, load_sem.at[3]),
        pltpu.make_async_copy(out_other_ref, weights.at[:, other_cut], load_sem.at[4]),
    ]
    for load in loads:
        load.start()

    barrier = pltpu.get_barrier_semaphore()
    for other in range(devices):
        @pl.when(me != other)
        def _(other=other):
            pl.semaphore_signal(
                barrier, inc=1, device_id={"seq": other}, device_id_type=pl.DeviceIdType.MESH
            )

    pl.semaphore_signal(
        barrier, inc=1, device_id=across, device_id_type=pl.DeviceIdType.MESH
    )
    pl.semaphore_wait(barrier, devices)

    def copy_to(source, target, send_sem, recv_sem, where):
        return pltpu.make_async_remote_copy(
            src_ref=source, dst_ref=target, send_sem=send_sem, recv_sem=recv_sem,
            device_id=where, device_id_type=pl.DeviceIdType.MESH,
        )

    def rows_of(part):
        return pl.ds(pl.multiple_of(part * part_rows, part_rows), part_rows)

    piece_rows = min(part_rows, rows)
    pieces = rows // piece_rows
    my_head = me // group

    def mixed_copy(step, piece):
        where = lax.rem(me + step, devices)
        cut = slice(piece * piece_rows, (piece + 1) * piece_rows)
        to = pl.ds(pl.multiple_of(core * rows + piece * piece_rows, piece_rows), piece_rows)
        return copy_to(
            mixed_far.at[where, :, cut],
            flat.at[pl.ds(pl.multiple_of(my_head * HEAD_DIM, HEAD_DIM), HEAD_DIM), to],
            mixed_send.at[step, piece], mixed_recv.at[me, piece], {"seq": where},
        )

    def mixed_home(piece):
        cut = slice(piece * piece_rows, (piece + 1) * piece_rows)
        to = pl.ds(pl.multiple_of(core * rows + piece * piece_rows, piece_rows), piece_rows)
        return pltpu.make_async_copy(
            mixed_far.at[me, :, cut],
            flat.at[pl.ds(pl.multiple_of(my_head * HEAD_DIM, HEAD_DIM), HEAD_DIM), to],
            mixed_send.at[0, piece],
        )

    for piece in range(pieces):
        mixed_home(piece).start()

        def send_mixed(step, carry, piece=piece):
            mixed_copy(step, piece).start()
            return carry

        lax.fori_loop(1, devices, send_mixed, 0)

    def wait_mixed(place, piece):
        to = pl.ds(place * rows + piece * piece_rows, piece_rows)

        def one(head, carry):
            source = head * group + place
            at = pl.ds(pl.multiple_of(head * HEAD_DIM, HEAD_DIM), HEAD_DIM)

            @pl.when(source != me)
            def _():
                copy_to(
                    flat.at[at, to], flat.at[at, to], mixed_send.at[0, piece],
                    mixed_recv.at[source, piece], {"seq": source},
                ).wait_recv()

            return carry

        lax.fori_loop(0, heads, one, 0)

    def flat_copy(part):
        at = rows_of(part)
        return copy_to(
            flat.at[:, at], flat_other.at[:, at], flat_send.at[part], flat_recv.at[part], across
        )

    def x_copy(part):
        at = rows_of(part)
        return copy_to(dsent.at[at, :], dgot.at[at, :], x_send.at[part], x_recv.at[part], across)

    span = part_rows // piece_rows
    turns = [
        (place * rows + piece * piece_rows) // part_rows
        for piece in range(pieces) for place in range(0, group, span)
    ]
    for piece in range(pieces):
        mixed_home(piece).wait()
    for turn, part in enumerate(turns):
        for place in range(group):
            for piece in range(pieces):
                if (place * rows + piece * piece_rows) // part_rows == part:
                    wait_mixed(place, piece)
        flat_copy(part).start()
    loads[0].wait()
    out_t[...] = weights[:, own_cut].T
    for load in loads[1:]:
        load.wait()
    first_half = half == 0

    def unit_rows(at):
        stream = mid[at, :]
        centred = stream - jnp.mean(stream, axis=-1, keepdims=True)
        spread = jnp.mean(centred * centred, axis=-1, keepdims=True)
        inverse = lax.rsqrt(spread + norm_eps)
        return centred * inverse, inverse

    def store_mid(part):
        at = rows_of(part)
        return pltpu.make_async_copy(mid.at[at, :], mid_ref.at[at, :], store_sem.at[0, part])

    def forward(part, carry):
        at = rows_of(part)
        flat_copy(part).wait_recv()
        own, other = flat[:, at], flat_other[:, at]
        low = jnp.where(first_half, own, other).T
        high = jnp.where(first_half, other, own).T
        projected = dot(low, weights[:, 0:columns], 1, 1) + dot(
            high, weights[:, columns:width], 1, 1
        )
        mid[at, :] = tokens[at, :].astype(F32) + projected
        store_mid(part).start()
        unit, _ = unit_rows(at)
        normed[at, :] = (unit * norms_ref[1:2, :] + norms_ref[3:4, :]).astype(BF)

        def hidden_block(index, total):
            cut = pl.ds(pl.multiple_of(index * block, block), block)
            up_cut = pl.ds(pl.multiple_of(width + index * block, block), block)
            down_cut = pl.ds(pl.multiple_of(width + hidden + index * block, block), block)
            up_w = weights[:, up_cut]
            up = dot(normed[at, :], up_w, 1, 0)
            dact = dot(dz[at, :], weights[:, down_cut], 1, 0)
            square = up * up
            bend = jnp.tanh(0.7978845608028654 * up * (1.0 + 0.044715 * square))
            grow = 0.5 + 0.5 * bend
            slope = grow + 0.5 * up * (1.0 - bend * bend) * (
                0.7978845608028654 + 0.10703222440890037 * square
            )
            act[at, cut] = (up * grow).astype(BF)
            dup_block = (dact * slope).astype(BF)
            dup[at, cut] = dup_block
            return total + dot(dup_block, up_w, 1, 1)

        total = lax.fori_loop(
            0, hidden // block, hidden_block, jnp.zeros((part_rows, width), F32)
        )
        dsent[at, :] = total.astype(BF)
        x_copy(part).start()
        return carry

    def forward_turn(turn, carry):
        return forward(lax.rem(turn, group) * (parts // group) + turn // group, carry)

    lax.fori_loop(0, parts, forward_turn if pieces > 1 else forward, 0)

    def head_copies(piece, head):
        start = piece * piece_rows
        owner = head * group + start // rows
        slot = lax.rem(piece, pieces)
        source = dout.at[
            pl.ds(pl.multiple_of(head * HEAD_DIM, HEAD_DIM), HEAD_DIM),
            pl.ds(pl.multiple_of(start, piece_rows), piece_rows),
        ]
        target = dout_ref.at[me, :, pl.ds(pl.multiple_of(slot * piece_rows, piece_rows), piece_rows)]
        away = copy_to(
            source, target, head_send.at[head, piece], head_recv.at[me, slot], {"seq": owner}
        )
        home = pltpu.make_async_copy(source, target, head_send.at[head, piece])
        return away, home, owner == me

    def send_heads(part):
        def send(index, carry):
            piece = part * (part_rows // piece_rows) + index // heads
            away, home, is_home = head_copies(piece, lax.rem(index, heads))

            @pl.when(is_home)
            def _():
                home.start()

            @pl.when(jnp.logical_not(is_home))
            def _():
                away.start()

            return carry

        lax.fori_loop(0, heads * (part_rows // piece_rows), send, 0)

    def store_dmid(part):
        at = rows_of(part)
        return pltpu.make_async_copy(dmid.at[at, :], dmid_ref.at[at, :], store_sem.at[1, part])

    def backward(part, sums):
        gain_sum, bias_sum = sums
        at = rows_of(part)
        x_copy(part).wait_recv()
        dnormed = dsent[at, :].astype(F32) + dgot[at, :].astype(F32)
        unit, inverse = unit_rows(at)
        dunit = dnormed * norms_ref[1:2, :]
        mean = jnp.mean(dunit, axis=-1, keepdims=True)
        along = jnp.mean(dunit * unit, axis=-1, keepdims=True)
        result = dz[at, :].astype(F32) + (dunit - mean - unit * along) * inverse
        dmid[at, :] = result
        store_dmid(part).start()
        low = result.astype(BF)
        dy[at, :] = low
        dout[:, at] = dot(out_t[...], low, 1, 1).astype(BF)
        send_heads(part)
        gain_sum = gain_sum + jnp.sum(dnormed * unit, axis=0, keepdims=True)
        bias_sum = bias_sum + jnp.sum(dnormed, axis=0, keepdims=True)
        return gain_sum, bias_sum

    def last_product(part, carry):
        at = rows_of(part)
        z[at, :] = dot(act[at, :], weights[:, width + hidden :], 1, 1).astype(BF)
        return carry

    lax.fori_loop(0, parts, last_product, 0)
    store_z = pltpu.make_async_copy(z, z_ref, load_sem.at[0])
    store_z.start()

    def grads_into(left_t, right_ref, first_column):
        blocks = right_ref.shape[1] // block

        def store(index, slot):
            cut = pl.ds(pl.multiple_of(first_column + index * block, block), block)
            return pltpu.make_async_copy(stage.at[slot], grads_ref.at[:, cut], stage_sem.at[slot])

        def one(index, carry):
            slot = lax.rem(index, 2)

            @pl.when(index >= 2)
            def _():
                store(index - 2, slot).wait()

            cut = pl.ds(pl.multiple_of(index * block, block), block)
            stage[slot] = dot(left_t, right_ref[:, cut], 1, 0).astype(BF)
            store(index, slot).start()
            return carry

        lax.fori_loop(0, blocks, one, 0)
        for index in range(blocks - 2, blocks):
            store(index, index % 2).wait()

    sums = (jnp.zeros((1, width), F32), jnp.zeros((1, width), F32))
    sums = backward(turns[0], sums)
    grads_into(normed[...].T, dup, columns)
    sums = backward(turns[1], sums)
    grads_into(dz[...].T, act, columns + hidden)
    for part in turns[2:]:
        sums = backward(part, sums)
    stage[0] = dot(dy[...].T, flat[...], 1, 1).astype(BF)
    store_out = pltpu.make_async_copy(stage.at[0], grads_ref.at[:, 0:columns], stage_sem.at[0])
    store_out.start()
    norm_grads_ref[...] = jnp.concatenate([*sums, jnp.zeros((6, width), F32)], axis=0)

    def wait_sent(index, carry):
        away, home, is_home = head_copies(index // heads, lax.rem(index, heads))

        @pl.when(is_home)
        def _():
            home.wait()

        @pl.when(jnp.logical_not(is_home))
        def _():
            away.wait_send()

        return carry

    lax.fori_loop(0, heads * (own_rows // piece_rows), wait_sent, 0)

    def wait_heads(index, carry):
        source = index // pieces
        slot = lax.rem(index, pieces)
        cut = pl.ds(pl.multiple_of(slot * piece_rows, piece_rows), piece_rows)

        @pl.when(source != me)
        def _():
            copy_to(
                dout.at[0:HEAD_DIM, 0:piece_rows], dout_ref.at[source, :, cut],
                head_send.at[0, 0], head_recv.at[source, slot], {"seq": source},
            ).wait_recv()

        return carry

    lax.fori_loop(0, devices * pieces, wait_heads, 0)
    for piece in range(pieces):
        def sent_mixed(step, carry, piece=piece):
            mixed_copy(step, piece).wait_send()
            return carry

        lax.fori_loop(1, devices, sent_mixed, 0)
    for part in range(parts):
        flat_copy(part).wait_send()
        x_copy(part).wait_send()
        store_mid(part).wait()
        store_dmid(part).wait()
    store_z.wait()
    store_out.wait()


def middle(mixed, tokens, dz, out_own, out_other, second, norms, devices, group):
    own_rows, width = tokens.shape
    rows = own_rows // group
    columns = out_own.shape[1]
    hidden = second.shape[1] // 2
    parts = 4
    piece_rows = min(own_rows // parts, rows)
    whole = pl.BlockSpec(memory_space=pltpu.VMEM)
    far = pl.BlockSpec(memory_space=pl.ANY)
    dma = pltpu.SemaphoreType.DMA
    vmem = pltpu.VMEM
    return pl.pallas_call(
        functools.partial(
            middle_kernel, devices=devices, group=group, columns=columns, hidden=hidden
        ),
        in_specs=[far] * 6 + [whole],
        out_specs=[far] * 5 + [whole],
        out_shape=[
            jax.ShapeDtypeStruct((devices, HEAD_DIM, rows), BF),
            jax.ShapeDtypeStruct((own_rows, width), F32),
            jax.ShapeDtypeStruct((own_rows, width), F32),
            jax.ShapeDtypeStruct((own_rows, width), BF),
            jax.ShapeDtypeStruct((width, columns + 2 * hidden), BF),
            jax.ShapeDtypeStruct((8, width), F32),
        ],
        scratch_shapes=[
            vmem((width, width + 2 * hidden), BF),
            vmem((own_rows, width), BF), vmem((own_rows, width), BF),
            vmem((columns, own_rows), BF), vmem((columns, own_rows), BF),
            vmem((own_rows, width), BF),
            vmem((own_rows, hidden), BF), vmem((own_rows, hidden), BF),
            vmem((own_rows, width), F32), vmem((own_rows, width), F32),
            vmem((own_rows, width), BF), vmem((own_rows, width), BF),
            vmem((own_rows, width), BF), vmem((own_rows, width), BF),
            vmem((columns, width), BF), vmem((columns, own_rows), BF),
            vmem((2, width, 512), BF),
            dma((5,)), dma((devices, rows // piece_rows)), dma((devices, rows // piece_rows)),
            dma((parts,)), dma((parts,)), dma((parts,)), dma((parts,)),
            dma((columns // HEAD_DIM, own_rows // piece_rows)),
            dma((devices, rows // piece_rows)),
            dma((2, parts)), dma((2,)),
        ],
        compiler_params=pltpu.CompilerParams(
            vmem_limit_bytes=60 * 2**20, collective_id=3, has_side_effects=True
        ),
        name="middle",
    )(mixed, tokens, dz, out_own, out_other, second, norms)


def scene_span(ends_ref, scenes, first, last):
    low = jnp.int32(0)
    high = ends_ref[scenes - 1]
    for scene in range(scenes):
        low = jnp.where(first >= ends_ref[scene], ends_ref[scene], low)
    for scene in reversed(range(scenes)):
        high = jnp.where(last < ends_ref[scene], ends_ref[scene], high)
    return low, high


def scene_inside(ends_ref, scenes, row, position):
    start = jnp.zeros_like(row)
    end = jnp.zeros_like(row)
    before = jnp.int32(0)
    for scene in range(scenes):
        start = jnp.where(row == STAT_ROWS + scene, before, start)
        end = jnp.where(row == STAT_ROWS + scene, ends_ref[scene], end)
        before = ends_ref[scene]
    return (position >= start) & (position < end)


def key_extra(ends_ref, scenes, first, rows):
    row = lax.broadcasted_iota(jnp.int32, (64, rows), 0)
    position = first + lax.broadcasted_iota(jnp.int32, (64, rows), 1)
    inside = scene_inside(ends_ref, scenes, row, position)
    return jnp.where(row < STAT_ROWS, -1.0, jnp.where(inside, 1.0, 0.0)).astype(BF)


def query_extra(ends_ref, scenes, first, rows, stat):
    row = lax.broadcasted_iota(jnp.int32, (64, rows), 0)
    position = first + lax.broadcasted_iota(jnp.int32, (64, rows), 1)
    inside = scene_inside(ends_ref, scenes, row, position)
    is_scene = (row >= STAT_ROWS) & (row < STAT_ROWS + scenes)
    extra = jnp.where(is_scene & jnp.logical_not(inside), neg_large, 0.0)
    if stat is not None:
        extra = stat_rows(row, stat, extra)
    return extra.astype(BF)


def stat_rows(row, stat, extra):
    top = stat.astype(BF).astype(F32)
    middle = (stat - top).astype(BF).astype(F32)
    bottom = stat - top - middle
    extra = jnp.where(row == 0, top, extra)
    extra = jnp.where(row == 1, middle, extra)
    return jnp.where(row == 2, bottom, extra)


def walk_tiles(process, first, count, unit, largest):
    steps = (count + largest - 1) // largest

    def step(index, carry):
        start = lax.div(count * index, steps)
        size = lax.div(count * (index + 1), steps) - start
        offset = pl.multiple_of((first + start) * unit, unit)
        choices = [functools.partial(process, offset, each) for each in range(1, largest + 1)]
        lax.switch(size - 1, choices)
        return carry

    lax.fori_loop(0, steps, step, 0)


def query_units(ends_ref, scenes, block, rows, span, core, unit):
    def local(position):
        inside = jnp.clip(lax.rem(position, span) - core * rows, 0, rows)
        return position // span * rows + inside

    low, high = scene_span(ends_ref, scenes, block * rows, block * rows + rows - 1)
    low, high = local(low), local(high)
    begin = low // unit
    return begin, jnp.where(low < high, (high + unit - 1) // unit - begin, 0)


def stored_units(total, scenes, rows, group, unit):
    longest = min(SCENE_MAX, total)
    each = (longest // rows + 2) * (longest // (group * unit) + 2)
    return -(-total * each // longest) + 4 * scenes + BACK_UNITS


FORWARD_BLOCKS = 8


def forward_kernel(
    ends_ref, me_ref, recv_ref, other_ref, out_ref, scale_ref, store_far,
    keys, values, probs, mixed, key_top, begins, counts, bases, state, sems,
    *, scenes, group, total,
):
    block = pl.program_id(0)
    core = me_ref[0]
    sources = recv_ref.shape[0]
    rows = recv_ref.shape[2]
    blocks = sources * group
    unit = min(256, rows)
    query_parts = rows // unit

    def unit_copy(slot, part, column, where):
        return pltpu.make_async_copy(
            probs.at[slot, part, :, column * rows : (column + 1) * rows],
            store_far.at[where], sems.at[slot],
        )

    def full_copy(slot, column, where):
        return pltpu.make_async_copy(
            probs.at[slot, :, :, column * rows : (column + 1) * rows],
            store_far.at[pl.ds(where, query_parts)], sems.at[slot],
        )

    def drain(slot):
        def one(index, carry):
            unit_copy(slot, 0, 0, 0).wait()
            return carry

        lax.fori_loop(0, state[slot], one, 0)
        state[slot] = 0

    @pl.when(block == 0)
    def _():
        key_top[0] = 0.0
        state[0] = 0
        state[1] = 0
        state[2] = 0

        def plan(index, base):
            begin, count = query_units(
                ends_ref, scenes, index, rows, group * rows, core, unit
            )
            begins[index] = begin
            counts[index] = count
            bases[index] = base
            return base + count

        lax.fori_loop(0, blocks, plan, jnp.int32(0))
        for piece in range(group):
            place = core ^ piece

            def load(source, carry, piece=piece, place=place):
                first = pl.multiple_of((source * group + place) * rows, rows)
                if piece == 0:
                    key = recv_ref[source, 64:128, :]
                    value = recv_ref[source, 128:192, :]
                else:
                    key = other_ref[piece - 1, source, 0:64, :]
                    value = other_ref[piece - 1, source, 64:128, :]
                at = pl.ds(first, rows)
                keys[0:64, at] = key
                keys[64:128, at] = key_extra(ends_ref, scenes, first, rows)
                values[at, :] = jnp.concatenate([value, jnp.ones((64, rows), BF)], axis=0).T
                wide = key.astype(F32)
                key_top[0] = jnp.maximum(key_top[0], jnp.max(jnp.sum(wide * wide, axis=0)))
                return carry

            lax.fori_loop(0, sources, load, 0)

    first = (block * group + core) * rows
    low, high = scene_span(ends_ref, scenes, first, first + rows - 1)
    query = recv_ref[block, 0:64, :]
    wide = query.astype(F32)
    query_top = jnp.max(jnp.sum(wide * wide, axis=0))
    extra = query_extra(ends_ref, scenes, first, rows, None)
    query = jnp.concatenate([query, extra], axis=0).T
    begin = low // rows
    count = (high + rows - 1) // rows - begin
    safe = query_top * key_top[0] <= SAFE_BOUND * SAFE_BOUND

    def scores_of(offset, size):
        return dot(query, keys[:, pl.ds(offset, size)], 1, 0)

    def keep(offset, size, weights):
        slot = lax.rem(state[2], 2)
        state[2] = state[2] + 1
        drain(slot)
        low_weights = weights.astype(BF)
        probs[slot, :, :, 0 : size * rows] = low_weights.reshape(query_parts, unit, size * rows)
        mixed[...] += dot(low_weights, values[pl.ds(offset, size * rows), :], 1, 0)
        for column in range(size):
            key_block = offset // rows + column
            place = block * query_parts - begins[key_block]
            inside = (place >= 0) & (place + query_parts <= counts[key_block])

            @pl.when(inside)
            def _(column=column, key_block=key_block, place=place):
                full_copy(slot, column, bases[key_block] + place).start()
                state[slot] = state[slot] + query_parts

            @pl.when(jnp.logical_not(inside))
            def _(column=column, key_block=key_block, place=place):
                for part in range(query_parts):
                    here = place + part

                    @pl.when((here >= 0) & (here < counts[key_block]))
                    def _(part=part, here=here):
                        unit_copy(slot, part, column, bases[key_block] + here).start()
                        state[slot] = state[slot] + 1

    mixed[...] = jnp.zeros_like(mixed)

    @pl.when(safe)
    def _():
        def process(offset, size):
            keep(offset, size, jnp.exp2(scores_of(offset, size * rows)))

        walk_tiles(process, begin, count, rows, FORWARD_BLOCKS)

    @pl.when(jnp.logical_not(safe))
    def _():
        def highest(index, top):
            offset = pl.multiple_of((begin + index) * rows, rows)
            return jnp.maximum(
                top, jnp.max(scores_of(offset, rows), axis=1, keepdims=True)
            )

        top = lax.fori_loop(0, count, highest, jnp.full((rows, 1), neg_large, F32))

        def process(index, carry):
            offset = pl.multiple_of((begin + index) * rows, rows)
            keep(offset, 1, jnp.exp2(scores_of(offset, rows) - top))
            return carry

        lax.fori_loop(0, count, process, 0)

    result = mixed[...].T
    out_ref[0] = (result[0:64, :] / result[64:65, :]).astype(BF)
    scale_ref[0] = 1.0 / result[64:65, :]

    @pl.when(block == sources - 1)
    def _():
        drain(0)
        drain(1)


def attention_forward(ends, me, recv, other, group):
    sources, _, rows = recv.shape
    total = sources * group * rows
    unit = min(256, rows)
    scenes = ends.shape[0]
    whole = pl.BlockSpec(memory_space=pltpu.VMEM)
    units = stored_units(total, scenes, rows, group, unit)
    return pl.pallas_call(
        functools.partial(forward_kernel, scenes=scenes, group=group, total=total),
        grid_spec=pltpu.PrefetchScalarGridSpec(
            num_scalar_prefetch=2,
            grid=(sources,),
            in_specs=[whole, whole],
            out_specs=[
                pl.BlockSpec((1, 64, rows), lambda b, *_: (b, 0, 0)),
                pl.BlockSpec((1, 1, rows), lambda b, *_: (b, 0, 0)),
                pl.BlockSpec(memory_space=pl.ANY),
            ],
            scratch_shapes=[
                pltpu.VMEM((128, total), BF),
                pltpu.VMEM((total, 128), BF),
                pltpu.VMEM((2, rows // unit, unit, FORWARD_BLOCKS * rows), BF),
                pltpu.VMEM((rows, 128), F32),
                pltpu.SMEM((1,), F32),
                pltpu.SMEM((sources * group,), jnp.int32),
                pltpu.SMEM((sources * group,), jnp.int32),
                pltpu.SMEM((sources * group,), jnp.int32),
                pltpu.SMEM((3,), jnp.int32),
                pltpu.SemaphoreType.DMA((2,)),
            ],
        ),
        out_shape=[
            jax.ShapeDtypeStruct((sources, 64, rows), BF),
            jax.ShapeDtypeStruct((sources, 1, rows), F32),
            jax.ShapeDtypeStruct((units, unit, rows), BF),
        ],
        compiler_params=pltpu.CompilerParams(vmem_limit_bytes=60 * 2**20),
        cost_estimate=pl.CostEstimate(
            flops=60 * 10**9, bytes_accessed=90 * 10**6, transcendentals=45 * 10**6
        ),
        name="attention_forward",
    )(ends, me, recv, other)


BACK_UNITS = 8


def backward_kernel(
    ends_ref, me_ref, recv_ref, others_ref, dout_ref, out_ref, scale_ref, store_far,
    dquery_ref, dkeys_ref,
    douts, queries_flat, douts_flat, dqueries, dkey, dvalue, probs, state, sems,
    *, scenes, group,
):
    block = pl.program_id(0)
    core = me_ref[0]
    sources = recv_ref.shape[0]
    rows = recv_ref.shape[2]
    span = group * rows
    unit = min(256, rows)

    def fetch(slot, first):
        return pltpu.make_async_copy(
            store_far.at[pl.ds(first, BACK_UNITS)], probs.at[slot], sems.at[slot]
        )

    @pl.when(block == 0)
    def _():
        state[0] = 0
        state[1] = 0
        fetch(0, 0).start()
        dqueries[...] = jnp.zeros_like(dqueries)

        def load(source, carry):
            at = pl.ds(pl.multiple_of(source * rows, rows), rows)
            dout = (dout_ref[source].astype(F32) * scale_ref[source]).astype(BF)
            delta = jnp.sum(
                dout.astype(F32) * out_ref[source].astype(F32), axis=0, keepdims=True
            )
            row = lax.broadcasted_iota(jnp.int32, (64, rows), 0)
            extra = stat_rows(row, delta, jnp.zeros((64, rows), F32)).astype(BF)
            douts[at, :] = jnp.concatenate([dout, extra], axis=0).T
            queries_flat[:, at] = recv_ref[source, 0:64, :]
            douts_flat[:, at] = dout
            return carry

        lax.fori_loop(0, sources, load, 0)

    source = block // group
    place = block % group
    own = place == core
    key = jnp.where(own, recv_ref[source, 64:128, :], others_ref[0, 0, 0:64, :])
    value = jnp.where(own, recv_ref[source, 128:192, :], others_ref[0, 0, 64:128, :])
    row = lax.broadcasted_iota(jnp.int32, (64, rows), 0)
    extra = jnp.where(row < STAT_ROWS, -1.0, 0.0).astype(BF)
    key_rows = jnp.concatenate([key, extra], axis=0).T
    value_wide = jnp.concatenate([value, extra], axis=0)
    begin, count = query_units(ends_ref, scenes, block, rows, span, core, unit)

    def process(offset, size):
        slot = lax.rem(state[1], 2)
        fetch(slot, 0).wait()
        following = state[0] + size
        fetch(1 - slot, following).start()
        state[0] = following
        state[1] = state[1] + 1
        at = pl.ds(offset, size * unit)
        kept = probs[slot, 0:size].reshape(size * unit, rows)
        dprobs = dot(douts[at, :], value_wide, 1, 0)
        dscores = (kept.astype(F32) * dprobs).astype(BF)
        dvalue[...] += dot(douts_flat[:, at], kept, 1, 0)
        dkey[...] += dot(queries_flat[:, at], dscores, 1, 0)
        dqueries[at, :] += dot(dscores, key_rows, 1, 0)

    dkey[...] = jnp.zeros_like(dkey)
    dvalue[...] = jnp.zeros_like(dvalue)
    walk_tiles(process, begin, count, unit, BACK_UNITS)
    dkeys_ref[0, 0, 0:64, :] = (dkey[...] * ln_2).astype(BF)
    dkeys_ref[0, 0, 64:128, :] = dvalue[...].astype(BF)

    @pl.when(block == sources * group - 1)
    def _():
        fetch(lax.rem(state[1], 2), 0).wait()

        def store(source, carry):
            at = pl.ds(pl.multiple_of(source * rows, rows), rows)
            dquery_ref[source] = (dqueries[at, :].T[0:64, :] * HEAD_DIM**-0.5).astype(BF)
            return carry

        lax.fori_loop(0, sources, store, 0)


def attention_backward(ends, me, recv, others, dout, out, scale, store, group):
    sources, _, rows = recv.shape
    mine = sources * rows
    unit = min(256, rows)
    whole = pl.BlockSpec(memory_space=pltpu.VMEM)

    def other_map(block, ends_ref, me_ref):
        return (jnp.maximum((block % group) ^ me_ref[0], 1) - 1, block // group, 0, 0)

    def piece_map(block, ends_ref, me_ref):
        return ((block % group) ^ me_ref[0], block // group, 0, 0)

    return pl.pallas_call(
        functools.partial(backward_kernel, scenes=ends.shape[0], group=group),
        grid_spec=pltpu.PrefetchScalarGridSpec(
            num_scalar_prefetch=2,
            grid=(sources * group,),
            in_specs=[whole, pl.BlockSpec((1, 1, 128, rows), other_map)]
            + [whole] * 3 + [pl.BlockSpec(memory_space=pl.ANY)],
            out_specs=[whole, pl.BlockSpec((1, 1, 128, rows), piece_map)],
            scratch_shapes=[
                pltpu.VMEM((mine, 128), BF),
                pltpu.VMEM((64, mine), BF),
                pltpu.VMEM((64, mine), BF),
                pltpu.VMEM((mine, 128), F32),
                pltpu.VMEM((64, rows), F32),
                pltpu.VMEM((64, rows), F32),
                pltpu.VMEM((2, BACK_UNITS, unit, rows), BF),
                pltpu.SMEM((2,), jnp.int32),
                pltpu.SemaphoreType.DMA((2,)),
            ],
        ),
        out_shape=[
            jax.ShapeDtypeStruct((sources, 64, rows), BF),
            jax.ShapeDtypeStruct((group, sources, 128, rows), BF),
        ],
        compiler_params=pltpu.CompilerParams(vmem_limit_bytes=VMEM_BYTES),
        cost_estimate=pl.CostEstimate(
            flops=150 * 10**9, bytes_accessed=150 * 10**6, transcendentals=0
        ),
        name="attention_backward",
    )(ends, me, recv, others, dout, out, scale, store)


def swap_tensor(part):
    return lax.ppermute(part, "tensor", [(0, 1), (1, 0)])


def per_device(
    tokens, scene_lengths, w_query, w_key, w_value, w_out, w_up, w_down,
    norm_gain, norm_bias, cotangent,
):
    own_rows, width = tokens.shape
    devices = lax.axis_size("seq")
    heads = w_query.shape[2] // HEAD_DIM
    columns = heads * HEAD_DIM
    hidden = w_up.shape[2]
    group = devices // heads
    rows = own_rows // group
    me = lax.rem(lax.axis_index("seq"), group).astype(jnp.int32).reshape(1)
    half = lax.axis_index("tensor")
    ends = jnp.cumsum(scene_lengths).astype(jnp.int32)

    recv, others, normed_one, w_first, out_own, norms, second_part = project(
        tokens, w_query, w_key, w_value, w_out, norm_gain, norm_bias, w_up, w_down, devices, group
    )
    out_other = swap_tensor(out_own)
    second_all = lax.all_gather(second_part, "seq", axis=0, tiled=True)
    def swap_core(part, by):
        return lax.ppermute(part, "seq", [(i, i ^ by) for i in range(devices)])

    if group > 2:
        others = jnp.stack([swap_core(recv[:, HEAD_DIM:, :], by) for by in range(1, group)])
    out_head, scale, store = attention_forward(ends, me, recv, others, group)

    dout, dmid, mid, z, grads_second, second_norms = middle(
        out_head, tokens, cotangent, out_own, out_other, second_all, norms, devices, group
    )
    z_other = swap_tensor(z)
    grads_second = lax.psum_scatter(grads_second, "seq", scatter_dimension=0, tiled=True)
    grads_second = grads_second.astype(F32)

    dquery, dpieces = attention_backward(
        ends, me, recv, others, dout, out_head, scale, store, group
    )
    if group > 2:
        dpieces = sum([dpieces[0].astype(F32)] + [
            swap_core(dpieces[by], by).astype(F32) for by in range(1, group)
        ]).astype(BF)[None]
    dstream, last, dquery_w, dkey_w, dvalue_w, dgain, dbias = finish(
        dquery, dpieces, normed_one, w_first, tokens, dmid, mid, z, z_other, norms, second_norms,
        devices, group,
    )
    return (
        last,
        dstream,
        dquery_w,
        dkey_w,
        dvalue_w,
        grads_second[:, :columns].T[None],
        grads_second[:, columns : columns + hidden][None],
        grads_second[:, columns + hidden :].T[None],
        dgain,
        dbias,
    )


def solution(mesh):
    placed = (
        P("seq", None),
        P(),
        P(None, "seq", "tensor"),
        P(None, "seq", "tensor"),
        P(None, "seq", "tensor"),
        P(None, "tensor", "seq"),
        P(None, "seq", "tensor"),
        P(None, "tensor", "seq"),
        P(None, None, "seq"),
        P(None, None, "seq"),
        P("seq", None),
    )
    return jax.shard_map(
        per_device,
        mesh=mesh,
        in_specs=placed,
        out_specs=(
            P("seq", None),
            P("seq", None),
            P(None, "seq", "tensor"),
            P(None, "seq", "tensor"),
            P(None, "seq", "tensor"),
            P(None, "tensor", "seq"),
            P(None, "seq", "tensor"),
            P(None, "tensor", "seq"),
            P(None, None, "seq"),
            P(None, None, "seq"),
        ),
        check_vma=False,
    )
```
